512 devices in a mesh: lon: 64 (over z_hi, y, x), lat: 8 (over z_lo, core).
Axes of the slice: x: 4, y: 8, z: 8 (z_hi: 2, z_lo: 4; z = z_hi * 4 + z_lo), core: 2. Of those that a mesh axis runs over, the one named last changes fastest.
Arguments:
- state: bfloat16 [128, 256, 512], P('lat', 'lon'), may hold values from -6 to 6
- conv_weight: bfloat16 [4608, 512], P('lon'), may hold values from -0.09375 to 0.09375
- conv_bias: float32 [512], replicated, may hold values from -5 to 5
- w_qkv: bfloat16 [512, 1536], replicated, may hold values from -0.5 to 0.5
- w_out: bfloat16 [512, 512], replicated, may hold values from -0.25 to 0.25
- cotangent: bfloat16 [128, 256, 512], P('lat', 'lon'), may hold values from -6 to 6
Outputs:
- state_grad: bfloat16 [128, 256, 512], P('lat', 'lon')
The draws below stay inside these ranges and needn't reach their ends.
All inputs are finite; a program needn't handle non-finite values.
Results may differ from the reference program's by a relative error of at most 0.029.
Values may be sent and summed in bfloat16 or wider, within the bound.
A program may use at most 64 MiB of HBM per device.

```python
import math
import jax
import jax.numpy as jnp
from jax import lax

C = 512
HEAD_DIM = 128
HEADS = 4
LAT = 128
LON = 256


def level_of(rng, dims, cuts, least, top_value):
    def one(position, blocks):
        heights = jax.random.uniform(jax.random.fold_in(jax.random.fold_in(rng, 6), position), (blocks,), jnp.float32, least / len(cuts), top_value / len(cuts))
        return jnp.repeat(jnp.exp(heights), dims[position] // blocks).reshape((-1,) + (1,) * (len(dims) - position - 1))

    gain = one(*cuts[0])
    for cut in cuts[1:]:
        gain = gain * one(*cut)
    return gain


def scatter_about(rng, shape, width, bound, split=(), held_as=jnp.bfloat16):
    drawn = width * jax.random.normal(rng, shape, jnp.float32)
    if split:
        drawn = drawn * level_of(rng, shape, split, -0.22, 0.18)
    return jnp.clip(drawn, -bound, bound).astype(held_as)


def setup_inputs(seed: int = 0) -> dict:
    streams_of = jax.random.split(jax.random.key(seed), 7)
    return {
        "state": scatter_about(streams_of[0], (LAT, LON, C), 1.0, 6.0, ((0, 8), (1, 64))),
        "conv_weight": scatter_about(streams_of[1], (9 * C, C), (9 * C) ** -0.5, 0.09375, ((0, 64),)),
        "conv_bias": scatter_about(streams_of[2], (C,), 1.0, 5.0, (), jnp.float32),
        "w_qkv": scatter_about(streams_of[3], (C, 3 * C), (C // 4) ** -0.5, 0.5),
        "w_out": scatter_about(streams_of[4], (C, C), C ** -0.5, 0.25),
        "cotangent": scatter_about(streams_of[5], (LAT, LON, C), 1.0, 6.0, ((0, 8), (1, 64))),
    }


softcap = 20.0

def border(field):
    wrapped = jnp.concatenate([field[:, -1:], field, field[:, :1]], axis=1)
    return jnp.pad(wrapped, ((1, 1), (0, 0), (0, 0)))

def rounded(value):
    return lax.optimization_barrier(value.astype(jnp.bfloat16)).astype(jnp.float32)

def row_attention(parts):
    queries, key_rows, value_rows, out_grad = parts
    inv_root = 1.0 / math.sqrt(HEAD_DIM)
    query_f = queries.astype(jnp.float32)
    key_f = key_rows.astype(jnp.float32)
    value_f = value_rows.astype(jnp.float32)
    grad_f = out_grad.astype(jnp.float32)
    raw = jnp.einsum('ihd,jhd->hij', query_f, key_f) * inv_root
    scores = softcap * jnp.tanh(raw / softcap)
    expo = jnp.exp(scores)
    probs = expo / lax.optimization_barrier(jnp.sum(expo, axis=-1, keepdims=True))
    probs_b = rounded(probs)
    attended = rounded(jnp.einsum('hij,jhd->ihd', probs_b, value_f))
    centre = lax.optimization_barrier(jnp.sum(grad_f * attended, axis=-1))
    dprobs = jnp.einsum('ihd,jhd->hij', grad_f, value_f)
    score_grad = rounded(probs * (dprobs - centre.T[:, :, None]) * (1.0 - jnp.square(scores / softcap)) * inv_root)
    grad_query = jnp.einsum('hij,jhd->ihd', score_grad, key_f).astype(jnp.bfloat16)
    grad_key = jnp.einsum('hij,ihd->jhd', score_grad, query_f).astype(jnp.bfloat16)
    grad_value = jnp.einsum('hij,ihd->jhd', probs_b, grad_f).astype(jnp.bfloat16)
    return jnp.concatenate([grad_query.reshape(LON, C), grad_key.reshape(LON, C), grad_value.reshape(LON, C)], axis=-1)

def reference(state, conv_weight, conv_bias, w_qkv, w_out, cotangent):
    padded = border(state)
    summed = jnp.zeros((LAT * LON, C), jnp.float32)
    for row_off in range(3):
        for col_off in range(3):
            tap_index = 3 * row_off + col_off
            windowed = padded[row_off:row_off + LAT, col_off:col_off + LON].reshape(LAT * LON, C)
            summed = summed + jnp.dot(windowed, conv_weight[tap_index * C:(tap_index + 1) * C], preferred_element_type=jnp.float32)
    preact = summed + conv_bias
    sigmoid_pre = jax.nn.sigmoid(preact)
    activated = (preact * sigmoid_pre).astype(jnp.bfloat16)
    projected = jnp.dot(activated, w_qkv, preferred_element_type=jnp.float32).astype(jnp.bfloat16)
    projected = projected.reshape(LAT, LON, 3, HEADS, HEAD_DIM)
    out_grad = jnp.dot(cotangent.reshape(LAT * LON, C), w_out.T, preferred_element_type=jnp.float32).astype(jnp.bfloat16)
    out_grad = out_grad.reshape(LAT, LON, HEADS, HEAD_DIM)
    qkv_grad = lax.map(row_attention, (projected[:, :, 0], projected[:, :, 1], projected[:, :, 2], out_grad))
    grad_act = cotangent.reshape(LAT * LON, C).astype(jnp.float32) + jnp.dot(qkv_grad.reshape(LAT * LON, 3 * C), w_qkv.T, preferred_element_type=jnp.float32)
    grad_pre = (grad_act * sigmoid_pre * (1.0 + preact * (1.0 - sigmoid_pre))).astype(jnp.bfloat16)
    padded_grad = border(grad_pre.reshape(LAT, LON, C))
    result = jnp.zeros((LAT * LON, C), jnp.float32)
    for row_off in range(3):
        for col_off in range(3):
            tap_index = 3 * row_off + col_off
            windowed = padded_grad[2 - row_off:2 - row_off + LAT, 2 - col_off:2 - col_off + LON].reshape(LAT * LON, C)
            result = result + jnp.dot(windowed, conv_weight[tap_index * C:(tap_index + 1) * C].T, preferred_element_type=jnp.float32)
    return result.astype(jnp.bfloat16).reshape(LAT, LON, C)
```

```python
import functools
import math

import jax
import jax.numpy as jnp
from jax import lax
from jax.experimental import pallas as pl
from jax.experimental.pallas import tpu as pltpu
from jax.sharding import PartitionSpec as P

X = 4
Y = 8
ZY = 16
LATS = 8
ROWS = ZY * LATS
CAP = 20.0
INV_ROOT = 1.0 / math.sqrt(128.0)
F32 = jnp.float32
BF16 = jnp.bfloat16
VMEM_LIMIT = 60 * 1024 * 1024

NN = (((1,), (0,)), ((), ()))
NT = (((1,), (1,)), ((), ()))
TN = (((0,), (0,)), ((), ()))


def dot(a, b, dims=NN):
    return lax.dot_general(a, b, dims, preferred_element_type=F32)


def kernel(
    st_hbm, ct_hbm, cw_hbm, bias_hbm, wqkv, wout, out,
    raw, raw_w, st, ct, wp, bias,
    rows, cots, flat, grid, cot_grid, cot_blocks, w_one, w_all, wq, wo,
    pre, acts, blocks, parts, parts_in, own_pre, pres, shifted, mine, sums_in, rims, rims_in,
    load_sem, w_send, w_recv, row_send, row_recv, cot_send, cot_recv, pre_send, pre_recv,
    end_send, rim_send, rim_recv,
    send, recv,
):
    lon = lax.axis_index("lon")
    lat = lax.axis_index("lat")
    zy, x = lon // X, lon % X
    z, y = zy // Y, zy % Y
    core = lat % 2
    sib = lat + 1 - 2 * core
    row = lat * ZY + zy
    up, down = (lat + 1) % LATS, (lat + LATS - 1) % LATS
    after, before = (row + 1) % ROWS, (row + ROWS - 1) % ROWS
    east, west = (x + 1) % X, (x + X - 1) % X

    def remote(src, dst, send_sem, recv_sem, to_zy, to_x, to_lat):
        return pltpu.make_async_remote_copy(
            src_ref=src,
            dst_ref=dst,
            send_sem=send_sem,
            recv_sem=recv_sem,
            device_id={"lon": to_zy * X + to_x, "lat": to_lat},
            device_id_type=pl.DeviceIdType.MESH,
        )

    started = []

    def push_to(src, dst, to_zy, to_x, to_lat):
        i = len(started)
        copy = remote(src, dst, send.at[i], recv.at[i], to_zy, to_x, to_lat)
        copy.start()
        started.append(copy)
        return copy

    def push(ref, to_zy, to_x, to_lat):
        return push_to(ref, ref, to_zy, to_x, to_lat)

    def load(i, src, dst):
        copy = pltpu.make_async_copy(src, dst, load_sem.at[i])
        copy.start()
        return copy

    weight_load = load(0, cw_hbm, raw_w)
    state_load = load(1, st_hbm, raw.at[0])
    cot_load = load(2, ct_hbm, raw.at[1])
    loads = [load(3, bias_hbm, bias)]
    for t in range(3):
        source = wqkv.at[:, pl.ds(pl.multiple_of(t * 512 + x * 128, 128), 128)]
        loads.append(load(4 + t, source, wq.at[:, 128 * t : 128 * (t + 1)]))
    loads.append(load(7, wout.at[pl.ds(pl.multiple_of(x * 128, 128), 128)], wo))

    barrier = pltpu.get_barrier_semaphore()

    def hello(to_zy, to_x, to_lat):
        pl.semaphore_signal(
            barrier,
            inc=1,
            device_id={"lon": to_zy * X + to_x, "lat": to_lat},
            device_id_type=pl.DeviceIdType.MESH,
        )

    other_zy = (1 - z) * Y + y
    for dx in range(1, X):
        hello(zy, (x + dx) % X, lat)
        hello(other_zy, (x + dx) % X, lat)
    hello(zy, x, sib)

    @pl.loop(1, ZY)
    def _(d):
        hello((zy + d) % ZY, x, lat)

    hello(ZY - 1, x, down)
    hello(0, x, up)

    @pl.when(x == 0)
    def _():
        for i in range(X):
            hello((zy + ZY - 1) % ZY, i, lat)

    @pl.when(x == X - 1)
    def _():
        for i in range(X):
            hello((zy + 1) % ZY, i, lat)

    weight_load.wait()
    for q in range(X):
        piece = raw_w[:, 128 * q : 128 * (q + 1)].astype(F32)
        wp[q] = jnp.concatenate([piece, jnp.zeros((8, 128), F32)], axis=0).astype(BF16)

    edge = (zy == 0) | (zy == ZY - 1)
    pl.semaphore_wait(barrier, 2 * (X - 1) + (ZY - 1) + 1 + 2 + jnp.where(edge, ZY, 0))

    def all_weights(start):
        @pl.when(x // 2 == core)
        def _():
            slot = z * 2 + x % 2
            for t in range(2 * X):
                to_z, to_x = t // X, t % X
                here = (to_z == z) & (to_x == x)
                if start:
                    @pl.when(here)
                    def _():
                        pltpu.make_async_copy(
                            wp.at[to_x], w_one.at[slot], w_recv.at[slot]
                        ).start()

                @pl.when(jnp.logical_not(here))
                def _():
                    copy = remote(
                        wp.at[to_x], w_one.at[slot], w_send.at[t], w_recv.at[slot],
                        to_z * Y + y, to_x, lat,
                    )
                    if start:
                        copy.start()
                    else:
                        copy.wait_send()

    all_weights(True)

    def relayout(which, dst):
        for r in range(16):
            for q in range(4):
                piece = raw[which, r, :, 128 * q : 128 * (q + 1)].astype(F32)
                flat[pl.ds(16 * r + q, 4, stride=4), :] = piece
        dst[...] = flat[0:256, :].astype(BF16).reshape(16, 16, 128)

    state_load.wait()
    relayout(0, st)

    def all_rows(src, dst, send_sem, recv_sem, start, first=0, last=ZY):
        @pl.loop(first, last)
        def _(t):
            if start:
                @pl.when(t == zy)
                def _():
                    pltpu.make_async_copy(src.at[t], dst, recv_sem).start()

            @pl.when(t != zy)
            def _():
                copy = remote(src.at[t], dst, send_sem.at[t], recv_sem, t, x, lat)
                if start:
                    copy.start()
                else:
                    copy.wait_send()

    all_rows(st, rows.at[1, zy, x], row_send, row_recv, True)

    for i in range(4):
        pltpu.make_async_copy(w_one.at[i], w_one.at[i], w_recv.at[i]).wait()

    def half(place, which):
        return pl.ds(pl.multiple_of((place * 2 + which) * 144, 16), 144)

    for i in range(2):
        both = [w_one[2 * i + s].astype(F32)[:72] for s in range(2)]
        w_all[i, half(y, core), :] = jnp.concatenate(both, axis=0).astype(BF16)

    right = z * Y + (y + 1) % Y
    left = z * Y + (y + Y - 1) % Y

    def ring(part, place, to):
        return push(w_all.at[part, half(place, core)], to, x, lat)

    rights = [[ring(0, y, right), ring(1, y, right)]]
    lefts = [[ring(1, y, left), ring(0, y, left)]]
    pair = [push(w_all.at[:, half(y, core)], zy, x, sib)]

    def forward(step):
        turns = (
            (rights, right, (y + Y - 1 - step) % Y, (0, 1)),
            (lefts, left, (y + 1 + step) % Y, (1, 0)),
        )
        for copies, _, _, _ in turns:
            copies.append([])
        for turn in range(len(rights[step])):
            for copies, to, got, parts_of in turns:
                copies[step][turn].wait_recv()
                part = parts_of[turn]
                if step < 2 or (step == 2 and turn == 0):
                    copies[step + 1].append(ring(part, got, to))
                pair.append(push(w_all.at[part, half(got, core)], zy, x, sib))

    pltpu.make_async_copy(rows.at[1, :, x], rows.at[1, :, x], row_recv).wait()
    to_after = push_to(rows.at[1, :, x], rows.at[0, :, x], after % ZY, x, after // ZY)
    to_before = push_to(rows.at[1, :, x], rows.at[2, :, x], before % ZY, x, before // ZY)
    row_east = push(rows.at[1, :, x], zy, east, lat)
    row_west = push(rows.at[1, :, x], zy, west, lat)

    cot_load.wait()
    relayout(1, ct)
    forward(0)

    to_after.wait_recv()
    to_before.wait_recv()
    above_east = push(rows.at[0, :, x], zy, east, lat)
    below_west = push(rows.at[2, :, x], zy, west, lat)
    below_east = push(rows.at[2, :, x], zy, east, lat)
    above_west = push(rows.at[0, :, x], zy, west, lat)
    row_east.wait_recv()
    row_on_east = push(rows.at[1, 0:8, west], zy, east, lat)
    row_west.wait_recv()
    row_on_west = push(rows.at[1, 8:16, east], zy, west, lat)

    forward(1)

    all_rows(ct, cots.at[zy, x], cot_send, cot_recv, True)
    above_east.wait_recv()
    above_on = push(rows.at[0, :, west], zy, east, lat)
    below_west.wait_recv()
    below_on = push(rows.at[2, :, east], zy, west, lat)

    forward(2)

    def whole_row(a):
        flat[...] = rows[a].reshape(1024, 128).astype(F32)
        for q in range(4):
            part = flat[pl.ds(q, 256, stride=4), :]
            if a == 0:
                part = jnp.where(row == 0, 0.0, part)
            if a == 2:
                part = jnp.where(row == ROWS - 1, 0.0, part)
            grid[a, :, 128 * q : 128 * (q + 1)] = part.astype(BF16)

    row_on_east.wait_recv()
    row_on_west.wait_recv()
    whole_row(1)

    pltpu.make_async_copy(cots.at[:, x], cots.at[:, x], cot_recv).wait()
    cot_x = [push(cots.at[:, x], zy, (x + dx) % X, lat) for dx in range(1, X)]

    forward(3)

    below_east.wait_recv()
    above_west.wait_recv()
    above_on.wait_recv()
    whole_row(0)
    below_on.wait_recv()
    whole_row(2)
    for copy in loads:
        copy.wait()
    for copy in pair:
        copy.wait_recv()

    def tap(i):
        if i < 4:
            return w_all[0, 512 * i : 512 * (i + 1), :]
        if i > 4:
            return w_all[1, 512 * i - 2304 : 512 * (i + 1) - 2304, :]
        return jnp.concatenate([w_all[0, 2048:2304, :], w_all[1, 0:256, :]], axis=0)

    two = jnp.zeros((256, 256), F32)
    third = jnp.zeros((256, 128), F32)
    for a in (1, 0, 2):
        two = two + dot(grid[a], jnp.concatenate([tap(3 * a), tap(3 * a + 1)], axis=1))
        third = third + dot(grid[a], tap(3 * a + 2))
    preact = (
        bias[pl.ds(x, 1), :]
        + pltpu.roll(two[:, 0:128], 1, 0)
        + two[:, 128:256]
        + pltpu.roll(third, 255, 0)
    )
    pre[...] = preact
    acts[x] = (preact * jax.nn.sigmoid(preact)).astype(BF16)
    act_x = [push(acts.at[x], zy, (x + dx) % X, lat) for dx in range(1, X)]

    for copy in cot_x:
        copy.wait_recv()
    flat[...] = cots[...].reshape(1024, 128).astype(F32)
    for q in range(4):
        part = flat[pl.ds(q, 256, stride=4), :].astype(BF16)
        cot_grid[:, 128 * q : 128 * (q + 1)] = part
        cot_blocks[q] = part
    out_grad = dot(cot_grid[...], wo[...], NT).astype(BF16)

    for copy in act_x:
        copy.wait_recv()
    activated = jnp.concatenate([acts[s] for s in range(X)], axis=1)
    projected = dot(activated, wq[...]).astype(BF16)
    queries, keys, values = (projected[:, 128 * t : 128 * (t + 1)] for t in range(3))
    capped = jnp.tanh(dot(queries, keys, NT) * (INV_ROOT / CAP))
    expo = jnp.exp(CAP * capped)
    probs = expo / jnp.sum(expo, axis=-1, keepdims=True)
    probs_b = probs.astype(BF16)
    attended = dot(probs_b, values).astype(BF16)
    centre = jnp.sum(out_grad.astype(F32) * attended.astype(F32), axis=-1, keepdims=True)
    score_grad = (
        probs * (dot(out_grad, values, NT) - centre) * (1.0 - capped * capped) * INV_ROOT
    ).astype(BF16)
    grads = jnp.concatenate(
        [
            dot(score_grad, keys).astype(BF16),
            dot(score_grad, queries, TN).astype(BF16),
            dot(probs_b, out_grad, TN).astype(BF16),
        ],
        axis=1,
    )
    head_part = dot(grads, wq[...], NT)
    for q in range(X):
        blocks[q] = head_part[:, 128 * q : 128 * (q + 1)]

    part_x = []
    for half_of in range(2):
        at = slice(128 * half_of, 128 * (half_of + 1))
        for dx in (2, 1, 3):
            to = (x + dx) % X
            parts[dx - 1, at] = blocks[to, at].astype(BF16)
            part_x.append(
                push_to(parts.at[dx - 1, at], parts_in.at[dx - 1, at], zy, to, lat)
            )

    def all_pres(first, start):
        all_rows(own_pre, pres.at[1 + zy], pre_send, pre_recv, start, first, first + 8)

        def ends(slot, to_lat):
            @pl.loop(first, first + 8)
            def _(t):
                copy = remote(
                    own_pre.at[t], pres.at[slot], end_send.at[t], pre_recv, t, x, to_lat
                )
                if start:
                    copy.start()
                else:
                    copy.wait_send()

        @pl.when(zy == ZY - 1)
        def _():
            ends(0, up)

        @pl.when(zy == 0)
        def _():
            ends(ZY + 1, down)

    for half_of in range(2):
        at = slice(128 * half_of, 128 * (half_of + 1))
        grad_act = blocks[x, at] + cot_blocks[x, at].astype(F32)
        preact = pre[at]
        s = jax.nn.sigmoid(preact)
        slope = s * (1.0 + preact * (1.0 - s))
        for copy in part_x[3 * half_of : 3 * half_of + 3]:
            copy.wait_recv()
        for i in range(X - 1):
            grad_act = grad_act + parts_in[i, at].astype(F32)
        own_pre[8 * half_of : 8 * (half_of + 1)] = (
            (grad_act * slope).astype(BF16).reshape(8, 16, 128)
        )
        all_pres(8 * half_of, True)

    pltpu.make_async_copy(pres, pres, pre_recv).wait()

    @pl.when(lat == 0)
    def _():
        pres[0] = jnp.zeros((16, 128), BF16)

    @pl.when(lat == LATS - 1)
    def _():
        pres[ZY + 1] = jnp.zeros((16, 128), BF16)

    around = jnp.concatenate(
        [pres[2 - a : 2 - a + ZY].reshape(256, 128) for a in range(3)], axis=1
    )
    column = lax.broadcasted_iota(jnp.int32, (256, 256), 0) % 16
    sum_x = []
    for h in range(2):
        at = slice(256 * h, 256 * (h + 1))
        result = jnp.zeros((256, 256), F32)
        for b in range(3):
            taps = jnp.concatenate([tap(3 * a + b)[at] for a in range(3)], axis=1)
            acc = dot(around, taps, NT)
            if b != 1:
                for q in range(2):
                    shifted[...] = acc[:, 128 * q : 128 * (q + 1)]
                    rim = shifted[pl.ds(0 if b == 0 else 15, 16, stride=16), :]
                    rims[b // 2, h, q] = rim.astype(BF16)
            if b == 0:
                acc = jnp.where(column == 15, 0.0, pltpu.roll(acc, 255, 0))
            if b == 2:
                acc = jnp.where(column == 0, 0.0, pltpu.roll(acc, 1, 0))
            result = result + acc
        for q in range(2):
            base = 512 * h + 256 * q
            flat[base : base + 256, :] = result[:, 128 * q : 128 * (q + 1)]
            for to in range(X):
                for j in range(4):
                    piece = flat[pl.ds(base + 4 * to + j, 16, stride=16), :]
                    mine[to, h, q, j] = piece.astype(BF16)
        for dx in (2, 1, 3):
            to = (x + dx) % X
            sum_x.append(push_to(mine.at[to, h], sums_in.at[dx - 1, h], zy, to, lat))

    rim_west = remote(
        rims.at[0], rims_in.at[x], rim_send.at[0], rim_recv.at[x],
        (zy + ZY - 1) % ZY, X - 1, lat,
    )
    rim_east = remote(
        rims.at[1], rims_in.at[x], rim_send.at[1], rim_recv.at[x], (zy + 1) % ZY, 0, lat
    )
    rim_west.start()
    rim_east.start()

    for h in range(2):
        total = mine[x, h].astype(F32)
        for copy in sum_x[3 * h : 3 * h + 3]:
            copy.wait_recv()
        for i in range(X - 1):
            total = total + sums_in[i, h].astype(F32)
        flat[128 * h : 128 * (h + 1), :] = total.reshape(128, 128)

    def add_rims(j):
        for i in range(X):
            pltpu.make_async_copy(rims_in.at[i], rims_in.at[i], rim_recv.at[i]).wait()
        for q in range(4):
            at = slice(64 * q + 16 * j, 64 * q + 16 * (j + 1))
            total = flat[at]
            for i in range(X):
                total = total + rims_in[i, q // 2, q % 2].astype(F32)
            flat[at] = total

    @pl.when(x == 0)
    def _():
        add_rims(0)

    @pl.when(x == X - 1)
    def _():
        add_rims(3)

    for t in range(ZY):
        out[t] = flat[pl.ds(t, 16, stride=16), :].astype(BF16)

    rim_west.wait_send()
    rim_east.wait_send()
    for copy in started:
        copy.wait_send()
    all_weights(False)
    all_rows(st, rows.at[1, zy, x], row_send, row_recv, False)
    all_rows(ct, cots.at[zy, x], cot_send, cot_recv, False)
    all_pres(0, False)
    all_pres(8, False)


PUSHES = 64


def body(state, conv_weight, conv_bias, w_qkv, w_out, cotangent):
    vmem = pl.BlockSpec(memory_space=pltpu.VMEM)
    anywhere = pl.BlockSpec(memory_space=pl.ANY)
    dma = pltpu.SemaphoreType.DMA
    out = pl.pallas_call(
        kernel,
        out_shape=jax.ShapeDtypeStruct((ZY, 16, 128), BF16),
        in_specs=[anywhere] * 6,
        out_specs=vmem,
        scratch_shapes=[
            pltpu.VMEM((2, 16, 4, 512), BF16),
            pltpu.VMEM((72, 512), BF16),
            pltpu.VMEM((ZY, 16, 128), BF16),
            pltpu.VMEM((ZY, 16, 128), BF16),
            pltpu.VMEM((X, 80, 128), BF16),
            pltpu.VMEM((X, 128), F32),
            pltpu.VMEM((3, ZY, X, 16, 128), BF16),
            pltpu.VMEM((ZY, X, 16, 128), BF16),
            pltpu.VMEM((1024, 128), F32),
            pltpu.VMEM((3, 256, 512), BF16),
            pltpu.VMEM((256, 512), BF16),
            pltpu.VMEM((4, 256, 128), BF16),
            pltpu.VMEM((4, 80, 128), BF16),
            pltpu.VMEM((2, 2304, 128), BF16),
            pltpu.VMEM((512, 384), BF16),
            pltpu.VMEM((128, 512), BF16),
            pltpu.VMEM((256, 128), F32),
            pltpu.VMEM((X, 256, 128), BF16),
            pltpu.VMEM((X, 256, 128), F32),
            pltpu.VMEM((3, 256, 128), BF16),
            pltpu.VMEM((3, 256, 128), BF16),
            pltpu.VMEM((ZY, 16, 128), BF16),
            pltpu.VMEM((ZY + 2, 16, 128), BF16),
            pltpu.VMEM((256, 128), F32),
            pltpu.VMEM((X, 2, 2, 4, ZY, 128), BF16),
            pltpu.VMEM((3, 2, 2, 4, ZY, 128), BF16),
            pltpu.VMEM((2, 2, 2, ZY, 128), BF16),
            pltpu.VMEM((X, 2, 2, ZY, 128), BF16),
            dma((8,)),
            dma((2 * X,)),
            dma((4,)),
            dma((ZY,)),
            dma,
            dma((ZY,)),
            dma,
            dma((ZY,)),
            dma,
            dma((ZY,)),
            dma((2,)),
            dma((X,)),
            dma((PUSHES,)),
            dma((PUSHES,)),
        ],
        compiler_params=pltpu.CompilerParams(
            collective_id=0, has_side_effects=True, vmem_limit_bytes=VMEM_LIMIT
        ),
    )(state, cotangent, conv_weight, conv_bias.reshape(X, 128), w_qkv, w_out)
    return out.reshape(16, 4, 4, 128).transpose(0, 2, 1, 3).reshape(16, 4, 512)


def solution(mesh):
    return jax.shard_map(
        body,
        mesh=mesh,
        in_specs=(P("lat", "lon", None), P("lon", None), P(), P(), P(), P("lat", "lon", None)),
        out_specs=P("lat", "lon", None),
        check_vma=False,
    )
```

```python
import functools
import math

import jax
import jax.numpy as jnp
from jax import lax
from jax.experimental import pallas as pl
from jax.experimental.pallas import tpu as pltpu
from jax.sharding import PartitionSpec as P

X = 4
Y = 8
ZY = 16
LATS = 8
ROWS = ZY * LATS
CAP = 20.0
INV_ROOT = 1.0 / math.sqrt(128.0)
F32 = jnp.float32
BF16 = jnp.bfloat16
VMEM_LIMIT = 60 * 1024 * 1024

NN = (((1,), (0,)), ((), ()))
NT = (((1,), (1,)), ((), ()))
TN = (((0,), (0,)), ((), ()))


def dot(a, b, dims=NN):
    return lax.dot_general(a, b, dims, preferred_element_type=F32)


def kernel(
    st_hbm, ct_hbm, cw_hbm, bias_hbm, wqkv, wout, out,
    raw, raw_w, st, ct, wp, bias,
    rows, cots, flat, grid, cot_grid, cot_blocks, w_one, w_all, wq, wo,
    pre, acts, blocks, parts, parts_in, own_pre, pres, shifted, mine, sums_in, rims, rims_in,
    load_sem, w_send, w_recv, row_send, row_recv, cot_send, cot_recv, pre_send, pre_recv,
    end_send, rim_send, rim_recv, middle_send, side_send, side_recv,
    send, recv,
):
    lon = lax.axis_index("lon")
    lat = lax.axis_index("lat")
    zy, x = lon // X, lon % X
    z, y = zy // Y, zy % Y
    core = lat % 2
    sib = lat + 1 - 2 * core
    mine_of = jnp.where(z == core, y, ZY - 1 - y)
    row = lat * ZY + mine_of
    up, down = (lat + 1) % LATS, (lat + LATS - 1) % LATS

    def owner(t):
        return jnp.where(t < Y, core * Y + t, (1 - core) * Y + ZY - 1 - t)

    east, west = (x + 1) % X, (x + X - 1) % X

    def remote(src, dst, send_sem, recv_sem, to_zy, to_x, to_lat):
        return pltpu.make_async_remote_copy(
            src_ref=src,
            dst_ref=dst,
            send_sem=send_sem,
            recv_sem=recv_sem,
            device_id={"lon": to_zy * X + to_x, "lat": to_lat},
            device_id_type=pl.DeviceIdType.MESH,
        )

    started = []

    def push_to(src, dst, to_zy, to_x, to_lat):
        i = len(started)
        copy = remote(src, dst, send.at[i], recv.at[i], to_zy, to_x, to_lat)
        copy.start()
        started.append(copy)
        return copy

    def push(ref, to_zy, to_x, to_lat):
        return push_to(ref, ref, to_zy, to_x, to_lat)

    def load(i, src, dst):
        copy = pltpu.make_async_copy(src, dst, load_sem.at[i])
        copy.start()
        return copy

    weight_load = load(0, cw_hbm, raw_w)
    state_load = load(1, st_hbm, raw.at[0])
    cot_load = load(2, ct_hbm, raw.at[1])
    loads = [load(3, bias_hbm, bias)]
    for t in range(3):
        source = wqkv.at[:, pl.ds(pl.multiple_of(t * 512 + x * 128, 128), 128)]
        loads.append(load(4 + t, source, wq.at[:, 128 * t : 128 * (t + 1)]))
    loads.append(load(7, wout.at[pl.ds(pl.multiple_of(x * 128, 128), 128)], wo))

    barrier = pltpu.get_barrier_semaphore()

    def hello(to_zy, to_x, to_lat):
        pl.semaphore_signal(
            barrier,
            inc=1,
            device_id={"lon": to_zy * X + to_x, "lat": to_lat},
            device_id_type=pl.DeviceIdType.MESH,
        )

    other_zy = (1 - z) * Y + y
    for dx in range(1, X):
        hello(zy, (x + dx) % X, lat)
    hello(zy, x, sib)

    @pl.loop(1, ZY)
    def _(d):
        hello((zy + d) % ZY, x, lat)

    hello(core * Y, x, down)
    hello((1 - core) * Y, x, up)

    plane = lat // 2
    near = jnp.where(plane < 2, 3, 0) * 2 + core
    for i in range(2):
        hello(other_zy, 2 * core + i, near)

    @pl.when(x == 0)
    def _():
        for i in range(X):
            hello((zy + ZY - 1) % ZY, i, lat)

    @pl.when(x == X - 1)
    def _():
        for i in range(X):
            hello((zy + 1) % ZY, i, lat)

    weight_load.wait()
    for q in range(X):
        piece = raw_w[:, 128 * q : 128 * (q + 1)].astype(F32)
        wp[q] = jnp.concatenate([piece, jnp.zeros((8, 128), F32)], axis=0).astype(BF16)

    edge = (mine_of == 0) | (mine_of == ZY - 1)
    sends_weight = x // 2 == core
    crosses = sends_weight & ((plane == 0) | (plane == 3))
    pl.semaphore_wait(
        barrier,
        (X - 1) + (ZY - 1) + 1 + 2 + jnp.where(edge, ZY, 0) + jnp.where(crosses, 2 * X, 0),
    )

    slot = z * 2 + x % 2

    def all_weights(start):
        def across(copy):
            if start:
                copy.start()
            else:
                copy.wait_send()

        @pl.when(crosses)
        def _():
            for k in range(2):
                to_lat = jnp.where(plane == 3, k, 2 + k) * 2 + core
                for t in range(X):
                    across(
                        remote(
                            wp.at[t], w_one.at[slot], w_send.at[X + X * k + t],
                            w_recv.at[slot], other_zy, t, to_lat,
                        )
                    )

        @pl.when(sends_weight)
        def _():
            for t in range(X):
                if start:
                    @pl.when(t == x)
                    def _():
                        pltpu.make_async_copy(
                            wp.at[t], w_one.at[slot], w_recv.at[slot]
                        ).start()

                @pl.when(t != x)
                def _():
                    across(
                        remote(
                            wp.at[t], w_one.at[slot], w_send.at[t], w_recv.at[slot],
                            zy, t, lat,
                        )
                    )

    all_weights(True)

    def relayout(which, dst):
        for r in range(16):
            for q in range(4):
                piece = raw[which, r, :, 128 * q : 128 * (q + 1)].astype(F32)
                flat[pl.ds(16 * r + q, 4, stride=4), :] = piece
        dst[...] = flat[0:256, :].astype(BF16).reshape(16, 16, 128)

    state_load.wait()
    relayout(0, st)

    def all_rows(src, dst, send_sem, recv_sem, start):
        @pl.loop(0, ZY)
        def _(t):
            if start:
                @pl.when(t == mine_of)
                def _():
                    pltpu.make_async_copy(src.at[t], dst, recv_sem).start()

            @pl.when(t != mine_of)
            def _():
                copy = remote(
                    src.at[t], dst, send_sem.at[t], recv_sem, owner(t), x, lat
                )
                if start:
                    copy.start()
                else:
                    copy.wait_send()

    def middle_rows(start):
        for i, t, to in ((0, Y - 1, Y), (1, Y, Y - 1)):
            dst = rows.at[2 * i, zy, x]
            if start:
                @pl.when(to == mine_of)
                def _():
                    pltpu.make_async_copy(st.at[t], dst, side_recv.at[i]).start()

            @pl.when(to != mine_of)
            def _():
                copy = remote(
                    st.at[t], dst, middle_send.at[i], side_recv.at[i], owner(to), x, lat
                )
                if start:
                    copy.start()
                else:
                    copy.wait_send()

    def side_rows(start):
        for i, last, middle, to_lat, step in (
            (0, ZY - 1, Y - 1, up, 1),
            (1, 0, Y, down, -1),
        ):
            @pl.when(mine_of != middle)
            def _():
                to_zy = jnp.where(mine_of == last, zy, owner(mine_of + step))
                copy = remote(
                    rows.at[1, :, x], rows.at[2 * i, :, x], side_send.at[i], side_recv.at[i],
                    to_zy, x, jnp.where(mine_of == last, to_lat, lat),
                )
                if start:
                    copy.start()
                else:
                    copy.wait_send()

    all_rows(st, rows.at[1, zy, x], row_send, row_recv, True)
    middle_rows(True)

    def half(place, which):
        return pl.ds(pl.multiple_of((place * 2 + which) * 144, 16), 144)

    def take_weight(part):
        both = []
        for i in range(2):
            at = w_one.at[2 * part + i]
            pltpu.make_async_copy(at, at, w_recv.at[2 * part + i]).wait()
            both.append(w_one[2 * part + i].astype(F32)[:72])
        w_all[part, half(y, core), :] = jnp.concatenate(both, axis=0).astype(BF16)

    right = z * Y + (y + 1) % Y
    left = z * Y + (y + Y - 1) % Y

    def ring(turn, place, to):
        return push(w_all.at[(z, 1 - z)[turn], half(place, core)], to, x, lat)

    rights = [[]]
    lefts = [[]]
    pair = []
    for turn in range(2):
        take_weight((z, 1 - z)[turn])
        rights[0].append(ring(turn, y, right))
        lefts[0].append(ring(turn, y, left))
        pair.append(push(w_all.at[(z, 1 - z)[turn], half(y, core)], zy, x, sib))

    def forward(step, turn):
        turns = (
            (rights, right, (y + Y - 1 - step) % Y, 0),
            (lefts, left, (y + 1 + step) % Y, 1),
        )
        for copies, to, got, last in turns:
            if turn == 0:
                copies.append([None, None])
            copy = copies[step][turn]
            if copy is None:
                continue
            copy.wait_recv()
            if step < 2 or (step == 2 and turn == last):
                copies[step + 1][turn] = ring(turn, got, to)
            pair.append(push(w_all.at[(z, 1 - z)[turn], half(got, core)], zy, x, sib))

    def round_x(whole, west_half, east_half):
        return (
            push(whole, zy, east, lat),
            push(whole, zy, west, lat),
            west_half,
            east_half,
        )

    def round_x_on(to_east, to_west, west_half, east_half):
        to_east.wait_recv()
        on_east = push(west_half, zy, east, lat)
        to_west.wait_recv()
        return on_east, push(east_half, zy, west, lat)

    forward(0, 0)
    pltpu.make_async_copy(rows.at[1, :, x], rows.at[1, :, x], row_recv).wait()
    side_rows(True)
    row_x = round_x(rows.at[1, :, x], rows.at[1, 0:8, west], rows.at[1, 8:16, east])
    forward(0, 1)
    cot_load.wait()
    relayout(1, ct)
    forward(1, 0)
    row_on = round_x_on(*row_x)
    for i in range(2):
        at = rows.at[2 * i, :, x]
        pltpu.make_async_copy(at, at, side_recv.at[i]).wait()
    above_east = push(rows.at[0, :, x], zy, east, lat)
    below_west = push(rows.at[2, :, x], zy, west, lat)
    below_east = push(rows.at[2, :, x], zy, east, lat)
    above_west = push(rows.at[0, :, x], zy, west, lat)
    forward(1, 1)
    forward(2, 0)
    all_rows(ct, cots.at[zy, x], cot_send, cot_recv, True)
    above_east.wait_recv()
    above_on = push(rows.at[0, :, west], zy, east, lat)
    below_west.wait_recv()
    below_on = push(rows.at[2, :, east], zy, west, lat)
    forward(2, 1)

    def whole_row(a):
        flat[...] = rows[a].reshape(1024, 128).astype(F32)
        for q in range(4):
            part = flat[pl.ds(q, 256, stride=4), :]
            if a == 0:
                part = jnp.where(row == 0, 0.0, part)
            if a == 2:
                part = jnp.where(row == ROWS - 1, 0.0, part)
            grid[a, :, 128 * q : 128 * (q + 1)] = part.astype(BF16)

    for copy in row_on:
        copy.wait_recv()
    whole_row(1)
    forward(3, 0)
    forward(3, 1)

    pltpu.make_async_copy(cots.at[:, x], cots.at[:, x], cot_recv).wait()
    cot_x = [push(cots.at[:, x], zy, (x + dx) % X, lat) for dx in range(1, X)]

    below_east.wait_recv()
    above_west.wait_recv()
    above_on.wait_recv()
    whole_row(0)
    below_on.wait_recv()
    whole_row(2)
    for copy in loads:
        copy.wait()
    for copy in pair:
        copy.wait_recv()

    def tap(i):
        if i < 4:
            return w_all[0, 512 * i : 512 * (i + 1), :]
        if i > 4:
            return w_all[1, 512 * i - 2304 : 512 * (i + 1) - 2304, :]
        return jnp.concatenate([w_all[0, 2048:2304, :], w_all[1, 0:256, :]], axis=0)

    two = jnp.zeros((256, 256), F32)
    third = jnp.zeros((256, 128), F32)
    for a in (1, 0, 2):
        two = two + dot(grid[a], jnp.concatenate([tap(3 * a), tap(3 * a + 1)], axis=1))
        third = third + dot(grid[a], tap(3 * a + 2))
    preact = (
        bias[pl.ds(x, 1), :]
        + pltpu.roll(two[:, 0:128], 1, 0)
        + two[:, 128:256]
        + pltpu.roll(third, 255, 0)
    )
    pre[...] = preact
    acts[x] = (preact * jax.nn.sigmoid(preact)).astype(BF16)
    low, high = slice(0, 128), slice(128, 256)
    act_x = [push(acts.at[x], zy, (x + dx) % X, lat) for dx in (2, 1, 3)]

    for copy in cot_x:
        copy.wait_recv()
    flat[...] = cots[...].reshape(1024, 128).astype(F32)
    for q in range(4):
        part = flat[pl.ds(q, 256, stride=4), :].astype(BF16)
        cot_grid[:, 128 * q : 128 * (q + 1)] = part
        cot_blocks[q] = part

    out_grad = dot(cot_grid[...], wo[...], NT).astype(BF16)
    for copy in act_x:
        copy.wait_recv()
    activated = jnp.concatenate([acts[s] for s in range(X)], axis=1)
    projected = dot(activated, wq[...]).astype(BF16)
    queries, keys, values = (projected[:, 128 * t : 128 * (t + 1)] for t in range(3))
    capped = jnp.tanh(dot(queries, keys, NT) * (INV_ROOT / CAP))
    expo = jnp.exp(CAP * capped)
    probs = expo / jnp.sum(expo, axis=-1, keepdims=True)
    probs_b = probs.astype(BF16)
    attended = dot(probs_b, values).astype(BF16)
    centre = jnp.sum(out_grad.astype(F32) * attended.astype(F32), axis=-1, keepdims=True)
    score_grad = (
        probs * (dot(out_grad, values, NT) - centre) * (1.0 - capped * capped) * INV_ROOT
    ).astype(BF16)
    grads = jnp.concatenate(
        [
            dot(score_grad, keys).astype(BF16),
            dot(score_grad, queries, TN).astype(BF16),
            dot(probs_b, out_grad, TN).astype(BF16),
        ],
        axis=1,
    )
    head_part = dot(grads, wq[...], NT)
    for q in range(X):
        blocks[q] = head_part[:, 128 * q : 128 * (q + 1)]

    part_x = []
    for half_of in range(2):
        at = (low, high)[half_of]
        for dx in (2, 1, 3):
            i = 3 * half_of + dx - 1
            to = (x + dx) % X
            parts[i] = blocks[to, at].astype(BF16)
            part_x.append(push_to(parts.at[i], parts_in.at[i], zy, to, lat))
    preact = pre[...]
    s = jax.nn.sigmoid(preact)
    pre[...] = s * (1.0 + preact * (1.0 - s))

    def all_pres(first, start):
        @pl.loop(first, first + 8)
        def _(t):
            dst = pres.at[1 + mine_of]
            if start:
                @pl.when(t == zy)
                def _():
                    pltpu.make_async_copy(own_pre.at[t], dst, pre_recv).start()

            @pl.when(t != zy)
            def _():
                copy = remote(own_pre.at[t], dst, pre_send.at[t], pre_recv, t, x, lat)
                if start:
                    copy.start()
                else:
                    copy.wait_send()

        def ends(slot, to_lat):
            @pl.loop(first, first + 8)
            def _(t):
                copy = remote(
                    own_pre.at[t], pres.at[slot], end_send.at[t], pre_recv, t, x, to_lat
                )
                if start:
                    copy.start()
                else:
                    copy.wait_send()

        @pl.when(mine_of == ZY - 1)
        def _():
            ends(0, up)

        @pl.when(mine_of == 0)
        def _():
            ends(ZY + 1, down)

    for half_of in range(2):
        at = (low, high)[half_of]
        grad_act = blocks[x, at] + cot_blocks[x, at].astype(F32)
        for i in range(3 * half_of, 3 * half_of + 3):
            part_x[i].wait_recv()
        for i in range(3 * half_of, 3 * half_of + 3):
            grad_act = grad_act + parts_in[i].astype(F32)
        own_pre[8 * half_of : 8 * (half_of + 1)] = (
            (grad_act * pre[at]).astype(BF16).reshape(8, 16, 128)
        )
        all_pres(8 * half_of, True)

    pltpu.make_async_copy(pres, pres, pre_recv).wait()

    @pl.when(lat == 0)
    def _():
        pres[0] = jnp.zeros((16, 128), BF16)

    @pl.when(lat == LATS - 1)
    def _():
        pres[ZY + 1] = jnp.zeros((16, 128), BF16)

    around = jnp.concatenate(
        [pres[2 - a : 2 - a + ZY].reshape(256, 128) for a in range(3)], axis=1
    )
    column = lax.broadcasted_iota(jnp.int32, (256, 256), 0) % 16
    sum_x = []
    for h in range(2):
        at = slice(256 * h, 256 * (h + 1))
        result = jnp.zeros((256, 256), F32)
        for b in range(3):
            taps = jnp.concatenate([tap(3 * a + b)[at] for a in range(3)], axis=1)
            acc = dot(around, taps, NT)
            if b != 1:
                for q in range(2):
                    shifted[...] = acc[:, 128 * q : 128 * (q + 1)]
                    rim = shifted[pl.ds(0 if b == 0 else 15, 16, stride=16), :]
                    rims[b // 2, h, q] = rim.astype(BF16)
            if b == 0:
                acc = jnp.where(column == 15, 0.0, pltpu.roll(acc, 255, 0))
            if b == 2:
                acc = jnp.where(column == 0, 0.0, pltpu.roll(acc, 1, 0))
            result = result + acc
        for q in range(2):
            base = 512 * h + 256 * q
            flat[base : base + 256, :] = result[:, 128 * q : 128 * (q + 1)]
            for to in range(X):
                for j in range(4):
                    piece = flat[pl.ds(base + 4 * to + j, 16, stride=16), :]
                    mine[to, h, q, j] = piece.astype(BF16)
        for dx in (2, 1, 3):
            to = (x + dx) % X
            sum_x.append(push_to(mine.at[to, h], sums_in.at[3 * h + dx - 1], zy, to, lat))

    rim_west = remote(
        rims.at[0], rims_in.at[x], rim_send.at[0], rim_recv.at[x],
        (zy + ZY - 1) % ZY, X - 1, lat,
    )
    rim_east = remote(
        rims.at[1], rims_in.at[x], rim_send.at[1], rim_recv.at[x], (zy + 1) % ZY, 0, lat
    )
    rim_west.start()
    rim_east.start()

    for h in range(2):
        total = mine[x, h].astype(F32)
        for copy in sum_x[3 * h : 3 * h + 3]:
            copy.wait_recv()
        for i in range(X - 1):
            total = total + sums_in[3 * h + i].astype(F32)
        flat[128 * h : 128 * (h + 1), :] = total.reshape(128, 128)

    def add_rims(j):
        for i in range(X):
            pltpu.make_async_copy(rims_in.at[i], rims_in.at[i], rim_recv.at[i]).wait()
        for q in range(4):
            at = slice(64 * q + 16 * j, 64 * q + 16 * (j + 1))
            total = flat[at]
            for i in range(X):
                total = total + rims_in[i, q // 2, q % 2].astype(F32)
            flat[at] = total

    @pl.when(x == 0)
    def _():
        add_rims(0)

    @pl.when(x == X - 1)
    def _():
        add_rims(3)

    for t in range(ZY):
        out[t] = flat[pl.ds(t, 16, stride=16), :].astype(BF16)

    rim_west.wait_send()
    rim_east.wait_send()
    for copy in started:
        copy.wait_send()
    all_weights(False)
    all_rows(st, rows.at[1, zy, x], row_send, row_recv, False)
    all_rows(ct, cots.at[zy, x], cot_send, cot_recv, False)
    middle_rows(False)
    side_rows(False)
    all_pres(0, False)
    all_pres(8, False)


PUSHES = 80


def body(state, conv_weight, conv_bias, w_qkv, w_out, cotangent):
    vmem = pl.BlockSpec(memory_space=pltpu.VMEM)
    anywhere = pl.BlockSpec(memory_space=pl.ANY)
    dma = pltpu.SemaphoreType.DMA
    out = pl.pallas_call(
        kernel,
        out_shape=jax.ShapeDtypeStruct((ZY, 16, 128), BF16),
        in_specs=[anywhere] * 6,
        out_specs=vmem,
        scratch_shapes=[
            pltpu.VMEM((2, 16, 4, 512), BF16),
            pltpu.VMEM((72, 512), BF16),
            pltpu.VMEM((ZY, 16, 128), BF16),
            pltpu.VMEM((ZY, 16, 128), BF16),
            pltpu.VMEM((X, 80, 128), BF16),
            pltpu.VMEM((X, 128), F32),
            pltpu.VMEM((3, ZY, X, 16, 128), BF16),
            pltpu.VMEM((ZY, X, 16, 128), BF16),
            pltpu.VMEM((1024, 128), F32),
            pltpu.VMEM((3, 256, 512), BF16),
            pltpu.VMEM((256, 512), BF16),
            pltpu.VMEM((4, 256, 128), BF16),
            pltpu.VMEM((4, 80, 128), BF16),
            pltpu.VMEM((2, 2304, 128), BF16),
            pltpu.VMEM((512, 384), BF16),
            pltpu.VMEM((128, 512), BF16),
            pltpu.VMEM((256, 128), F32),
            pltpu.VMEM((X, 256, 128), BF16),
            pltpu.VMEM((X, 256, 128), F32),
            pltpu.VMEM((6, 128, 128), BF16),
            pltpu.VMEM((6, 128, 128), BF16),
            pltpu.VMEM((ZY, 16, 128), BF16),
            pltpu.VMEM((ZY + 2, 16, 128), BF16),
            pltpu.VMEM((256, 128), F32),
            pltpu.VMEM((X, 2, 2, 4, ZY, 128), BF16),
            pltpu.VMEM((6, 2, 4, ZY, 128), BF16),
            pltpu.VMEM((2, 2, 2, ZY, 128), BF16),
            pltpu.VMEM((X, 2, 2, ZY, 128), BF16),
            dma((8,)),
            dma((3 * X,)),
            dma((4,)),
            dma((ZY,)),
            dma,
            dma((ZY,)),
            dma,
            dma((ZY,)),
            dma,
            dma((ZY,)),
            dma((2,)),
            dma((X,)),
            dma((2,)),
            dma((2,)),
            dma((2,)),
            dma((PUSHES,)),
            dma((PUSHES,)),
        ],
        compiler_params=pltpu.CompilerParams(
            collective_id=0, has_side_effects=True, vmem_limit_bytes=VMEM_LIMIT
        ),
    )(state, cotangent, conv_weight, conv_bias.reshape(X, 128), w_qkv, w_out)
    return out.reshape(16, 4, 4, 128).transpose(0, 2, 1, 3).reshape(16, 4, 512)


def solution(mesh):
    return jax.shard_map(
        body,
        mesh=mesh,
        in_specs=(P("lat", "lon", None), P("lon", None), P(), P(), P(), P("lat", "lon", None)),
        out_specs=P("lat", "lon", None),
        check_vma=False,
    )
```

```python
import functools
import math

import jax
import jax.numpy as jnp
from jax import lax
from jax.experimental import pallas as pl
from jax.experimental.pallas import tpu as pltpu
from jax.sharding import PartitionSpec as P

X = 4
Y = 8
ZY = 16
LATS = 8
ROWS = ZY * LATS
CAP = 20.0
INV_ROOT = 1.0 / math.sqrt(128.0)
F32 = jnp.float32
BF16 = jnp.bfloat16
VMEM_LIMIT = 60 * 1024 * 1024

NN = (((1,), (0,)), ((), ()))
NT = (((1,), (1,)), ((), ()))
TN = (((0,), (0,)), ((), ()))


def dot(a, b, dims=NN):
    return lax.dot_general(a, b, dims, preferred_element_type=F32)


def kernel(
    st_hbm, ct_hbm, cw_hbm, bias_hbm, wqkv, wout, out,
    raw, raw_w, st, ct, wp, bias,
    rows, cots, flat, grid, cot_grid, cot_blocks, w_one, w_all, wq, wo,
    pre, acts, blocks, parts, parts_in, own_pre, pres, shifted, mine, sums_in, rims, rims_in,
    w_turned, wq_turned,
    load_sem, w_send, w_recv, row_send, row_recv, cot_send, cot_recv, pre_send, pre_recv,
    end_send, rim_send, rim_recv, middle_send, side_send, side_recv,
    send, recv,
):
    lon = lax.axis_index("lon")
    lat = lax.axis_index("lat")
    zy, x = lon // X, lon % X
    z, y = zy // Y, zy % Y
    core = lat % 2
    sib = lat + 1 - 2 * core
    mine_of = jnp.where(z == core, y, ZY - 1 - y)
    row = lat * ZY + mine_of
    up, down = (lat + 1) % LATS, (lat + LATS - 1) % LATS

    def owner(t):
        return jnp.where(t < Y, core * Y + t, (1 - core) * Y + ZY - 1 - t)

    east, west = (x + 1) % X, (x + X - 1) % X

    def remote(src, dst, send_sem, recv_sem, to_zy, to_x, to_lat):
        return pltpu.make_async_remote_copy(
            src_ref=src,
            dst_ref=dst,
            send_sem=send_sem,
            recv_sem=recv_sem,
            device_id={"lon": to_zy * X + to_x, "lat": to_lat},
            device_id_type=pl.DeviceIdType.MESH,
        )

    started = []

    def push_to(src, dst, to_zy, to_x, to_lat):
        i = len(started)
        copy = remote(src, dst, send.at[i], recv.at[i], to_zy, to_x, to_lat)
        copy.start()
        started.append(copy)
        return copy

    def push(ref, to_zy, to_x, to_lat):
        return push_to(ref, ref, to_zy, to_x, to_lat)

    def load(i, src, dst):
        copy = pltpu.make_async_copy(src, dst, load_sem.at[i])
        copy.start()
        return copy

    weight_load = load(0, cw_hbm, raw_w)
    state_load = load(1, st_hbm, raw.at[0])
    cot_load = load(2, ct_hbm, raw.at[1])
    loads = [load(3, bias_hbm, bias)]
    for t in range(3):
        source = wqkv.at[:, pl.ds(pl.multiple_of(t * 512 + x * 128, 128), 128)]
        loads.append(load(4 + t, source, wq.at[:, 128 * t : 128 * (t + 1)]))
    loads.append(load(7, wout.at[pl.ds(pl.multiple_of(x * 128, 128), 128)], wo))

    barrier = pltpu.get_barrier_semaphore()

    def hello(to_zy, to_x, to_lat):
        pl.semaphore_signal(
            barrier,
            inc=1,
            device_id={"lon": to_zy * X + to_x, "lat": to_lat},
            device_id_type=pl.DeviceIdType.MESH,
        )

    other_zy = (1 - z) * Y + y
    for dx in range(1, X):
        hello(zy, (x + dx) % X, lat)
    hello(zy, x, sib)

    @pl.loop(1, ZY)
    def _(d):
        hello((zy + d) % ZY, x, lat)

    hello(core * Y, x, down)
    hello((1 - core) * Y, x, up)

    plane = lat // 2
    near = jnp.where(plane < 2, 3, 0) * 2 + core
    for i in range(2):
        hello(other_zy, 2 * core + i, near)

    @pl.when(x == 0)
    def _():
        for i in range(X):
            hello((zy + ZY - 1) % ZY, i, lat)

    @pl.when(x == X - 1)
    def _():
        for i in range(X):
            hello((zy + 1) % ZY, i, lat)

    weight_load.wait()
    for q in range(X):
        piece = raw_w[:, 128 * q : 128 * (q + 1)].astype(F32)
        wp[q] = jnp.concatenate([piece, jnp.zeros((8, 128), F32)], axis=0).astype(BF16)

    edge = (mine_of == 0) | (mine_of == ZY - 1)
    sends_weight = x // 2 == core
    crosses = sends_weight & ((plane == 0) | (plane == 3))
    pl.semaphore_wait(
        barrier,
        (X - 1) + (ZY - 1) + 1 + 2 + jnp.where(edge, ZY, 0) + jnp.where(crosses, 2 * X, 0),
    )

    slot = z * 2 + x % 2

    def all_weights(start):
        def across(copy):
            if start:
                copy.start()
            else:
                copy.wait_send()

        @pl.when(crosses)
        def _():
            for k in range(2):
                to_lat = jnp.where(plane == 3, k, 2 + k) * 2 + core
                for t in range(X):
                    across(
                        remote(
                            wp.at[t], w_one.at[slot], w_send.at[X + X * k + t],
                            w_recv.at[slot], other_zy, t, to_lat,
                        )
                    )

        @pl.when(sends_weight)
        def _():
            for t in range(X):
                if start:
                    @pl.when(t == x)
                    def _():
                        pltpu.make_async_copy(
                            wp.at[t], w_one.at[slot], w_recv.at[slot]
                        ).start()

                @pl.when(t != x)
                def _():
                    across(
                        remote(
                            wp.at[t], w_one.at[slot], w_send.at[t], w_recv.at[slot],
                            zy, t, lat,
                        )
                    )

    all_weights(True)

    def relayout(which, dst):
        for r in range(16):
            for q in range(4):
                piece = raw[which, r, :, 128 * q : 128 * (q + 1)].astype(F32)
                flat[pl.ds(16 * r + q, 4, stride=4), :] = piece
        dst[...] = flat[0:256, :].astype(BF16).reshape(16, 16, 128)

    state_load.wait()
    relayout(0, st)

    def all_rows(src, dst, send_sem, recv_sem, start):
        @pl.loop(0, ZY)
        def _(t):
            if start:
                @pl.when(t == mine_of)
                def _():
                    pltpu.make_async_copy(src.at[t], dst, recv_sem).start()

            @pl.when(t != mine_of)
            def _():
                copy = remote(
                    src.at[t], dst, send_sem.at[t], recv_sem, owner(t), x, lat
                )
                if start:
                    copy.start()
                else:
                    copy.wait_send()

    def middle_rows(start):
        for i, t, to in ((0, Y - 1, Y), (1, Y, Y - 1)):
            dst = rows.at[2 * i, zy, x]
            if start:
                @pl.when(to == mine_of)
                def _():
                    pltpu.make_async_copy(st.at[t], dst, side_recv.at[i]).start()

            @pl.when(to != mine_of)
            def _():
                copy = remote(
                    st.at[t], dst, middle_send.at[i], side_recv.at[i], owner(to), x, lat
                )
                if start:
                    copy.start()
                else:
                    copy.wait_send()

    def side_rows(start):
        for i, last, middle, to_lat, step in (
            (0, ZY - 1, Y - 1, up, 1),
            (1, 0, Y, down, -1),
        ):
            @pl.when(mine_of != middle)
            def _():
                to_zy = jnp.where(mine_of == last, zy, owner(mine_of + step))
                copy = remote(
                    rows.at[1, :, x], rows.at[2 * i, :, x], side_send.at[i], side_recv.at[i],
                    to_zy, x, jnp.where(mine_of == last, to_lat, lat),
                )
                if start:
                    copy.start()
                else:
                    copy.wait_send()

    all_rows(st, rows.at[1, zy, x], row_send, row_recv, True)
    middle_rows(True)

    def half(place, which):
        return pl.ds(pl.multiple_of((place * 2 + which) * 144, 16), 144)

    def take_weight(part):
        both = []
        for i in range(2):
            at = w_one.at[2 * part + i]
            pltpu.make_async_copy(at, at, w_recv.at[2 * part + i]).wait()
            both.append(w_one[2 * part + i].astype(F32)[:72])
        w_all[part, half(y, core), :] = jnp.concatenate(both, axis=0).astype(BF16)

    right = z * Y + (y + 1) % Y
    left = z * Y + (y + Y - 1) % Y

    def ring(turn, place, to):
        return push(w_all.at[(z, 1 - z)[turn], half(place, core)], to, x, lat)

    rights = [[]]
    lefts = [[]]
    pair = []
    for turn in range(2):
        take_weight((z, 1 - z)[turn])
        rights[0].append(ring(turn, y, right))
        lefts[0].append(ring(turn, y, left))
        pair.append(push(w_all.at[(z, 1 - z)[turn], half(y, core)], zy, x, sib))

    def forward(step, turn):
        turns = (
            (rights, right, (y + Y - 1 - step) % Y, 0),
            (lefts, left, (y + 1 + step) % Y, 1),
        )
        for copies, to, got, last in turns:
            if turn == 0:
                copies.append([None, None])
            copy = copies[step][turn]
            if copy is None:
                continue
            copy.wait_recv()
            if step < 2 or (step == 2 and turn == last):
                copies[step + 1][turn] = ring(turn, got, to)
            pair.append(push(w_all.at[(z, 1 - z)[turn], half(got, core)], zy, x, sib))

    def round_x(whole, west_half, east_half):
        return (
            push(whole, zy, east, lat),
            push(whole, zy, west, lat),
            west_half,
            east_half,
        )

    def round_x_on(to_east, to_west, west_half, east_half):
        to_east.wait_recv()
        on_east = push(west_half, zy, east, lat)
        to_west.wait_recv()
        return on_east, push(east_half, zy, west, lat)

    cot_load.wait()
    relayout(1, ct)
    all_rows(ct, cots.at[zy, x], cot_send, cot_recv, True)

    forward(0, 0)
    pltpu.make_async_copy(rows.at[1, :, x], rows.at[1, :, x], row_recv).wait()
    side_rows(True)
    row_x = round_x(rows.at[1, :, x], rows.at[1, 0:8, west], rows.at[1, 8:16, east])
    forward(0, 1)
    forward(1, 0)
    row_on = round_x_on(*row_x)
    for i in range(2):
        at = rows.at[2 * i, :, x]
        pltpu.make_async_copy(at, at, side_recv.at[i]).wait()
    above_east = push(rows.at[0, :, x], zy, east, lat)
    below_west = push(rows.at[2, :, x], zy, west, lat)
    below_east = push(rows.at[2, :, x], zy, east, lat)
    above_west = push(rows.at[0, :, x], zy, west, lat)
    forward(1, 1)
    forward(2, 0)
    above_east.wait_recv()
    above_on = push(rows.at[0, :, west], zy, east, lat)
    below_west.wait_recv()
    below_on = push(rows.at[2, :, east], zy, west, lat)
    forward(2, 1)

    def whole_row(a):
        flat[...] = rows[a].reshape(1024, 128).astype(F32)
        for q in range(4):
            part = flat[pl.ds(q, 256, stride=4), :]
            if a == 0:
                part = jnp.where(row == 0, 0.0, part)
            if a == 2:
                part = jnp.where(row == ROWS - 1, 0.0, part)
            grid[a, :, 128 * q : 128 * (q + 1)] = part.astype(BF16)

    for copy in row_on:
        copy.wait_recv()
    whole_row(1)
    forward(3, 0)
    forward(3, 1)

    pltpu.make_async_copy(cots.at[:, x], cots.at[:, x], cot_recv).wait()
    cot_x = [push(cots.at[:, x], zy, (x + dx) % X, lat) for dx in range(1, X)]

    below_east.wait_recv()
    above_west.wait_recv()
    above_on.wait_recv()
    whole_row(0)
    below_on.wait_recv()
    whole_row(2)
    for copy in loads:
        copy.wait()
    for copy in pair:
        copy.wait_recv()

    def tap(i):
        if i < 4:
            return w_all[0, 512 * i : 512 * (i + 1), :]
        if i > 4:
            return w_all[1, 512 * i - 2304 : 512 * (i + 1) - 2304, :]
        return jnp.concatenate([w_all[0, 2048:2304, :], w_all[1, 0:256, :]], axis=0)

    two = jnp.zeros((256, 256), F32)
    third = jnp.zeros((256, 128), F32)
    for a in (1, 0, 2):
        two = two + dot(grid[a], jnp.concatenate([tap(3 * a), tap(3 * a + 1)], axis=1))
        third = third + dot(grid[a], tap(3 * a + 2))
    preact = (
        bias[pl.ds(x, 1), :]
        + pltpu.roll(two[:, 0:128], 1, 0)
        + two[:, 128:256]
        + pltpu.roll(third, 255, 0)
    )
    pre[...] = preact
    acts[x] = (preact * jax.nn.sigmoid(preact)).astype(BF16)
    low, high = slice(0, 128), slice(128, 256)
    act_x = [push(acts.at[x], zy, (x + dx) % X, lat) for dx in (2, 1, 3)]

    for a in range(3):
        for b in range(3):
            w_turned[b, 128 * a : 128 * (a + 1), :] = tap(3 * a + b).T
    for t in range(3):
        wq_turned[128 * t : 128 * (t + 1), :] = wq[:, 128 * t : 128 * (t + 1)].T

    for copy in cot_x:
        copy.wait_recv()
    flat[...] = cots[...].reshape(1024, 128).astype(F32)
    for q in range(4):
        part = flat[pl.ds(q, 256, stride=4), :].astype(BF16)
        cot_grid[:, 128 * q : 128 * (q + 1)] = part
        cot_blocks[q] = part

    out_grad = dot(cot_grid[...], wo[...], NT).astype(BF16)
    for copy in act_x:
        copy.wait_recv()
    activated = jnp.concatenate([acts[s] for s in range(X)], axis=1)
    projected = dot(activated, wq[...]).astype(BF16)
    queries, keys, values = (projected[:, 128 * t : 128 * (t + 1)] for t in range(3))
    capped = jnp.tanh(dot(queries, keys, NT) * (INV_ROOT / CAP))
    expo = jnp.exp(CAP * capped)
    probs = expo / jnp.sum(expo, axis=-1, keepdims=True)
    probs_b = probs.astype(BF16)
    attended = dot(probs_b, values).astype(BF16)
    centre = jnp.sum(out_grad.astype(F32) * attended.astype(F32), axis=-1, keepdims=True)
    score_grad = (
        probs * (dot(out_grad, values, NT) - centre) * (1.0 - capped * capped) * INV_ROOT
    ).astype(BF16)
    grads = jnp.concatenate(
        [
            dot(score_grad, keys).astype(BF16),
            dot(score_grad, queries, TN).astype(BF16),
            dot(probs_b, out_grad, TN).astype(BF16),
        ],
        axis=1,
    )
    head_part = dot(grads, wq_turned[...])
    for q in range(X):
        blocks[q] = head_part[:, 128 * q : 128 * (q + 1)]

    part_x = []
    for half_of in range(2):
        at = (low, high)[half_of]
        for dx in (2, 1, 3):
            i = 3 * half_of + dx - 1
            to = (x + dx) % X
            parts[i] = blocks[to, at].astype(BF16)
            part_x.append(push_to(parts.at[i], parts_in.at[i], zy, to, lat))
    preact = pre[...]
    s = jax.nn.sigmoid(preact)
    pre[...] = s * (1.0 + preact * (1.0 - s))

    def all_pres(first, start):
        @pl.loop(first, first + 8)
        def _(t):
            dst = pres.at[1 + mine_of]
            if start:
                @pl.when(t == zy)
                def _():
                    pltpu.make_async_copy(own_pre.at[t], dst, pre_recv).start()

            @pl.when(t != zy)
            def _():
                copy = remote(own_pre.at[t], dst, pre_send.at[t], pre_recv, t, x, lat)
                if start:
                    copy.start()
                else:
                    copy.wait_send()

        def ends(slot, to_lat):
            @pl.loop(first, first + 8)
            def _(t):
                copy = remote(
                    own_pre.at[t], pres.at[slot], end_send.at[t], pre_recv, t, x, to_lat
                )
                if start:
                    copy.start()
                else:
                    copy.wait_send()

        @pl.when(mine_of == ZY - 1)
        def _():
            ends(0, up)

        @pl.when(mine_of == 0)
        def _():
            ends(ZY + 1, down)

    for half_of in range(2):
        at = (low, high)[half_of]
        grad_act = blocks[x, at] + cot_blocks[x, at].astype(F32)
        for i in range(3 * half_of, 3 * half_of + 3):
            part_x[i].wait_recv()
        for i in range(3 * half_of, 3 * half_of + 3):
            grad_act = grad_act + parts_in[i].astype(F32)
        own_pre[8 * half_of : 8 * (half_of + 1)] = (
            (grad_act * pre[at]).astype(BF16).reshape(8, 16, 128)
        )
        all_pres(8 * half_of, True)

    pltpu.make_async_copy(pres, pres, pre_recv).wait()

    @pl.when(lat == 0)
    def _():
        pres[0] = jnp.zeros((16, 128), BF16)

    @pl.when(lat == LATS - 1)
    def _():
        pres[ZY + 1] = jnp.zeros((16, 128), BF16)

    around = jnp.concatenate(
        [pres[2 - a : 2 - a + ZY].reshape(256, 128) for a in range(3)], axis=1
    )
    column = lax.broadcasted_iota(jnp.int32, (256, 256), 0) % 16
    sum_x = []
    for h in range(2):
        at = slice(256 * h, 256 * (h + 1))
        result = jnp.zeros((256, 256), F32)
        for b in range(3):
            acc = dot(around, w_turned[b, :, at])
            if b != 1:
                for q in range(2):
                    shifted[...] = acc[:, 128 * q : 128 * (q + 1)]
                    rim = shifted[pl.ds(0 if b == 0 else 15, 16, stride=16), :]
                    rims[b // 2, h, q] = rim.astype(BF16)
            if b == 0:
                acc = jnp.where(column == 15, 0.0, pltpu.roll(acc, 255, 0))
            if b == 2:
                acc = jnp.where(column == 0, 0.0, pltpu.roll(acc, 1, 0))
            result = result + acc
        for q in range(2):
            base = 512 * h + 256 * q
            flat[base : base + 256, :] = result[:, 128 * q : 128 * (q + 1)]
            for to in range(X):
                for j in range(4):
                    piece = flat[pl.ds(base + 4 * to + j, 16, stride=16), :]
                    mine[to, h, q, j] = piece.astype(BF16)
        for dx in (2, 1, 3):
            to = (x + dx) % X
            sum_x.append(push_to(mine.at[to, h], sums_in.at[3 * h + dx - 1], zy, to, lat))

    rim_west = remote(
        rims.at[0], rims_in.at[x], rim_send.at[0], rim_recv.at[x],
        (zy + ZY - 1) % ZY, X - 1, lat,
    )
    rim_east = remote(
        rims.at[1], rims_in.at[x], rim_send.at[1], rim_recv.at[x], (zy + 1) % ZY, 0, lat
    )
    rim_west.start()
    rim_east.start()

    for h in range(2):
        total = mine[x, h].astype(F32)
        for copy in sum_x[3 * h : 3 * h + 3]:
            copy.wait_recv()
        for i in range(X - 1):
            total = total + sums_in[3 * h + i].astype(F32)
        flat[128 * h : 128 * (h + 1), :] = total.reshape(128, 128)

    def add_rims(j):
        for i in range(X):
            pltpu.make_async_copy(rims_in.at[i], rims_in.at[i], rim_recv.at[i]).wait()
        for q in range(4):
            at = slice(64 * q + 16 * j, 64 * q + 16 * (j + 1))
            total = flat[at]
            for i in range(X):
                total = total + rims_in[i, q // 2, q % 2].astype(F32)
            flat[at] = total

    @pl.when(x == 0)
    def _():
        add_rims(0)

    @pl.when(x == X - 1)
    def _():
        add_rims(3)

    for t in range(ZY):
        out[t] = flat[pl.ds(t, 16, stride=16), :].astype(BF16)

    rim_west.wait_send()
    rim_east.wait_send()
    for copy in started:
        copy.wait_send()
    all_weights(False)
    all_rows(st, rows.at[1, zy, x], row_send, row_recv, False)
    all_rows(ct, cots.at[zy, x], cot_send, cot_recv, False)
    middle_rows(False)
    side_rows(False)
    all_pres(0, False)
    all_pres(8, False)


PUSHES = 80


def body(state, conv_weight, conv_bias, w_qkv, w_out, cotangent):
    vmem = pl.BlockSpec(memory_space=pltpu.VMEM)
    anywhere = pl.BlockSpec(memory_space=pl.ANY)
    dma = pltpu.SemaphoreType.DMA
    out = pl.pallas_call(
        kernel,
        out_shape=jax.ShapeDtypeStruct((ZY, 16, 128), BF16),
        in_specs=[anywhere] * 6,
        out_specs=vmem,
        scratch_shapes=[
            pltpu.VMEM((2, 16, 4, 512), BF16),
            pltpu.VMEM((72, 512), BF16),
            pltpu.VMEM((ZY, 16, 128), BF16),
            pltpu.VMEM((ZY, 16, 128), BF16),
            pltpu.VMEM((X, 80, 128), BF16),
            pltpu.VMEM((X, 128), F32),
            pltpu.VMEM((3, ZY, X, 16, 128), BF16),
            pltpu.VMEM((ZY, X, 16, 128), BF16),
            pltpu.VMEM((1024, 128), F32),
            pltpu.VMEM((3, 256, 512), BF16),
            pltpu.VMEM((256, 512), BF16),
            pltpu.VMEM((4, 256, 128), BF16),
            pltpu.VMEM((4, 80, 128), BF16),
            pltpu.VMEM((2, 2304, 128), BF16),
            pltpu.VMEM((512, 384), BF16),
            pltpu.VMEM((128, 512), BF16),
            pltpu.VMEM((256, 128), F32),
            pltpu.VMEM((X, 256, 128), BF16),
            pltpu.VMEM((X, 256, 128), F32),
            pltpu.VMEM((6, 128, 128), BF16),
            pltpu.VMEM((6, 128, 128), BF16),
            pltpu.VMEM((ZY, 16, 128), BF16),
            pltpu.VMEM((ZY + 2, 16, 128), BF16),
            pltpu.VMEM((256, 128), F32),
            pltpu.VMEM((X, 2, 2, 4, ZY, 128), BF16),
            pltpu.VMEM((6, 2, 4, ZY, 128), BF16),
            pltpu.VMEM((2, 2, 2, ZY, 128), BF16),
            pltpu.VMEM((X, 2, 2, ZY, 128), BF16),
            pltpu.VMEM((3, 384, 512), BF16),
            pltpu.VMEM((384, 512), BF16),
            dma((8,)),
            dma((3 * X,)),
            dma((4,)),
            dma((ZY,)),
            dma,
            dma((ZY,)),
            dma,
            dma((ZY,)),
            dma,
            dma((ZY,)),
            dma((2,)),
            dma((X,)),
            dma((2,)),
            dma((2,)),
            dma((2,)),
            dma((PUSHES,)),
            dma((PUSHES,)),
        ],
        compiler_params=pltpu.CompilerParams(
            collective_id=0, has_side_effects=True, vmem_limit_bytes=VMEM_LIMIT
        ),
    )(state, cotangent, conv_weight, conv_bias.reshape(X, 128), w_qkv, w_out)
    return out.reshape(16, 4, 4, 128).transpose(0, 2, 1, 3).reshape(16, 4, 512)


def solution(mesh):
    return jax.shard_map(
        body,
        mesh=mesh,
        in_specs=(P("lat", "lon", None), P("lon", None), P(), P(), P(), P("lat", "lon", None)),
        out_specs=P("lat", "lon", None),
        check_vma=False,
    )
```

```python
import functools
import math

import jax
import jax.numpy as jnp
from jax import lax
from jax.experimental import pallas as pl
from jax.experimental.pallas import tpu as pltpu
from jax.sharding import PartitionSpec as P

X = 4
Y = 8
ZY = 16
LATS = 8
ROWS = ZY * LATS
CAP = 20.0
INV_ROOT = 1.0 / math.sqrt(128.0)
F32 = jnp.float32
BF16 = jnp.bfloat16
VMEM_LIMIT = 60 * 1024 * 1024

NN = (((1,), (0,)), ((), ()))
NT = (((1,), (1,)), ((), ()))
TN = (((0,), (0,)), ((), ()))


def dot(a, b, dims=NN):
    return lax.dot_general(a, b, dims, preferred_element_type=F32)


def kernel(
    st_hbm, ct_hbm, cw_hbm, bias_hbm, wqkv, wout, out,
    raw, raw_w, st, ct, wp, bias,
    rows, cots, flat, grid, cot_grid, cot_blocks, w_one, w_all, wq, wo,
    pre, acts, blocks, parts, parts_in, own_pre, pres, shifted, mine, sums_in, rims, rims_in,
    w_turned, wq_turned,
    load_sem, w_send, w_recv, row_send, row_recv, cot_send, cot_recv, pre_send, pre_recv,
    end_send, rim_send, rim_recv, middle_send, side_send, side_recv,
    send, recv,
):
    lon = lax.axis_index("lon")
    lat = lax.axis_index("lat")
    zy, x = lon // X, lon % X
    z, y = zy // Y, zy % Y
    core = lat % 2
    sib = lat + 1 - 2 * core
    mine_of = jnp.where(z == core, y, ZY - 1 - y)
    row = lat * ZY + mine_of
    up, down = (lat + 1) % LATS, (lat + LATS - 1) % LATS

    def owner(t):
        return jnp.where(t < Y, core * Y + t, (1 - core) * Y + ZY - 1 - t)

    east, west = (x + 1) % X, (x + X - 1) % X

    def remote(src, dst, send_sem, recv_sem, to_zy, to_x, to_lat):
        return pltpu.make_async_remote_copy(
            src_ref=src,
            dst_ref=dst,
            send_sem=send_sem,
            recv_sem=recv_sem,
            device_id={"lon": to_zy * X + to_x, "lat": to_lat},
            device_id_type=pl.DeviceIdType.MESH,
        )

    started = []

    def push_to(src, dst, to_zy, to_x, to_lat):
        i = len(started)
        copy = remote(src, dst, send.at[i], recv.at[i], to_zy, to_x, to_lat)
        copy.start()
        started.append(copy)
        return copy

    drained = [0]

    def drain():
        for copy in started[drained[0] :]:
            copy.wait_send()
        drained[0] = len(started)

    def push(ref, to_zy, to_x, to_lat):
        return push_to(ref, ref, to_zy, to_x, to_lat)

    def load(i, src, dst):
        copy = pltpu.make_async_copy(src, dst, load_sem.at[i])
        copy.start()
        return copy

    weight_load = load(0, cw_hbm, raw_w)
    state_load = load(1, st_hbm, raw.at[0])
    cot_load = load(2, ct_hbm, raw.at[1])
    loads = [load(3, bias_hbm, bias)]
    for t in range(3):
        source = wqkv.at[:, pl.ds(pl.multiple_of(t * 512 + x * 128, 128), 128)]
        loads.append(load(4 + t, source, wq.at[:, 128 * t : 128 * (t + 1)]))
    loads.append(load(7, wout.at[pl.ds(pl.multiple_of(x * 128, 128), 128)], wo))

    barrier = pltpu.get_barrier_semaphore()

    def hello(to_zy, to_x, to_lat):
        pl.semaphore_signal(
            barrier,
            inc=1,
            device_id={"lon": to_zy * X + to_x, "lat": to_lat},
            device_id_type=pl.DeviceIdType.MESH,
        )

    other_zy = (1 - z) * Y + y
    for dx in range(1, X):
        hello(zy, (x + dx) % X, lat)
    hello(zy, x, sib)

    @pl.loop(1, ZY)
    def _(d):
        hello((zy + d) % ZY, x, lat)

    hello(core * Y, x, down)
    hello((1 - core) * Y, x, up)

    plane = lat // 2
    near = jnp.where(plane < 2, 3, 0) * 2 + core
    for i in range(2):
        hello(other_zy, 2 * core + i, near)

    @pl.when(x == 0)
    def _():
        for i in range(X):
            hello((zy + ZY - 1) % ZY, i, lat)

    @pl.when(x == X - 1)
    def _():
        for i in range(X):
            hello((zy + 1) % ZY, i, lat)

    weight_load.wait()
    for q in range(X):
        piece = raw_w[:, 128 * q : 128 * (q + 1)].astype(F32)
        wp[q] = jnp.concatenate([piece, jnp.zeros((8, 128), F32)], axis=0).astype(BF16)

    edge = (mine_of == 0) | (mine_of == ZY - 1)
    sends_weight = x // 2 == core
    crosses = sends_weight & ((plane == 0) | (plane == 3))
    pl.semaphore_wait(
        barrier,
        (X - 1) + (ZY - 1) + 1 + 2 + jnp.where(edge, ZY, 0) + jnp.where(crosses, 2 * X, 0),
    )

    slot = z * 2 + x % 2

    def all_weights(start):
        def across(copy):
            if start:
                copy.start()
            else:
                copy.wait_send()

        @pl.when(crosses)
        def _():
            for k in range(2):
                to_lat = jnp.where(plane == 3, k, 2 + k) * 2 + core
                for t in range(X):
                    across(
                        remote(
                            wp.at[t], w_one.at[slot], w_send.at[X + X * k + t],
                            w_recv.at[slot], other_zy, t, to_lat,
                        )
                    )

        @pl.when(sends_weight)
        def _():
            for t in range(X):
                if start:
                    @pl.when(t == x)
                    def _():
                        pltpu.make_async_copy(
                            wp.at[t], w_one.at[slot], w_recv.at[slot]
                        ).start()

                @pl.when(t != x)
                def _():
                    across(
                        remote(
                            wp.at[t], w_one.at[slot], w_send.at[t], w_recv.at[slot],
                            zy, t, lat,
                        )
                    )

    all_weights(True)

    def relayout(which, dst):
        for r in range(16):
            for q in range(4):
                piece = raw[which, r, :, 128 * q : 128 * (q + 1)].astype(F32)
                flat[pl.ds(16 * r + q, 4, stride=4), :] = piece
        dst[...] = flat[0:256, :].astype(BF16).reshape(16, 16, 128)

    state_load.wait()
    relayout(0, st)

    def all_rows(src, dst, send_sem, recv_sem, start):
        @pl.loop(0, ZY)
        def _(t):
            if start:
                @pl.when(t == mine_of)
                def _():
                    pltpu.make_async_copy(src.at[t], dst, recv_sem).start()

            @pl.when(t != mine_of)
            def _():
                copy = remote(
                    src.at[t], dst, send_sem.at[t], recv_sem, owner(t), x, lat
                )
                if start:
                    copy.start()
                else:
                    copy.wait_send()

    def middle_rows(start):
        for i, t, to in ((0, Y - 1, Y), (1, Y, Y - 1)):
            dst = rows.at[2 * i, zy, x]
            if start:
                @pl.when(to == mine_of)
                def _():
                    pltpu.make_async_copy(st.at[t], dst, side_recv.at[i]).start()

            @pl.when(to != mine_of)
            def _():
                copy = remote(
                    st.at[t], dst, middle_send.at[i], side_recv.at[i], owner(to), x, lat
                )
                if start:
                    copy.start()
                else:
                    copy.wait_send()

    def side_rows(start):
        for i, last, middle, to_lat, step in (
            (0, ZY - 1, Y - 1, up, 1),
            (1, 0, Y, down, -1),
        ):
            @pl.when(mine_of != middle)
            def _():
                to_zy = jnp.where(mine_of == last, zy, owner(mine_of + step))
                copy = remote(
                    rows.at[1, :, x], rows.at[2 * i, :, x], side_send.at[i], side_recv.at[i],
                    to_zy, x, jnp.where(mine_of == last, to_lat, lat),
                )
                if start:
                    copy.start()
                else:
                    copy.wait_send()

    all_rows(st, rows.at[1, zy, x], row_send, row_recv, True)
    middle_rows(True)

    def half(place, which):
        return pl.ds(pl.multiple_of((place * 2 + which) * 144, 16), 144)

    def take_weight(part):
        both = []
        for i in range(2):
            at = w_one.at[2 * part + i]
            pltpu.make_async_copy(at, at, w_recv.at[2 * part + i]).wait()
            both.append(w_one[2 * part + i].astype(F32)[:72])
        w_all[part, half(y, core), :] = jnp.concatenate(both, axis=0).astype(BF16)

    right = z * Y + (y + 1) % Y
    left = z * Y + (y + Y - 1) % Y

    def ring(turn, place, to):
        return push(w_all.at[(z, 1 - z)[turn], half(place, core)], to, x, lat)

    rights = [[]]
    lefts = [[]]
    pair = []
    for turn in range(2):
        take_weight((z, 1 - z)[turn])
        rights[0].append(ring(turn, y, right))
        lefts[0].append(ring(turn, y, left))
        pair.append(push(w_all.at[(z, 1 - z)[turn], half(y, core)], zy, x, sib))

    def forward(step, turn):
        turns = (
            (rights, right, (y + Y - 1 - step) % Y, 0),
            (lefts, left, (y + 1 + step) % Y, 1),
        )
        for copies, to, got, last in turns:
            if turn == 0:
                copies.append([None, None])
            copy = copies[step][turn]
            if copy is None:
                continue
            copy.wait_recv()
            if step < 2 or (step == 2 and turn == last):
                copies[step + 1][turn] = ring(turn, got, to)
            pair.append(push(w_all.at[(z, 1 - z)[turn], half(got, core)], zy, x, sib))

    def round_x(whole, west_half, east_half):
        return (
            push(whole, zy, east, lat),
            push(whole, zy, west, lat),
            west_half,
            east_half,
        )

    def round_x_on(to_east, to_west, west_half, east_half):
        to_east.wait_recv()
        on_east = push(west_half, zy, east, lat)
        to_west.wait_recv()
        return on_east, push(east_half, zy, west, lat)

    cot_load.wait()
    relayout(1, ct)
    all_rows(ct, cots.at[zy, x], cot_send, cot_recv, True)

    forward(0, 0)
    pltpu.make_async_copy(rows.at[1, :, x], rows.at[1, :, x], row_recv).wait()
    side_rows(True)
    row_x = round_x(rows.at[1, :, x], rows.at[1, 0:8, west], rows.at[1, 8:16, east])
    forward(0, 1)
    forward(1, 0)
    row_on = round_x_on(*row_x)
    for i in range(2):
        at = rows.at[2 * i, :, x]
        pltpu.make_async_copy(at, at, side_recv.at[i]).wait()
    above_east = push(rows.at[0, :, x], zy, east, lat)
    below_west = push(rows.at[2, :, x], zy, west, lat)
    below_east = push(rows.at[2, :, x], zy, east, lat)
    above_west = push(rows.at[0, :, x], zy, west, lat)
    forward(1, 1)
    forward(2, 0)
    above_east.wait_recv()
    above_on = push(rows.at[0, :, west], zy, east, lat)
    below_west.wait_recv()
    below_on = push(rows.at[2, :, east], zy, west, lat)
    forward(2, 1)

    def whole_row(a):
        flat[...] = rows[a].reshape(1024, 128).astype(F32)
        for q in range(4):
            part = flat[pl.ds(q, 256, stride=4), :]
            if a == 0:
                part = jnp.where(row == 0, 0.0, part)
            if a == 2:
                part = jnp.where(row == ROWS - 1, 0.0, part)
            grid[a, :, 128 * q : 128 * (q + 1)] = part.astype(BF16)

    for copy in row_on:
        copy.wait_recv()
    whole_row(1)
    forward(3, 0)
    forward(3, 1)

    pltpu.make_async_copy(cots.at[:, x], cots.at[:, x], cot_recv).wait()
    cot_x = [push(cots.at[:, x], zy, (x + dx) % X, lat) for dx in range(1, X)]

    below_east.wait_recv()
    above_west.wait_recv()
    above_on.wait_recv()
    whole_row(0)
    below_on.wait_recv()
    whole_row(2)
    for copy in loads:
        copy.wait()
    for copy in pair:
        copy.wait_recv()

    def tap(i):
        if i < 4:
            return w_all[0, 512 * i : 512 * (i + 1), :]
        if i > 4:
            return w_all[1, 512 * i - 2304 : 512 * (i + 1) - 2304, :]
        return jnp.concatenate([w_all[0, 2048:2304, :], w_all[1, 0:256, :]], axis=0)

    two = jnp.zeros((256, 256), F32)
    third = jnp.zeros((256, 128), F32)
    for a in (1, 0, 2):
        two = two + dot(grid[a], jnp.concatenate([tap(3 * a), tap(3 * a + 1)], axis=1))
        third = third + dot(grid[a], tap(3 * a + 2))
    preact = (
        bias[pl.ds(x, 1), :]
        + pltpu.roll(two[:, 0:128], 1, 0)
        + two[:, 128:256]
        + pltpu.roll(third, 255, 0)
    )
    pre[...] = preact
    acts[x] = (preact * jax.nn.sigmoid(preact)).astype(BF16)
    low, high = slice(0, 128), slice(128, 256)
    act_x = [push(acts.at[x], zy, (x + dx) % X, lat) for dx in (2, 1, 3)]

    for a in range(3):
        for b in range(3):
            w_turned[b, 128 * a : 128 * (a + 1), :] = tap(3 * a + b).T
    for t in range(3):
        wq_turned[128 * t : 128 * (t + 1), :] = wq[:, 128 * t : 128 * (t + 1)].T

    for copy in cot_x:
        copy.wait_recv()
    flat[...] = cots[...].reshape(1024, 128).astype(F32)
    for q in range(4):
        part = flat[pl.ds(q, 256, stride=4), :].astype(BF16)
        cot_grid[:, 128 * q : 128 * (q + 1)] = part
        cot_blocks[q] = part

    out_grad = dot(cot_grid[...], wo[...], NT).astype(BF16)
    for copy in act_x:
        copy.wait_recv()
    activated = jnp.concatenate([acts[s] for s in range(X)], axis=1)
    projected = dot(activated, wq[...]).astype(BF16)
    queries, keys, values = (projected[:, 128 * t : 128 * (t + 1)] for t in range(3))
    capped = jnp.tanh(dot(queries, keys, NT) * (INV_ROOT / CAP))
    expo = jnp.exp(CAP * capped)
    probs = expo / jnp.sum(expo, axis=-1, keepdims=True)
    probs_b = probs.astype(BF16)
    attended = dot(probs_b, values).astype(BF16)
    centre = jnp.sum(out_grad.astype(F32) * attended.astype(F32), axis=-1, keepdims=True)
    score_grad = (
        probs * (dot(out_grad, values, NT) - centre) * (1.0 - capped * capped) * INV_ROOT
    ).astype(BF16)
    grads = jnp.concatenate(
        [
            dot(score_grad, keys).astype(BF16),
            dot(score_grad, queries, TN).astype(BF16),
            dot(probs_b, out_grad, TN).astype(BF16),
        ],
        axis=1,
    )
    head_part = dot(grads, wq_turned[...])
    for q in range(X):
        blocks[q] = head_part[:, 128 * q : 128 * (q + 1)]

    early = len(started)
    part_x = []
    for half_of in range(2):
        at = (low, high)[half_of]
        for dx in (2, 1, 3):
            i = 3 * half_of + dx - 1
            to = (x + dx) % X
            parts[i] = blocks[to, at].astype(BF16)
            part_x.append(push_to(parts.at[i], parts_in.at[i], zy, to, lat))
    preact = pre[...]
    s = jax.nn.sigmoid(preact)
    pre[...] = s * (1.0 + preact * (1.0 - s))
    for copy in started[:early]:
        copy.wait_send()
    drained[0] = early
    all_weights(False)
    all_rows(st, rows.at[1, zy, x], row_send, row_recv, False)
    all_rows(ct, cots.at[zy, x], cot_send, cot_recv, False)
    middle_rows(False)
    side_rows(False)

    def all_pres(first, start):
        @pl.loop(first, first + 8)
        def _(t):
            dst = pres.at[1 + mine_of]
            if start:
                @pl.when(t == zy)
                def _():
                    pltpu.make_async_copy(own_pre.at[t], dst, pre_recv).start()

            @pl.when(t != zy)
            def _():
                copy = remote(own_pre.at[t], dst, pre_send.at[t], pre_recv, t, x, lat)
                if start:
                    copy.start()
                else:
                    copy.wait_send()

        def ends(slot, to_lat):
            @pl.loop(first, first + 8)
            def _(t):
                copy = remote(
                    own_pre.at[t], pres.at[slot], end_send.at[t], pre_recv, t, x, to_lat
                )
                if start:
                    copy.start()
                else:
                    copy.wait_send()

        @pl.when(mine_of == ZY - 1)
        def _():
            ends(0, up)

        @pl.when(mine_of == 0)
        def _():
            ends(ZY + 1, down)

    for half_of in range(2):
        at = (low, high)[half_of]
        grad_act = blocks[x, at] + cot_blocks[x, at].astype(F32)
        for i in range(3 * half_of, 3 * half_of + 3):
            part_x[i].wait_recv()
        for i in range(3 * half_of, 3 * half_of + 3):
            grad_act = grad_act + parts_in[i].astype(F32)
        own_pre[8 * half_of : 8 * (half_of + 1)] = (
            (grad_act * pre[at]).astype(BF16).reshape(8, 16, 128)
        )
        all_pres(8 * half_of, True)

    drain()
    pltpu.make_async_copy(pres, pres, pre_recv).wait()

    @pl.when(lat == 0)
    def _():
        pres[0] = jnp.zeros((16, 128), BF16)

    @pl.when(lat == LATS - 1)
    def _():
        pres[ZY + 1] = jnp.zeros((16, 128), BF16)

    around = jnp.concatenate(
        [pres[2 - a : 2 - a + ZY].reshape(256, 128) for a in range(3)], axis=1
    )
    column = lax.broadcasted_iota(jnp.int32, (256, 256), 0) % 16
    sum_x = []
    for h in range(2):
        at = slice(256 * h, 256 * (h + 1))
        result = jnp.zeros((256, 256), F32)
        for b in range(3):
            acc = dot(around, w_turned[b, :, at])
            if b != 1:
                for q in range(2):
                    shifted[...] = acc[:, 128 * q : 128 * (q + 1)]
                    rim = shifted[pl.ds(0 if b == 0 else 15, 16, stride=16), :]
                    rims[b // 2, h, q] = rim.astype(BF16)
            if b == 0:
                acc = jnp.where(column == 15, 0.0, pltpu.roll(acc, 255, 0))
            if b == 2:
                acc = jnp.where(column == 0, 0.0, pltpu.roll(acc, 1, 0))
            result = result + acc
        for q in range(2):
            base = 512 * h + 256 * q
            flat[base : base + 256, :] = result[:, 128 * q : 128 * (q + 1)]
            for to in range(X):
                for j in range(4):
                    piece = flat[pl.ds(base + 4 * to + j, 16, stride=16), :]
                    mine[to, h, q, j] = piece.astype(BF16)
        for dx in (2, 1, 3):
            to = (x + dx) % X
            sum_x.append(push_to(mine.at[to, h], sums_in.at[3 * h + dx - 1], zy, to, lat))

    rim_west = remote(
        rims.at[0], rims_in.at[x], rim_send.at[0], rim_recv.at[x],
        (zy + ZY - 1) % ZY, X - 1, lat,
    )
    rim_east = remote(
        rims.at[1], rims_in.at[x], rim_send.at[1], rim_recv.at[x], (zy + 1) % ZY, 0, lat
    )
    rim_west.start()
    rim_east.start()
    all_pres(0, False)
    all_pres(8, False)

    for h in range(2):
        total = mine[x, h].astype(F32)
        for copy in sum_x[3 * h : 3 * h + 3]:
            copy.wait_recv()
        for i in range(X - 1):
            total = total + sums_in[3 * h + i].astype(F32)
        flat[128 * h : 128 * (h + 1), :] = total.reshape(128, 128)

    def add_rims(j):
        for i in range(X):
            pltpu.make_async_copy(rims_in.at[i], rims_in.at[i], rim_recv.at[i]).wait()
        for q in range(4):
            at = slice(64 * q + 16 * j, 64 * q + 16 * (j + 1))
            total = flat[at]
            for i in range(X):
                total = total + rims_in[i, q // 2, q % 2].astype(F32)
            flat[at] = total

    @pl.when(x == 0)
    def _():
        add_rims(0)

    @pl.when(x == X - 1)
    def _():
        add_rims(3)

    for t in range(ZY):
        out[t] = flat[pl.ds(t, 16, stride=16), :].astype(BF16)

    rim_west.wait_send()
    rim_east.wait_send()
    drain()


PUSHES = 80


def body(state, conv_weight, conv_bias, w_qkv, w_out, cotangent):
    vmem = pl.BlockSpec(memory_space=pltpu.VMEM)
    anywhere = pl.BlockSpec(memory_space=pl.ANY)
    dma = pltpu.SemaphoreType.DMA
    out = pl.pallas_call(
        kernel,
        out_shape=jax.ShapeDtypeStruct((ZY, 16, 128), BF16),
        in_specs=[anywhere] * 6,
        out_specs=vmem,
        scratch_shapes=[
            pltpu.VMEM((2, 16, 4, 512), BF16),
            pltpu.VMEM((72, 512), BF16),
            pltpu.VMEM((ZY, 16, 128), BF16),
            pltpu.VMEM((ZY, 16, 128), BF16),
            pltpu.VMEM((X, 80, 128), BF16),
            pltpu.VMEM((X, 128), F32),
            pltpu.VMEM((3, ZY, X, 16, 128), BF16),
            pltpu.VMEM((ZY, X, 16, 128), BF16),
            pltpu.VMEM((1024, 128), F32),
            pltpu.VMEM((3, 256, 512), BF16),
            pltpu.VMEM((256, 512), BF16),
            pltpu.VMEM((4, 256, 128), BF16),
            pltpu.VMEM((4, 80, 128), BF16),
            pltpu.VMEM((2, 2304, 128), BF16),
            pltpu.VMEM((512, 384), BF16),
            pltpu.VMEM((128, 512), BF16),
            pltpu.VMEM((256, 128), F32),
            pltpu.VMEM((X, 256, 128), BF16),
            pltpu.VMEM((X, 256, 128), F32),
            pltpu.VMEM((6, 128, 128), BF16),
            pltpu.VMEM((6, 128, 128), BF16),
            pltpu.VMEM((ZY, 16, 128), BF16),
            pltpu.VMEM((ZY + 2, 16, 128), BF16),
            pltpu.VMEM((256, 128), F32),
            pltpu.VMEM((X, 2, 2, 4, ZY, 128), BF16),
            pltpu.VMEM((6, 2, 4, ZY, 128), BF16),
            pltpu.VMEM((2, 2, 2, ZY, 128), BF16),
            pltpu.VMEM((X, 2, 2, ZY, 128), BF16),
            pltpu.VMEM((3, 384, 512), BF16),
            pltpu.VMEM((384, 512), BF16),
            dma((8,)),
            dma((3 * X,)),
            dma((4,)),
            dma((ZY,)),
            dma,
            dma((ZY,)),
            dma,
            dma((ZY,)),
            dma,
            dma((ZY,)),
            dma((2,)),
            dma((X,)),
            dma((2,)),
            dma((2,)),
            dma((2,)),
            dma((PUSHES,)),
            dma((PUSHES,)),
        ],
        compiler_params=pltpu.CompilerParams(
            collective_id=0, has_side_effects=True, vmem_limit_bytes=VMEM_LIMIT
        ),
    )(state, cotangent, conv_weight, conv_bias.reshape(X, 128), w_qkv, w_out)
    return out.reshape(16, 4, 4, 128).transpose(0, 2, 1, 3).reshape(16, 4, 512)


def solution(mesh):
    return jax.shard_map(
        body,
        mesh=mesh,
        in_specs=(P("lat", "lon", None), P("lon", None), P(), P(), P(), P("lat", "lon", None)),
        out_specs=P("lat", "lon", None),
        check_vma=False,
    )
```

```python
import functools
import math

import jax
import jax.numpy as jnp
from jax import lax
from jax.experimental import pallas as pl
from jax.experimental.pallas import tpu as pltpu
from jax.sharding import PartitionSpec as P

X = 4
Y = 8
ZY = 16
LATS = 8
ROWS = ZY * LATS
CAP = 20.0
INV_ROOT = 1.0 / math.sqrt(128.0)
F32 = jnp.float32
BF16 = jnp.bfloat16
VMEM_LIMIT = 60 * 1024 * 1024

NN = (((1,), (0,)), ((), ()))
NT = (((1,), (1,)), ((), ()))
TN = (((0,), (0,)), ((), ()))


def dot(a, b, dims=NN):
    return lax.dot_general(a, b, dims, preferred_element_type=F32)


def kernel(
    st_hbm, ct_hbm, cw_hbm, bias_hbm, wqkv, wout, out,
    raw, raw_w, st, ct, wp, bias,
    rows, cots, flat, grid, cot_grid, cot_blocks, w_one, w_all, wq, wo,
    pre, acts, blocks, parts, parts_in, own_pre, pres, mine, sums_in, rims, rims_in,
    w_turned, wq_turned,
    load_sem, w_send, w_recv, row_send, row_recv, cot_send, cot_recv, pre_send, pre_recv,
    end_send, rim_send, rim_recv, middle_send, side_send, side_recv,
    send, recv,
):
    lon = lax.axis_index("lon")
    lat = lax.axis_index("lat")
    zy, x = lon // X, lon % X
    z, y = zy // Y, zy % Y
    core = lat % 2
    sib = lat + 1 - 2 * core
    mine_of = jnp.where(z == core, y, ZY - 1 - y)
    row = lat * ZY + mine_of
    up, down = (lat + 1) % LATS, (lat + LATS - 1) % LATS

    def owner(t):
        return jnp.where(t < Y, core * Y + t, (1 - core) * Y + ZY - 1 - t)

    east, west = (x + 1) % X, (x + X - 1) % X

    def remote(src, dst, send_sem, recv_sem, to_zy, to_x, to_lat):
        return pltpu.make_async_remote_copy(
            src_ref=src,
            dst_ref=dst,
            send_sem=send_sem,
            recv_sem=recv_sem,
            device_id={"lon": to_zy * X + to_x, "lat": to_lat},
            device_id_type=pl.DeviceIdType.MESH,
        )

    started = []

    def push_to(src, dst, to_zy, to_x, to_lat):
        i = len(started)
        copy = remote(src, dst, send.at[i], recv.at[i], to_zy, to_x, to_lat)
        copy.start()
        started.append(copy)
        return copy

    drained = [0]

    def drain():
        for copy in started[drained[0] :]:
            copy.wait_send()
        drained[0] = len(started)

    def push(ref, to_zy, to_x, to_lat):
        return push_to(ref, ref, to_zy, to_x, to_lat)

    def load(i, src, dst):
        copy = pltpu.make_async_copy(src, dst, load_sem.at[i])
        copy.start()
        return copy

    weight_load = load(0, cw_hbm, raw_w)
    state_load = load(1, st_hbm, raw.at[0])
    cot_load = load(2, ct_hbm, raw.at[1])
    loads = [load(3, bias_hbm, bias)]
    for t in range(3):
        source = wqkv.at[:, pl.ds(pl.multiple_of(t * 512 + x * 128, 128), 128)]
        loads.append(load(4 + t, source, wq.at[:, 128 * t : 128 * (t + 1)]))
    loads.append(load(7, wout.at[pl.ds(pl.multiple_of(x * 128, 128), 128)], wo))

    barrier = pltpu.get_barrier_semaphore()

    def hello(to_zy, to_x, to_lat):
        pl.semaphore_signal(
            barrier,
            inc=1,
            device_id={"lon": to_zy * X + to_x, "lat": to_lat},
            device_id_type=pl.DeviceIdType.MESH,
        )

    other_zy = (1 - z) * Y + y
    for dx in range(1, X):
        hello(zy, (x + dx) % X, lat)
    hello(zy, x, sib)

    @pl.loop(1, ZY)
    def _(d):
        hello((zy + d) % ZY, x, lat)

    hello(core * Y, x, down)
    hello((1 - core) * Y, x, up)

    plane = lat // 2
    near = jnp.where(plane < 2, 3, 0) * 2 + core
    for i in range(2):
        hello(other_zy, 2 * core + i, near)

    @pl.when(x == 0)
    def _():
        for i in range(X):
            hello((zy + ZY - 1) % ZY, i, lat)

    @pl.when(x == X - 1)
    def _():
        for i in range(X):
            hello((zy + 1) % ZY, i, lat)

    weight_load.wait()
    for q in range(X):
        piece = raw_w[:, 128 * q : 128 * (q + 1)].astype(F32)
        wp[q] = jnp.concatenate([piece, jnp.zeros((8, 128), F32)], axis=0).astype(BF16)

    edge = (mine_of == 0) | (mine_of == ZY - 1)
    sends_weight = x // 2 == core
    crosses = sends_weight & ((plane == 0) | (plane == 3))
    pl.semaphore_wait(
        barrier,
        (X - 1) + (ZY - 1) + 1 + 2 + jnp.where(edge, ZY, 0) + jnp.where(crosses, 2 * X, 0),
    )

    slot = z * 2 + x % 2

    def all_weights(start):
        def across(copy):
            if start:
                copy.start()
            else:
                copy.wait_send()

        @pl.when(crosses)
        def _():
            for k in range(2):
                to_lat = jnp.where(plane == 3, k, 2 + k) * 2 + core
                for t in range(X):
                    across(
                        remote(
                            wp.at[t], w_one.at[slot], w_send.at[X + X * k + t],
                            w_recv.at[slot], other_zy, t, to_lat,
                        )
                    )

        @pl.when(sends_weight)
        def _():
            for t in range(X):
                if start:
                    @pl.when(t == x)
                    def _():
                        pltpu.make_async_copy(
                            wp.at[t], w_one.at[slot], w_recv.at[slot]
                        ).start()

                @pl.when(t != x)
                def _():
                    across(
                        remote(
                            wp.at[t], w_one.at[slot], w_send.at[t], w_recv.at[slot],
                            zy, t, lat,
                        )
                    )

    all_weights(True)

    def relayout(which, dst):
        for r in range(16):
            for q in range(4):
                piece = raw[which, r, :, 128 * q : 128 * (q + 1)].astype(F32)
                flat[pl.ds(16 * r + q, 4, stride=4), :] = piece
        dst[...] = flat[0:256, :].astype(BF16).reshape(16, 16, 128)

    state_load.wait()
    relayout(0, st)

    lead = jnp.where(z == core, Y, 0)

    def all_rows(src, dst, send_sem, recv_sem, start):
        @pl.loop(0, ZY)
        def _(i):
            t = (i + lead) % ZY

            if start:
                @pl.when(t == mine_of)
                def _():
                    pltpu.make_async_copy(src.at[t], dst, recv_sem).start()

            @pl.when(t != mine_of)
            def _():
                copy = remote(
                    src.at[t], dst, send_sem.at[t], recv_sem, owner(t), x, lat
                )
                if start:
                    copy.start()
                else:
                    copy.wait_send()

    def middle_rows(start):
        for i, t, to in ((0, Y - 1, Y), (1, Y, Y - 1)):
            dst = rows.at[2 * i, zy, x]
            if start:
                @pl.when(to == mine_of)
                def _():
                    pltpu.make_async_copy(st.at[t], dst, side_recv.at[i]).start()

            @pl.when(to != mine_of)
            def _():
                copy = remote(
                    st.at[t], dst, middle_send.at[i], side_recv.at[i], owner(to), x, lat
                )
                if start:
                    copy.start()
                else:
                    copy.wait_send()

    def side_rows(start):
        for i, last, middle, to_lat, step in (
            (0, ZY - 1, Y - 1, up, 1),
            (1, 0, Y, down, -1),
        ):
            @pl.when(mine_of != middle)
            def _():
                to_zy = jnp.where(mine_of == last, zy, owner(mine_of + step))
                copy = remote(
                    rows.at[1, :, x], rows.at[2 * i, :, x], side_send.at[i], side_recv.at[i],
                    to_zy, x, jnp.where(mine_of == last, to_lat, lat),
                )
                if start:
                    copy.start()
                else:
                    copy.wait_send()

    all_rows(st, rows.at[1, zy, x], row_send, row_recv, True)
    middle_rows(True)

    def half(place, which):
        return pl.ds(pl.multiple_of((place * 2 + which) * 144, 16), 144)

    def take_weight(part):
        both = []
        for i in range(2):
            at = w_one.at[2 * part + i]
            pltpu.make_async_copy(at, at, w_recv.at[2 * part + i]).wait()
            both.append(w_one[2 * part + i].astype(F32)[:72])
        w_all[part, half(y, core), :] = jnp.concatenate(both, axis=0).astype(BF16)

    right = z * Y + (y + 1) % Y
    left = z * Y + (y + Y - 1) % Y

    def ring(turn, place, to):
        return push(w_all.at[(z, 1 - z)[turn], half(place, core)], to, x, lat)

    rights = [[]]
    lefts = [[]]
    pair = []
    for turn in range(2):
        take_weight((z, 1 - z)[turn])
        rights[0].append(ring(turn, y, right))
        lefts[0].append(ring(turn, y, left))
        pair.append(push(w_all.at[(z, 1 - z)[turn], half(y, core)], zy, x, sib))

    def forward(step, turn):
        turns = (
            (rights, right, (y + Y - 1 - step) % Y, 0),
            (lefts, left, (y + 1 + step) % Y, 1),
        )
        for copies, to, got, last in turns:
            if turn == 0:
                copies.append([None, None])
            copy = copies[step][turn]
            if copy is None:
                continue
            copy.wait_recv()
            if step < 2 or (step == 2 and turn == last):
                copies[step + 1][turn] = ring(turn, got, to)
            pair.append(push(w_all.at[(z, 1 - z)[turn], half(got, core)], zy, x, sib))

    def round_x(whole, west_half, east_half):
        return (
            push(whole, zy, east, lat),
            push(whole, zy, west, lat),
            west_half,
            east_half,
        )

    def round_x_on(to_east, to_west, west_half, east_half):
        to_east.wait_recv()
        on_east = push(west_half, zy, east, lat)
        to_west.wait_recv()
        return on_east, push(east_half, zy, west, lat)

    cot_load.wait()
    relayout(1, ct)
    all_rows(ct, cots.at[zy, x], cot_send, cot_recv, True)

    forward(0, 0)
    pltpu.make_async_copy(rows.at[1, :, x], rows.at[1, :, x], row_recv).wait()
    side_rows(True)
    row_x = round_x(rows.at[1, :, x], rows.at[1, 0:8, west], rows.at[1, 8:16, east])
    forward(0, 1)
    forward(1, 0)
    row_on = round_x_on(*row_x)
    for i in range(2):
        at = rows.at[2 * i, :, x]
        pltpu.make_async_copy(at, at, side_recv.at[i]).wait()
    above_east = push(rows.at[0, :, x], zy, east, lat)
    below_west = push(rows.at[2, :, x], zy, west, lat)
    below_east = push(rows.at[2, :, x], zy, east, lat)
    above_west = push(rows.at[0, :, x], zy, west, lat)
    forward(1, 1)
    forward(2, 0)
    above_east.wait_recv()
    above_on = push(rows.at[0, :, west], zy, east, lat)
    below_west.wait_recv()
    below_on = push(rows.at[2, :, east], zy, west, lat)
    forward(2, 1)

    def whole_row(a):
        flat[...] = rows[a].reshape(1024, 128).astype(F32)
        for q in range(4):
            part = flat[pl.ds(q, 256, stride=4), :]
            if a == 0:
                part = jnp.where(row == 0, 0.0, part)
            if a == 2:
                part = jnp.where(row == ROWS - 1, 0.0, part)
            grid[a, :, 128 * q : 128 * (q + 1)] = part.astype(BF16)

    for copy in row_on:
        copy.wait_recv()
    whole_row(1)
    forward(3, 0)
    forward(3, 1)

    pltpu.make_async_copy(cots.at[:, x], cots.at[:, x], cot_recv).wait()
    cot_x = [push(cots.at[:, x], zy, (x + dx) % X, lat) for dx in range(1, X)]

    below_east.wait_recv()
    above_west.wait_recv()
    above_on.wait_recv()
    whole_row(0)
    below_on.wait_recv()
    whole_row(2)
    for copy in loads:
        copy.wait()
    for copy in pair:
        copy.wait_recv()

    def tap(i):
        if i < 4:
            return w_all[0, 512 * i : 512 * (i + 1), :]
        if i > 4:
            return w_all[1, 512 * i - 2304 : 512 * (i + 1) - 2304, :]
        return jnp.concatenate([w_all[0, 2048:2304, :], w_all[1, 0:256, :]], axis=0)

    two = jnp.zeros((256, 256), F32)
    third = jnp.zeros((256, 128), F32)
    for a in (1, 0, 2):
        two = two + dot(grid[a], jnp.concatenate([tap(3 * a), tap(3 * a + 1)], axis=1))
        third = third + dot(grid[a], tap(3 * a + 2))
    preact = (
        bias[pl.ds(x, 1), :]
        + pltpu.roll(two[:, 0:128], 1, 0)
        + two[:, 128:256]
        + pltpu.roll(third, 255, 0)
    )
    pre[...] = preact
    acts[x] = (preact * jax.nn.sigmoid(preact)).astype(BF16)
    act_x = [push(acts.at[x], zy, (x + dx) % X, lat) for dx in (2, 1, 3)]

    for a in range(3):
        for b in range(3):
            w_turned[b, 128 * a : 128 * (a + 1), :] = tap(3 * a + b).T
    for t in range(3):
        wq_turned[128 * t : 128 * (t + 1), :] = wq[:, 128 * t : 128 * (t + 1)].T

    for copy in cot_x:
        copy.wait_recv()
    flat[...] = cots[...].reshape(1024, 128).astype(F32)
    for q in range(4):
        part = flat[pl.ds(q, 256, stride=4), :].astype(BF16)
        cot_grid[:, 128 * q : 128 * (q + 1)] = part
        cot_blocks[q] = part

    out_grad = dot(cot_grid[...], wo[...], NT).astype(BF16)
    for copy in act_x:
        copy.wait_recv()
    activated = jnp.concatenate([acts[s] for s in range(X)], axis=1)
    projected = dot(activated, wq[...]).astype(BF16)
    queries, keys, values = (projected[:, 128 * t : 128 * (t + 1)] for t in range(3))
    capped = jnp.tanh(dot(queries, keys, NT) * (INV_ROOT / CAP))
    expo = jnp.exp(CAP * capped)
    probs = expo / jnp.sum(expo, axis=-1, keepdims=True)
    probs_b = probs.astype(BF16)
    attended = dot(probs_b, values).astype(BF16)
    centre = jnp.sum(out_grad.astype(F32) * attended.astype(F32), axis=-1, keepdims=True)
    score_grad = (
        probs * (dot(out_grad, values, NT) - centre) * (1.0 - capped * capped) * INV_ROOT
    ).astype(BF16)
    grads = jnp.concatenate(
        [
            dot(score_grad, keys).astype(BF16),
            dot(score_grad, queries, TN).astype(BF16),
            dot(probs_b, out_grad, TN).astype(BF16),
        ],
        axis=1,
    )
    head_part = dot(grads, wq_turned[...])
    for q in range(X):
        blocks[q] = head_part[:, 128 * q : 128 * (q + 1)]

    early = len(started)
    part_x = []
    sides = (1 - z, z)
    halves = [pl.ds(pl.multiple_of(side * 128, 128), 128) for side in sides]
    for half_of in range(2):
        at = halves[half_of]
        for dx in (2, 1, 3):
            i = 3 * half_of + dx - 1
            to = (x + dx) % X
            parts[i] = blocks[to, at].astype(BF16)
            part_x.append(push_to(parts.at[i], parts_in.at[i], zy, to, lat))
    preact = pre[...]
    s = jax.nn.sigmoid(preact)
    pre[...] = s * (1.0 + preact * (1.0 - s))
    for copy in started[:early]:
        copy.wait_send()
    drained[0] = early
    all_weights(False)
    all_rows(st, rows.at[1, zy, x], row_send, row_recv, False)
    all_rows(ct, cots.at[zy, x], cot_send, cot_recv, False)
    middle_rows(False)
    side_rows(False)

    def all_pres(first, start):
        @pl.loop(first, first + 8)
        def _(t):
            dst = pres.at[1 + mine_of]
            if start:
                @pl.when(t == zy)
                def _():
                    pltpu.make_async_copy(own_pre.at[t], dst, pre_recv).start()

            @pl.when(t != zy)
            def _():
                copy = remote(own_pre.at[t], dst, pre_send.at[t], pre_recv, t, x, lat)
                if start:
                    copy.start()
                else:
                    copy.wait_send()

        def ends(slot, to_lat):
            @pl.loop(first, first + 8)
            def _(t):
                copy = remote(
                    own_pre.at[t], pres.at[slot], end_send.at[t], pre_recv, t, x, to_lat
                )
                if start:
                    copy.start()
                else:
                    copy.wait_send()

        @pl.when(mine_of == ZY - 1)
        def _():
            ends(0, up)

        @pl.when(mine_of == 0)
        def _():
            ends(ZY + 1, down)

    for half_of in range(2):
        at = halves[half_of]
        first = 8 * sides[half_of]
        grad_act = blocks[x, at] + cot_blocks[x, at].astype(F32)
        for i in range(3 * half_of, 3 * half_of + 3):
            part_x[i].wait_recv()
        for i in range(3 * half_of, 3 * half_of + 3):
            grad_act = grad_act + parts_in[i].astype(F32)
        own_pre[pl.ds(first, 8)] = (
            (grad_act * pre[at]).astype(BF16).reshape(8, 16, 128)
        )
        all_pres(first, True)

    drain()
    pltpu.make_async_copy(pres, pres, pre_recv).wait()

    @pl.when(lat == 0)
    def _():
        pres[0] = jnp.zeros((16, 128), BF16)

    @pl.when(lat == LATS - 1)
    def _():
        pres[ZY + 1] = jnp.zeros((16, 128), BF16)

    around = jnp.concatenate(
        [pres[2 - a : 2 - a + ZY].reshape(256, 128) for a in range(3)], axis=1
    )

    flat[0:288, :] = pres[...].reshape(288, 128).astype(F32)
    for side, b, at in ((0, 0, 0), (1, 2, 15)):
        edge_of = [flat[pl.ds(16 * (2 - a) + at, 16, stride=16), :] for a in range(3)]
        rim = dot(jnp.concatenate(edge_of, axis=1).astype(BF16), w_turned[b])
        for q in range(4):
            rims[side, q // 2, q % 2] = rim[:, 128 * q : 128 * (q + 1)].astype(BF16)
    rim_west = remote(
        rims.at[0], rims_in.at[x], rim_send.at[0], rim_recv.at[x],
        (zy + ZY - 1) % ZY, X - 1, lat,
    )
    rim_east = remote(
        rims.at[1], rims_in.at[x], rim_send.at[1], rim_recv.at[x], (zy + 1) % ZY, 0, lat
    )
    rim_west.start()
    rim_east.start()

    column = lax.broadcasted_iota(jnp.int32, (256, 256), 0) % 16
    sum_x = []
    for h in range(2):
        at = slice(256 * h, 256 * (h + 1))
        result = jnp.zeros((256, 256), F32)
        for b in range(3):
            acc = dot(around, w_turned[b, :, at])
            if b == 0:
                acc = jnp.where(column == 15, 0.0, pltpu.roll(acc, 255, 0))
            if b == 2:
                acc = jnp.where(column == 0, 0.0, pltpu.roll(acc, 1, 0))
            result = result + acc
        for q in range(2):
            base = 512 * h + 256 * q
            flat[base : base + 256, :] = result[:, 128 * q : 128 * (q + 1)]
            for to in range(X):
                for j in range(4):
                    piece = flat[pl.ds(base + 4 * to + j, 16, stride=16), :]
                    mine[to, h, q, j] = piece.astype(BF16)
        for dx in (2, 1, 3):
            to = (x + dx) % X
            sum_x.append(push_to(mine.at[to, h], sums_in.at[3 * h + dx - 1], zy, to, lat))

    all_pres(0, False)
    all_pres(8, False)

    for h in range(2):
        total = mine[x, h].astype(F32)
        for copy in sum_x[3 * h : 3 * h + 3]:
            copy.wait_recv()
        for i in range(X - 1):
            total = total + sums_in[3 * h + i].astype(F32)
        flat[128 * h : 128 * (h + 1), :] = total.reshape(128, 128)

    def add_rims(j):
        for i in range(X):
            pltpu.make_async_copy(rims_in.at[i], rims_in.at[i], rim_recv.at[i]).wait()
        for q in range(4):
            at = slice(64 * q + 16 * j, 64 * q + 16 * (j + 1))
            total = flat[at]
            for i in range(X):
                total = total + rims_in[i, q // 2, q % 2].astype(F32)
            flat[at] = total

    @pl.when(x == 0)
    def _():
        add_rims(0)

    @pl.when(x == X - 1)
    def _():
        add_rims(3)

    for t in range(ZY):
        out[t] = flat[pl.ds(t, 16, stride=16), :].astype(BF16)

    rim_west.wait_send()
    rim_east.wait_send()
    drain()


PUSHES = 80


def body(state, conv_weight, conv_bias, w_qkv, w_out, cotangent):
    vmem = pl.BlockSpec(memory_space=pltpu.VMEM)
    anywhere = pl.BlockSpec(memory_space=pl.ANY)
    dma = pltpu.SemaphoreType.DMA
    out = pl.pallas_call(
        kernel,
        out_shape=jax.ShapeDtypeStruct((ZY, 16, 128), BF16),
        in_specs=[anywhere] * 6,
        out_specs=vmem,
        scratch_shapes=[
            pltpu.VMEM((2, 16, 4, 512), BF16),
            pltpu.VMEM((72, 512), BF16),
            pltpu.VMEM((ZY, 16, 128), BF16),
            pltpu.VMEM((ZY, 16, 128), BF16),
            pltpu.VMEM((X, 80, 128), BF16),
            pltpu.VMEM((X, 128), F32),
            pltpu.VMEM((3, ZY, X, 16, 128), BF16),
            pltpu.VMEM((ZY, X, 16, 128), BF16),
            pltpu.VMEM((1024, 128), F32),
            pltpu.VMEM((3, 256, 512), BF16),
            pltpu.VMEM((256, 512), BF16),
            pltpu.VMEM((4, 256, 128), BF16),
            pltpu.VMEM((4, 80, 128), BF16),
            pltpu.VMEM((2, 2304, 128), BF16),
            pltpu.VMEM((512, 384), BF16),
            pltpu.VMEM((128, 512), BF16),
            pltpu.VMEM((256, 128), F32),
            pltpu.VMEM((X, 256, 128), BF16),
            pltpu.VMEM((X, 256, 128), F32),
            pltpu.VMEM((6, 128, 128), BF16),
            pltpu.VMEM((6, 128, 128), BF16),
            pltpu.VMEM((ZY, 16, 128), BF16),
            pltpu.VMEM((ZY + 2, 16, 128), BF16),
            pltpu.VMEM((X, 2, 2, 4, ZY, 128), BF16),
            pltpu.VMEM((6, 2, 4, ZY, 128), BF16),
            pltpu.VMEM((2, 2, 2, ZY, 128), BF16),
            pltpu.VMEM((X, 2, 2, ZY, 128), BF16),
            pltpu.VMEM((3, 384, 512), BF16),
            pltpu.VMEM((384, 512), BF16),
            dma((8,)),
            dma((3 * X,)),
            dma((4,)),
            dma((ZY,)),
            dma,
            dma((ZY,)),
            dma,
            dma((ZY,)),
            dma,
            dma((ZY,)),
            dma((2,)),
            dma((X,)),
            dma((2,)),
            dma((2,)),
            dma((2,)),
            dma((PUSHES,)),
            dma((PUSHES,)),
        ],
        compiler_params=pltpu.CompilerParams(
            collective_id=0, has_side_effects=True, vmem_limit_bytes=VMEM_LIMIT
        ),
    )(state, cotangent, conv_weight, conv_bias.reshape(X, 128), w_qkv, w_out)
    return out.reshape(16, 4, 4, 128).transpose(0, 2, 1, 3).reshape(16, 4, 512)


def solution(mesh):
    return jax.shard_map(
        body,
        mesh=mesh,
        in_specs=(P("lat", "lon", None), P("lon", None), P(), P(), P(), P("lat", "lon", None)),
        out_specs=P("lat", "lon", None),
        check_vma=False,
    )
```

```python
import functools
import math

import jax
import jax.numpy as jnp
from jax import lax
from jax.experimental import pallas as pl
from jax.experimental.pallas import tpu as pltpu
from jax.sharding import PartitionSpec as P

X = 4
Y = 8
ZY = 16
LATS = 8
ROWS = ZY * LATS
CAP = 20.0
INV_ROOT = 1.0 / math.sqrt(128.0)
F32 = jnp.float32
BF16 = jnp.bfloat16
VMEM_LIMIT = 60 * 1024 * 1024

NN = (((1,), (0,)), ((), ()))
NT = (((1,), (1,)), ((), ()))
TN = (((0,), (0,)), ((), ()))


def dot(a, b, dims=NN):
    return lax.dot_general(a, b, dims, preferred_element_type=F32)


def kernel(
    st_hbm, ct_hbm, cw_hbm, bias_hbm, wqkv, wout, out,
    raw, raw_w, st, ct, wp, bias,
    rows, cots, flat, grid, cot_grid, cot_blocks, w_one, w_all, wq, wo,
    pre, acts, blocks, parts, parts_in, own_pre, pres, mine, sums_in, rims, rims_in,
    w_turned, wq_turned,
    load_sem, w_send, w_recv, row_send, row_recv, cot_send, cot_recv, pre_send, pre_recv,
    end_send, rim_send, rim_recv, middle_send, side_send, side_recv,
    send, recv,
):
    lon = lax.axis_index("lon")
    lat = lax.axis_index("lat")
    zy, x = lon // X, lon % X
    z, y = zy // Y, zy % Y
    core = lat % 2
    sib = lat + 1 - 2 * core
    mine_of = jnp.where(z == core, y, ZY - 1 - y)
    row = lat * ZY + mine_of
    up, down = (lat + 1) % LATS, (lat + LATS - 1) % LATS

    def owner(t):
        return jnp.where(t < Y, core * Y + t, (1 - core) * Y + ZY - 1 - t)

    east, west = (x + 1) % X, (x + X - 1) % X

    def remote(src, dst, send_sem, recv_sem, to_zy, to_x, to_lat):
        return pltpu.make_async_remote_copy(
            src_ref=src,
            dst_ref=dst,
            send_sem=send_sem,
            recv_sem=recv_sem,
            device_id={"lon": to_zy * X + to_x, "lat": to_lat},
            device_id_type=pl.DeviceIdType.MESH,
        )

    started = []

    def push_to(src, dst, to_zy, to_x, to_lat):
        i = len(started)
        copy = remote(src, dst, send.at[i], recv.at[i], to_zy, to_x, to_lat)
        copy.start()
        started.append(copy)
        return copy

    drained = [0]

    def drain():
        for copy in started[drained[0] :]:
            copy.wait_send()
        drained[0] = len(started)

    def push(ref, to_zy, to_x, to_lat):
        return push_to(ref, ref, to_zy, to_x, to_lat)

    def load(i, src, dst):
        copy = pltpu.make_async_copy(src, dst, load_sem.at[i])
        copy.start()
        return copy

    weight_load = load(0, cw_hbm, raw_w)
    state_load = load(1, st_hbm, raw.at[0])
    cot_load = load(2, ct_hbm, raw.at[1])
    loads = [load(3, bias_hbm, bias)]
    for t in range(3):
        source = wqkv.at[:, pl.ds(pl.multiple_of(t * 512 + x * 128, 128), 128)]
        loads.append(load(4 + t, source, wq.at[:, 128 * t : 128 * (t + 1)]))
    loads.append(load(7, wout.at[pl.ds(pl.multiple_of(x * 128, 128), 128)], wo))

    barrier = pltpu.get_barrier_semaphore()

    def hello(to_zy, to_x, to_lat):
        pl.semaphore_signal(
            barrier,
            inc=1,
            device_id={"lon": to_zy * X + to_x, "lat": to_lat},
            device_id_type=pl.DeviceIdType.MESH,
        )

    other_zy = (1 - z) * Y + y
    for dx in range(1, X):
        hello(zy, (x + dx) % X, lat)
    hello(zy, x, sib)

    @pl.loop(1, ZY)
    def _(d):
        hello((zy + d) % ZY, x, lat)

    hello(core * Y, x, down)
    hello((1 - core) * Y, x, up)

    plane = lat // 2
    near = jnp.where(plane < 2, 3, 0) * 2 + core
    for i in range(2):
        hello(other_zy, 2 * core + i, near)

    @pl.when(x == 0)
    def _():
        for i in range(X):
            hello((zy + ZY - 1) % ZY, i, lat)

    @pl.when(x == X - 1)
    def _():
        for i in range(X):
            hello((zy + 1) % ZY, i, lat)

    weight_load.wait()
    for q in range(X):
        piece = raw_w[:, 128 * q : 128 * (q + 1)].astype(F32)
        wp[q] = jnp.concatenate([piece, jnp.zeros((8, 128), F32)], axis=0).astype(BF16)

    edge = (mine_of == 0) | (mine_of == ZY - 1)
    sends_weight = x // 2 == core
    crosses = sends_weight & ((plane == 0) | (plane == 3))
    pl.semaphore_wait(
        barrier,
        (X - 1) + (ZY - 1) + 1 + 2 + jnp.where(edge, ZY, 0) + jnp.where(crosses, 2 * X, 0),
    )

    slot = z * 2 + x % 2

    def all_weights(start):
        def across(copy):
            if start:
                copy.start()
            else:
                copy.wait_send()

        @pl.when(crosses)
        def _():
            for k in range(2):
                to_lat = jnp.where(plane == 3, k, 2 + k) * 2 + core
                for t in range(X):
                    across(
                        remote(
                            wp.at[t], w_one.at[slot], w_send.at[X + X * k + t],
                            w_recv.at[slot], other_zy, t, to_lat,
                        )
                    )

        @pl.when(sends_weight)
        def _():
            for t in range(X):
                if start:
                    @pl.when(t == x)
                    def _():
                        pltpu.make_async_copy(
                            wp.at[t], w_one.at[slot], w_recv.at[slot]
                        ).start()

                @pl.when(t != x)
                def _():
                    across(
                        remote(
                            wp.at[t], w_one.at[slot], w_send.at[t], w_recv.at[slot],
                            zy, t, lat,
                        )
                    )

    all_weights(True)

    def relayout(which, dst):
        for r in range(16):
            for q in range(4):
                piece = raw[which, r, :, 128 * q : 128 * (q + 1)].astype(F32)
                flat[pl.ds(16 * r + q, 4, stride=4), :] = piece
        dst[...] = flat[0:256, :].astype(BF16).reshape(16, 16, 128)

    state_load.wait()
    relayout(0, st)

    lead = jnp.where(z == core, Y, 0)

    def all_rows(src, dst, send_sem, recv_sem, start):
        @pl.loop(0, ZY)
        def _(i):
            t = (i + lead) % ZY

            if start:
                @pl.when(t == mine_of)
                def _():
                    pltpu.make_async_copy(src.at[t], dst, recv_sem).start()

            @pl.when(t != mine_of)
            def _():
                copy = remote(
                    src.at[t], dst, send_sem.at[t], recv_sem, owner(t), x, lat
                )
                if start:
                    copy.start()
                else:
                    copy.wait_send()

    def middle_rows(start):
        for i, t, to in ((0, Y - 1, Y), (1, Y, Y - 1)):
            dst = rows.at[2 * i, zy, x]
            if start:
                @pl.when(to == mine_of)
                def _():
                    pltpu.make_async_copy(st.at[t], dst, side_recv.at[i]).start()

            @pl.when(to != mine_of)
            def _():
                copy = remote(
                    st.at[t], dst, middle_send.at[i], side_recv.at[i], owner(to), x, lat
                )
                if start:
                    copy.start()
                else:
                    copy.wait_send()

    def side_rows(start):
        for i, last, middle, to_lat, step in (
            (0, ZY - 1, Y - 1, up, 1),
            (1, 0, Y, down, -1),
        ):
            @pl.when(mine_of != middle)
            def _():
                to_zy = jnp.where(mine_of == last, zy, owner(mine_of + step))
                copy = remote(
                    rows.at[1, :, x], rows.at[2 * i, :, x], side_send.at[i], side_recv.at[i],
                    to_zy, x, jnp.where(mine_of == last, to_lat, lat),
                )
                if start:
                    copy.start()
                else:
                    copy.wait_send()

    all_rows(st, rows.at[1, zy, x], row_send, row_recv, True)
    middle_rows(True)

    def half(place, which):
        return pl.ds(pl.multiple_of((place * 2 + which) * 144, 16), 144)

    def take_weight(part):
        both = []
        for i in range(2):
            at = w_one.at[2 * part + i]
            pltpu.make_async_copy(at, at, w_recv.at[2 * part + i]).wait()
            both.append(w_one[2 * part + i].astype(F32)[:72])
        w_all[part, half(y, core), :] = jnp.concatenate(both, axis=0).astype(BF16)

    def along(turn, place, step):
        to = z * Y + (y + Y + step) % Y
        return push(w_all.at[(z, 1 - z)[turn], half(place, core)], to, x, lat)

    pair = []

    def to_pair(turn, place):
        pair.append(push(w_all.at[(z, 1 - z)[turn], half(place, core)], zy, x, sib))

    take_weight(z)
    rights, lefts = [along(0, y, 1)], [along(0, y, -1)]
    to_pair(0, y)
    take_weight(1 - z)
    nearest = [along(1, y, step) for step in (1, -1, 2, -2)]
    to_pair(1, y)

    def forward(step):
        for copies, way, steps in ((rights, 1, 4), (lefts, -1, 3)):
            if step < steps:
                copies[step].wait_recv()
                place = (y + Y - way * (step + 1)) % Y
                if step + 1 < steps:
                    copies.append(along(0, place, way))
                to_pair(0, place)

    handed = []

    def hand_on(which, on):
        step = (1, -1, 2, -2)[which]
        nearest[which].wait_recv()
        place = (y + Y - step) % Y
        if on:
            by = 2 if step > 0 else -2
            handed.append((along(1, place, by), (y + Y - step - by) % Y))
        to_pair(1, place)

    def round_x(whole, west_half, east_half):
        return (
            push(whole, zy, east, lat),
            push(whole, zy, west, lat),
            west_half,
            east_half,
        )

    def round_x_on(to_east, to_west, west_half, east_half):
        to_east.wait_recv()
        on_east = push(west_half, zy, east, lat)
        to_west.wait_recv()
        return on_east, push(east_half, zy, west, lat)

    cot_load.wait()
    relayout(1, ct)
    all_rows(ct, cots.at[zy, x], cot_send, cot_recv, True)

    forward(0)
    pltpu.make_async_copy(rows.at[1, :, x], rows.at[1, :, x], row_recv).wait()
    side_rows(True)
    row_x = round_x(rows.at[1, :, x], rows.at[1, 0:8, west], rows.at[1, 8:16, east])
    hand_on(0, True)
    hand_on(1, True)
    forward(1)
    hand_on(2, False)
    hand_on(3, True)
    row_on = round_x_on(*row_x)
    for i in range(2):
        at = rows.at[2 * i, :, x]
        pltpu.make_async_copy(at, at, side_recv.at[i]).wait()
    side_x = [
        [push(rows.at[2 * i, :, x], zy, (x + dx) % X, lat) for i in range(2)]
        for dx in (2, 1, 3)
    ]
    forward(2)
    for copy, place in handed:
        copy.wait_recv()
        to_pair(1, place)

    def whole_row(a):
        flat[...] = rows[a].reshape(1024, 128).astype(F32)
        for q in range(4):
            part = flat[pl.ds(q, 256, stride=4), :]
            if a == 0:
                part = jnp.where(row == 0, 0.0, part)
            if a == 2:
                part = jnp.where(row == ROWS - 1, 0.0, part)
            grid[a, :, 128 * q : 128 * (q + 1)] = part.astype(BF16)

    for copy in row_on:
        copy.wait_recv()
    whole_row(1)

    pltpu.make_async_copy(cots.at[:, x], cots.at[:, x], cot_recv).wait()
    cot_x = [push(cots.at[:, x], zy, (x + dx) % X, lat) for dx in range(1, X)]

    forward(3)

    for i in range(2):
        for copies in side_x:
            copies[i].wait_recv()
        whole_row(2 * i)
    for copy in loads:
        copy.wait()
    for copy in pair:
        copy.wait_recv()

    def tap(i):
        if i < 4:
            return w_all[0, 512 * i : 512 * (i + 1), :]
        if i > 4:
            return w_all[1, 512 * i - 2304 : 512 * (i + 1) - 2304, :]
        return jnp.concatenate([w_all[0, 2048:2304, :], w_all[1, 0:256, :]], axis=0)

    two = jnp.zeros((256, 256), F32)
    third = jnp.zeros((256, 128), F32)
    for a in (1, 0, 2):
        two = two + dot(grid[a], jnp.concatenate([tap(3 * a), tap(3 * a + 1)], axis=1))
        third = third + dot(grid[a], tap(3 * a + 2))
    preact = (
        bias[pl.ds(x, 1), :]
        + pltpu.roll(two[:, 0:128], 1, 0)
        + two[:, 128:256]
        + pltpu.roll(third, 255, 0)
    )
    pre[...] = preact
    acts[x] = (preact * jax.nn.sigmoid(preact)).astype(BF16)
    act_x = [push(acts.at[x], zy, (x + dx) % X, lat) for dx in (2, 1, 3)]

    for a in range(3):
        for b in range(3):
            w_turned[b, 128 * a : 128 * (a + 1), :] = tap(3 * a + b).T
    for t in range(3):
        wq_turned[128 * t : 128 * (t + 1), :] = wq[:, 128 * t : 128 * (t + 1)].T

    for copy in cot_x:
        copy.wait_recv()
    flat[...] = cots[...].reshape(1024, 128).astype(F32)
    for q in range(4):
        part = flat[pl.ds(q, 256, stride=4), :].astype(BF16)
        cot_grid[:, 128 * q : 128 * (q + 1)] = part
        cot_blocks[q] = part

    out_grad = dot(cot_grid[...], wo[...], NT).astype(BF16)
    for copy in act_x:
        copy.wait_recv()
    activated = jnp.concatenate([acts[s] for s in range(X)], axis=1)
    projected = dot(activated, wq[...]).astype(BF16)
    queries, keys, values = (projected[:, 128 * t : 128 * (t + 1)] for t in range(3))
    capped = jnp.tanh(dot(queries, keys, NT) * (INV_ROOT / CAP))
    expo = jnp.exp(CAP * capped)
    probs = expo / jnp.sum(expo, axis=-1, keepdims=True)
    probs_b = probs.astype(BF16)
    attended = dot(probs_b, values).astype(BF16)
    centre = jnp.sum(out_grad.astype(F32) * attended.astype(F32), axis=-1, keepdims=True)
    score_grad = (
        probs * (dot(out_grad, values, NT) - centre) * (1.0 - capped * capped) * INV_ROOT
    ).astype(BF16)
    grads = jnp.concatenate(
        [
            dot(score_grad, keys).astype(BF16),
            dot(score_grad, queries, TN).astype(BF16),
            dot(probs_b, out_grad, TN).astype(BF16),
        ],
        axis=1,
    )
    head_part = dot(grads, wq_turned[...])
    for q in range(X):
        blocks[q] = head_part[:, 128 * q : 128 * (q + 1)]

    early = len(started)
    part_x = []
    sides = (1 - z, z)
    halves = [pl.ds(pl.multiple_of(side * 128, 128), 128) for side in sides]
    for half_of in range(2):
        at = halves[half_of]
        for dx in (2, 1, 3):
            i = 3 * half_of + dx - 1
            to = (x + dx) % X
            parts[i] = blocks[to, at].astype(BF16)
            part_x.append(push_to(parts.at[i], parts_in.at[i], zy, to, lat))
    preact = pre[...]
    s = jax.nn.sigmoid(preact)
    pre[...] = s * (1.0 + preact * (1.0 - s))
    for copy in started[:early]:
        copy.wait_send()
    drained[0] = early
    all_weights(False)
    all_rows(st, rows.at[1, zy, x], row_send, row_recv, False)
    all_rows(ct, cots.at[zy, x], cot_send, cot_recv, False)
    middle_rows(False)
    side_rows(False)

    def all_pres(first, start):
        @pl.loop(first, first + 8)
        def _(t):
            dst = pres.at[1 + mine_of]
            if start:
                @pl.when(t == zy)
                def _():
                    pltpu.make_async_copy(own_pre.at[t], dst, pre_recv).start()

            @pl.when(t != zy)
            def _():
                copy = remote(own_pre.at[t], dst, pre_send.at[t], pre_recv, t, x, lat)
                if start:
                    copy.start()
                else:
                    copy.wait_send()

        def ends(slot, to_lat):
            @pl.loop(first, first + 8)
            def _(t):
                copy = remote(
                    own_pre.at[t], pres.at[slot], end_send.at[t], pre_recv, t, x, to_lat
                )
                if start:
                    copy.start()
                else:
                    copy.wait_send()

        @pl.when(mine_of == ZY - 1)
        def _():
            ends(0, up)

        @pl.when(mine_of == 0)
        def _():
            ends(ZY + 1, down)

    for half_of in range(2):
        at = halves[half_of]
        first = 8 * sides[half_of]
        grad_act = blocks[x, at] + cot_blocks[x, at].astype(F32)
        for i in range(3 * half_of, 3 * half_of + 3):
            part_x[i].wait_recv()
        for i in range(3 * half_of, 3 * half_of + 3):
            grad_act = grad_act + parts_in[i].astype(F32)
        own_pre[pl.ds(first, 8)] = (
            (grad_act * pre[at]).astype(BF16).reshape(8, 16, 128)
        )
        all_pres(first, True)

    drain()
    pltpu.make_async_copy(pres, pres, pre_recv).wait()

    @pl.when(lat == 0)
    def _():
        pres[0] = jnp.zeros((16, 128), BF16)

    @pl.when(lat == LATS - 1)
    def _():
        pres[ZY + 1] = jnp.zeros((16, 128), BF16)

    around = jnp.concatenate(
        [pres[2 - a : 2 - a + ZY].reshape(256, 128) for a in range(3)], axis=1
    )

    flat[0:288, :] = pres[...].reshape(288, 128).astype(F32)
    for side, b, at in ((0, 0, 0), (1, 2, 15)):
        edge_of = [flat[pl.ds(16 * (2 - a) + at, 16, stride=16), :] for a in range(3)]
        rim = dot(jnp.concatenate(edge_of, axis=1).astype(BF16), w_turned[b])
        for q in range(4):
            rims[side, q // 2, q % 2] = rim[:, 128 * q : 128 * (q + 1)].astype(BF16)
    rim_west = remote(
        rims.at[0], rims_in.at[x], rim_send.at[0], rim_recv.at[x],
        (zy + ZY - 1) % ZY, X - 1, lat,
    )
    rim_east = remote(
        rims.at[1], rims_in.at[x], rim_send.at[1], rim_recv.at[x], (zy + 1) % ZY, 0, lat
    )
    rim_west.start()
    rim_east.start()

    column = lax.broadcasted_iota(jnp.int32, (256, 256), 0) % 16
    sum_x = []
    for h in range(2):
        at = slice(256 * h, 256 * (h + 1))
        result = jnp.zeros((256, 256), F32)
        for b in range(3):
            acc = dot(around, w_turned[b, :, at])
            if b == 0:
                acc = jnp.where(column == 15, 0.0, pltpu.roll(acc, 255, 0))
            if b == 2:
                acc = jnp.where(column == 0, 0.0, pltpu.roll(acc, 1, 0))
            result = result + acc
        for q in range(2):
            base = 512 * h + 256 * q
            flat[base : base + 256, :] = result[:, 128 * q : 128 * (q + 1)]
            for to in range(X):
                for j in range(4):
                    piece = flat[pl.ds(base + 4 * to + j, 16, stride=16), :]
                    mine[to, h, q, j] = piece.astype(BF16)
        for dx in (2, 1, 3):
            to = (x + dx) % X
            sum_x.append(push_to(mine.at[to, h], sums_in.at[3 * h + dx - 1], zy, to, lat))

    all_pres(0, False)
    all_pres(8, False)

    for h in range(2):
        total = mine[x, h].astype(F32)
        for copy in sum_x[3 * h : 3 * h + 3]:
            copy.wait_recv()
        for i in range(X - 1):
            total = total + sums_in[3 * h + i].astype(F32)
        flat[128 * h : 128 * (h + 1), :] = total.reshape(128, 128)

    def add_rims(j):
        for i in range(X):
            pltpu.make_async_copy(rims_in.at[i], rims_in.at[i], rim_recv.at[i]).wait()
        for q in range(4):
            at = slice(64 * q + 16 * j, 64 * q + 16 * (j + 1))
            total = flat[at]
            for i in range(X):
                total = total + rims_in[i, q // 2, q % 2].astype(F32)
            flat[at] = total

    @pl.when(x == 0)
    def _():
        add_rims(0)

    @pl.when(x == X - 1)
    def _():
        add_rims(3)

    for t in range(ZY):
        out[t] = flat[pl.ds(t, 16, stride=16), :].astype(BF16)

    rim_west.wait_send()
    rim_east.wait_send()
    drain()


PUSHES = 80


def body(state, conv_weight, conv_bias, w_qkv, w_out, cotangent):
    vmem = pl.BlockSpec(memory_space=pltpu.VMEM)
    anywhere = pl.BlockSpec(memory_space=pl.ANY)
    dma = pltpu.SemaphoreType.DMA
    out = pl.pallas_call(
        kernel,
        out_shape=jax.ShapeDtypeStruct((ZY, 16, 128), BF16),
        in_specs=[anywhere] * 6,
        out_specs=vmem,
        scratch_shapes=[
            pltpu.VMEM((2, 16, 4, 512), BF16),
            pltpu.VMEM((72, 512), BF16),
            pltpu.VMEM((ZY, 16, 128), BF16),
            pltpu.VMEM((ZY, 16, 128), BF16),
            pltpu.VMEM((X, 80, 128), BF16),
            pltpu.VMEM((X, 128), F32),
            pltpu.VMEM((3, ZY, X, 16, 128), BF16),
            pltpu.VMEM((ZY, X, 16, 128), BF16),
            pltpu.VMEM((1024, 128), F32),
            pltpu.VMEM((3, 256, 512), BF16),
            pltpu.VMEM((256, 512), BF16),
            pltpu.VMEM((4, 256, 128), BF16),
            pltpu.VMEM((4, 80, 128), BF16),
            pltpu.VMEM((2, 2304, 128), BF16),
            pltpu.VMEM((512, 384), BF16),
            pltpu.VMEM((128, 512), BF16),
            pltpu.VMEM((256, 128), F32),
            pltpu.VMEM((X, 256, 128), BF16),
            pltpu.VMEM((X, 256, 128), F32),
            pltpu.VMEM((6, 128, 128), BF16),
            pltpu.VMEM((6, 128, 128), BF16),
            pltpu.VMEM((ZY, 16, 128), BF16),
            pltpu.VMEM((ZY + 2, 16, 128), BF16),
            pltpu.VMEM((X, 2, 2, 4, ZY, 128), BF16),
            pltpu.VMEM((6, 2, 4, ZY, 128), BF16),
            pltpu.VMEM((2, 2, 2, ZY, 128), BF16),
            pltpu.VMEM((X, 2, 2, ZY, 128), BF16),
            pltpu.VMEM((3, 384, 512), BF16),
            pltpu.VMEM((384, 512), BF16),
            dma((8,)),
            dma((3 * X,)),
            dma((4,)),
            dma((ZY,)),
            dma,
            dma((ZY,)),
            dma,
            dma((ZY,)),
            dma,
            dma((ZY,)),
            dma((2,)),
            dma((X,)),
            dma((2,)),
            dma((2,)),
            dma((2,)),
            dma((PUSHES,)),
            dma((PUSHES,)),
        ],
        compiler_params=pltpu.CompilerParams(
            collective_id=0, has_side_effects=True, vmem_limit_bytes=VMEM_LIMIT
        ),
    )(state, cotangent, conv_weight, conv_bias.reshape(X, 128), w_qkv, w_out)
    return out.reshape(16, 4, 4, 128).transpose(0, 2, 1, 3).reshape(16, 4, 512)


def solution(mesh):
    return jax.shard_map(
        body,
        mesh=mesh,
        in_specs=(P("lat", "lon", None), P("lon", None), P(), P(), P(), P("lat", "lon", None)),
        out_specs=P("lat", "lon", None),
        check_vma=False,
    )
```

```python
import functools
import math

import jax
import jax.numpy as jnp
from jax import lax
from jax.experimental import pallas as pl
from jax.experimental.pallas import tpu as pltpu
from jax.sharding import PartitionSpec as P

X = 4
Y = 8
ZY = 16
LATS = 8
ROWS = ZY * LATS
CAP = 20.0
INV_ROOT = 1.0 / math.sqrt(128.0)
F32 = jnp.float32
BF16 = jnp.bfloat16
VMEM_LIMIT = 60 * 1024 * 1024

NN = (((1,), (0,)), ((), ()))
NT = (((1,), (1,)), ((), ()))
TN = (((0,), (0,)), ((), ()))


def dot(a, b, dims=NN):
    return lax.dot_general(a, b, dims, preferred_element_type=F32)


def kernel(
    st_hbm, ct_hbm, cw_hbm, bias_hbm, wqkv, wout, out,
    raw, raw_w, st, ct, wp, bias,
    rows, cots, flat, grid, cot_grid, cot_blocks, w_one, w_all, wq, wo,
    pre, acts, blocks, parts, parts_in, own_pre, pres, mine, sums_in, rims, rims_in,
    w_turned, wq_turned,
    load_sem, w_send, w_recv, row_send, row_recv, cot_send, cot_recv, pre_send, pre_recv,
    end_send, rim_send, rim_recv, middle_send, side_send, side_recv,
    send, recv,
):
    lon = lax.axis_index("lon")
    lat = lax.axis_index("lat")
    zy, x = lon // X, lon % X
    z, y = zy // Y, zy % Y
    core = lat % 2
    sib = lat + 1 - 2 * core
    mine_of = jnp.where(z == core, y, ZY - 1 - y)
    row = lat * ZY + mine_of
    up, down = (lat + 1) % LATS, (lat + LATS - 1) % LATS

    def owner(t):
        return jnp.where(t < Y, core * Y + t, (1 - core) * Y + ZY - 1 - t)

    east, west = (x + 1) % X, (x + X - 1) % X

    def remote(src, dst, send_sem, recv_sem, to_zy, to_x, to_lat):
        return pltpu.make_async_remote_copy(
            src_ref=src,
            dst_ref=dst,
            send_sem=send_sem,
            recv_sem=recv_sem,
            device_id={"lon": to_zy * X + to_x, "lat": to_lat},
            device_id_type=pl.DeviceIdType.MESH,
        )

    started = []

    def push_to(src, dst, to_zy, to_x, to_lat):
        i = len(started)
        copy = remote(src, dst, send.at[i], recv.at[i], to_zy, to_x, to_lat)
        copy.start()
        started.append(copy)
        return copy

    drained = [0]

    def drain():
        for copy in started[drained[0] :]:
            copy.wait_send()
        drained[0] = len(started)

    def push(ref, to_zy, to_x, to_lat):
        return push_to(ref, ref, to_zy, to_x, to_lat)

    def load(i, src, dst):
        copy = pltpu.make_async_copy(src, dst, load_sem.at[i])
        copy.start()
        return copy

    weight_load = load(0, cw_hbm, raw_w)
    state_load = load(1, st_hbm, raw.at[0])
    cot_load = load(2, ct_hbm, raw.at[1])
    barrier = pltpu.get_barrier_semaphore()

    def hello(to_zy, to_x, to_lat):
        pl.semaphore_signal(
            barrier,
            inc=1,
            device_id={"lon": to_zy * X + to_x, "lat": to_lat},
            device_id_type=pl.DeviceIdType.MESH,
        )

    other_zy = (1 - z) * Y + y
    for dx in range(1, X):
        hello(zy, (x + dx) % X, lat)
    hello(zy, x, sib)

    @pl.loop(1, ZY)
    def _(d):
        hello((zy + d) % ZY, x, lat)

    hello(core * Y, x, down)
    hello((1 - core) * Y, x, up)

    plane = lat // 2
    near = jnp.where(plane < 2, 3, 0) * 2 + core
    for i in range(2):
        hello(other_zy, 2 * core + i, near)

    @pl.when(x == 0)
    def _():
        for i in range(X):
            hello((zy + ZY - 1) % ZY, i, lat)

    @pl.when(x == X - 1)
    def _():
        for i in range(X):
            hello((zy + 1) % ZY, i, lat)

    loads = [load(3, bias_hbm, bias)]
    for t in range(3):
        source = wqkv.at[:, pl.ds(pl.multiple_of(t * 512 + x * 128, 128), 128)]
        loads.append(load(4 + t, source, wq.at[:, 128 * t : 128 * (t + 1)]))
    loads.append(load(7, wout.at[pl.ds(pl.multiple_of(x * 128, 128), 128)], wo))

    weight_load.wait()
    for q in range(X):
        piece = raw_w[:, 128 * q : 128 * (q + 1)].astype(F32)
        wp[q] = jnp.concatenate([piece, jnp.zeros((8, 128), F32)], axis=0).astype(BF16)

    edge = (mine_of == 0) | (mine_of == ZY - 1)
    sends_weight = x // 2 == core
    crosses = sends_weight & ((plane == 0) | (plane == 3))
    pl.semaphore_wait(
        barrier,
        (X - 1) + (ZY - 1) + 1 + 2 + jnp.where(edge, ZY, 0) + jnp.where(crosses, 2 * X, 0),
    )

    slot = z * 2 + x % 2

    def all_weights(start):
        def across(copy):
            if start:
                copy.start()
            else:
                copy.wait_send()

        @pl.when(crosses)
        def _():
            for k in range(2):
                to_lat = jnp.where(plane == 3, k, 2 + k) * 2 + core
                for t in range(X):
                    across(
                        remote(
                            wp.at[t], w_one.at[slot], w_send.at[X + X * k + t],
                            w_recv.at[slot], other_zy, t, to_lat,
                        )
                    )

        @pl.when(sends_weight)
        def _():
            for t in range(X):
                if start:
                    @pl.when(t == x)
                    def _():
                        pltpu.make_async_copy(
                            wp.at[t], w_one.at[slot], w_recv.at[slot]
                        ).start()

                @pl.when(t != x)
                def _():
                    across(
                        remote(
                            wp.at[t], w_one.at[slot], w_send.at[t], w_recv.at[slot],
                            zy, t, lat,
                        )
                    )

    all_weights(True)

    def relayout(which, dst):
        for r in range(16):
            for q in range(4):
                piece = raw[which, r, :, 128 * q : 128 * (q + 1)].astype(F32)
                flat[pl.ds(16 * r + q, 4, stride=4), :] = piece
        dst[...] = flat[0:256, :].astype(BF16).reshape(16, 16, 128)

    state_load.wait()
    relayout(0, st)

    lead = jnp.where(z == core, Y, 0)

    def all_rows(src, dst, send_sem, recv_sem, start):
        @pl.loop(0, ZY)
        def _(i):
            t = (i + lead) % ZY

            if start:
                @pl.when(t == mine_of)
                def _():
                    pltpu.make_async_copy(src.at[t], dst, recv_sem).start()

            @pl.when(t != mine_of)
            def _():
                copy = remote(
                    src.at[t], dst, send_sem.at[t], recv_sem, owner(t), x, lat
                )
                if start:
                    copy.start()
                else:
                    copy.wait_send()

    def middle_rows(start):
        for i, t, to in ((0, Y - 1, Y), (1, Y, Y - 1)):
            dst = rows.at[2 * i, zy, x]
            if start:
                @pl.when(to == mine_of)
                def _():
                    pltpu.make_async_copy(st.at[t], dst, side_recv.at[i]).start()

            @pl.when(to != mine_of)
            def _():
                copy = remote(
                    st.at[t], dst, middle_send.at[i], side_recv.at[i], owner(to), x, lat
                )
                if start:
                    copy.start()
                else:
                    copy.wait_send()

    def side_rows(start):
        for i, last, middle, to_lat, step in (
            (0, ZY - 1, Y - 1, up, 1),
            (1, 0, Y, down, -1),
        ):
            @pl.when(mine_of != middle)
            def _():
                to_zy = jnp.where(mine_of == last, zy, owner(mine_of + step))
                copy = remote(
                    rows.at[1, :, x], rows.at[2 * i, :, x], side_send.at[i], side_recv.at[i],
                    to_zy, x, jnp.where(mine_of == last, to_lat, lat),
                )
                if start:
                    copy.start()
                else:
                    copy.wait_send()

    all_rows(st, rows.at[1, zy, x], row_send, row_recv, True)
    middle_rows(True)

    def half(place, which):
        return pl.ds(pl.multiple_of((place * 2 + which) * 144, 16), 144)

    def take_weight(part):
        both = []
        for i in range(2):
            at = w_one.at[2 * part + i]
            pltpu.make_async_copy(at, at, w_recv.at[2 * part + i]).wait()
            both.append(w_one[2 * part + i].astype(F32)[:72])
        w_all[part, half(y, core), :] = jnp.concatenate(both, axis=0).astype(BF16)

    def along(turn, place, step):
        to = z * Y + (y + Y + step) % Y
        return push(w_all.at[(z, 1 - z)[turn], half(place, core)], to, x, lat)

    pair = []

    def to_pair(turn, place):
        pair.append(push(w_all.at[(z, 1 - z)[turn], half(place, core)], zy, x, sib))

    take_weight(z)
    rights, lefts = [along(0, y, 1)], [along(0, y, -1)]
    to_pair(0, y)
    take_weight(1 - z)
    nearest = [along(1, y, step) for step in (1, -1, 2, -2)]
    to_pair(1, y)

    def forward(step):
        for copies, way, steps in ((rights, 1, 4), (lefts, -1, 3)):
            if step < steps:
                copies[step].wait_recv()
                place = (y + Y - way * (step + 1)) % Y
                if step + 1 < steps:
                    copies.append(along(0, place, way))
                to_pair(0, place)

    handed = []

    def hand_on(which, on):
        step = (1, -1, 2, -2)[which]
        nearest[which].wait_recv()
        place = (y + Y - step) % Y
        if on:
            by = 2 if step > 0 else -2
            handed.append((along(1, place, by), (y + Y - step - by) % Y))
        to_pair(1, place)

    def round_x(whole, west_half, east_half):
        return (
            push(whole, zy, east, lat),
            push(whole, zy, west, lat),
            west_half,
            east_half,
        )

    def round_x_on(to_east, to_west, west_half, east_half):
        to_east.wait_recv()
        on_east = push(west_half, zy, east, lat)
        to_west.wait_recv()
        return on_east, push(east_half, zy, west, lat)

    cot_load.wait()
    relayout(1, ct)
    all_rows(ct, cots.at[zy, x], cot_send, cot_recv, True)

    forward(0)
    pltpu.make_async_copy(rows.at[1, :, x], rows.at[1, :, x], row_recv).wait()
    side_rows(True)
    row_x = round_x(rows.at[1, :, x], rows.at[1, 0:8, west], rows.at[1, 8:16, east])
    hand_on(0, True)
    hand_on(1, True)
    forward(1)
    hand_on(2, False)
    hand_on(3, True)
    row_on = round_x_on(*row_x)
    for i in range(2):
        at = rows.at[2 * i, :, x]
        pltpu.make_async_copy(at, at, side_recv.at[i]).wait()
    side_x = [
        [push(rows.at[2 * i, :, x], zy, (x + dx) % X, lat) for i in range(2)]
        for dx in (2, 1, 3)
    ]
    forward(2)
    for copy, place in handed:
        copy.wait_recv()
        to_pair(1, place)

    def whole_row(a):
        flat[...] = rows[a].reshape(1024, 128).astype(F32)
        for q in range(4):
            part = flat[pl.ds(q, 256, stride=4), :]
            if a == 0:
                part = jnp.where(row == 0, 0.0, part)
            if a == 2:
                part = jnp.where(row == ROWS - 1, 0.0, part)
            grid[a, :, 128 * q : 128 * (q + 1)] = part.astype(BF16)

    for copy in row_on:
        copy.wait_recv()
    whole_row(1)

    pltpu.make_async_copy(cots.at[:, x], cots.at[:, x], cot_recv).wait()
    cot_x = [push(cots.at[:, x], zy, (x + dx) % X, lat) for dx in range(1, X)]

    forward(3)

    for copy in loads:
        copy.wait()
    for copy in pair:
        copy.wait_recv()

    def tap(i):
        if i < 4:
            return w_all[0, 512 * i : 512 * (i + 1), :]
        if i > 4:
            return w_all[1, 512 * i - 2304 : 512 * (i + 1) - 2304, :]
        return jnp.concatenate([w_all[0, 2048:2304, :], w_all[1, 0:256, :]], axis=0)

    two = jnp.zeros((256, 256), F32)
    third = jnp.zeros((256, 128), F32)
    for a in (1, 0, 2):
        if a != 1:
            for copies in side_x:
                copies[a // 2].wait_recv()
            whole_row(a)
        two = two + dot(grid[a], jnp.concatenate([tap(3 * a), tap(3 * a + 1)], axis=1))
        third = third + dot(grid[a], tap(3 * a + 2))
    preact = (
        bias[pl.ds(x, 1), :]
        + pltpu.roll(two[:, 0:128], 1, 0)
        + two[:, 128:256]
        + pltpu.roll(third, 255, 0)
    )
    pre[...] = preact
    acts[x] = (preact * jax.nn.sigmoid(preact)).astype(BF16)
    act_x = [push(acts.at[x], zy, (x + dx) % X, lat) for dx in (2, 1, 3)]

    for a in range(3):
        for b in range(3):
            w_turned[b, 128 * a : 128 * (a + 1), :] = tap(3 * a + b).T
    for t in range(3):
        wq_turned[128 * t : 128 * (t + 1), :] = wq[:, 128 * t : 128 * (t + 1)].T

    for copy in cot_x:
        copy.wait_recv()
    flat[...] = cots[...].reshape(1024, 128).astype(F32)
    for q in range(4):
        part = flat[pl.ds(q, 256, stride=4), :].astype(BF16)
        cot_grid[:, 128 * q : 128 * (q + 1)] = part
        cot_blocks[q] = part

    out_grad = dot(cot_grid[...], wo[...], NT).astype(BF16)
    for copy in act_x:
        copy.wait_recv()
    activated = jnp.concatenate([acts[s] for s in range(X)], axis=1)
    projected = dot(activated, wq[...]).astype(BF16)
    queries, keys, values = (projected[:, 128 * t : 128 * (t + 1)] for t in range(3))
    capped = jnp.tanh(dot(queries, keys, NT) * (INV_ROOT / CAP))
    expo = jnp.exp(CAP * capped)
    probs = expo * (1.0 / jnp.sum(expo, axis=-1, keepdims=True))
    probs_b = probs.astype(BF16)
    attended = dot(probs_b, values).astype(BF16)
    centre = jnp.sum(out_grad.astype(F32) * attended.astype(F32), axis=-1, keepdims=True)
    score_grad = (
        probs * (dot(out_grad, values, NT) - centre) * (1.0 - capped * capped) * INV_ROOT
    ).astype(BF16)
    grads = jnp.concatenate(
        [
            dot(score_grad, keys).astype(BF16),
            dot(score_grad, queries, TN).astype(BF16),
            dot(probs_b, out_grad, TN).astype(BF16),
        ],
        axis=1,
    )
    head_part = dot(grads, wq_turned[...])
    for q in range(X):
        blocks[q] = head_part[:, 128 * q : 128 * (q + 1)]

    early = len(started)
    part_x = []
    sides = (1 - z, z)
    halves = [pl.ds(pl.multiple_of(side * 128, 128), 128) for side in sides]
    for half_of in range(2):
        at = halves[half_of]
        for dx in (2, 1, 3):
            i = 3 * half_of + dx - 1
            to = (x + dx) % X
            parts[i] = blocks[to, at].astype(BF16)
            part_x.append(push_to(parts.at[i], parts_in.at[i], zy, to, lat))
    preact = pre[...]
    s = jax.nn.sigmoid(preact)
    pre[...] = s * (1.0 + preact * (1.0 - s))
    for copy in started[:early]:
        copy.wait_send()
    drained[0] = early
    all_weights(False)
    all_rows(st, rows.at[1, zy, x], row_send, row_recv, False)
    all_rows(ct, cots.at[zy, x], cot_send, cot_recv, False)
    middle_rows(False)
    side_rows(False)

    def all_pres(first, start):
        @pl.loop(first, first + 8)
        def _(t):
            dst = pres.at[1 + mine_of]
            if start:
                @pl.when(t == zy)
                def _():
                    pltpu.make_async_copy(own_pre.at[t], dst, pre_recv).start()

            @pl.when(t != zy)
            def _():
                copy = remote(own_pre.at[t], dst, pre_send.at[t], pre_recv, t, x, lat)
                if start:
                    copy.start()
                else:
                    copy.wait_send()

        def ends(slot, to_lat):
            @pl.loop(first, first + 8)
            def _(t):
                copy = remote(
                    own_pre.at[t], pres.at[slot], end_send.at[t], pre_recv, t, x, to_lat
                )
                if start:
                    copy.start()
                else:
                    copy.wait_send()

        @pl.when(mine_of == ZY - 1)
        def _():
            ends(0, up)

        @pl.when(mine_of == 0)
        def _():
            ends(ZY + 1, down)

    for half_of in range(2):
        at = halves[half_of]
        first = 8 * sides[half_of]
        grad_act = blocks[x, at] + cot_blocks[x, at].astype(F32)
        for i in range(3 * half_of, 3 * half_of + 3):
            part_x[i].wait_recv()
        for i in range(3 * half_of, 3 * half_of + 3):
            grad_act = grad_act + parts_in[i].astype(F32)
        own_pre[pl.ds(first, 8)] = (
            (grad_act * pre[at]).astype(BF16).reshape(8, 16, 128)
        )
        all_pres(first, True)

    drain()
    pltpu.make_async_copy(pres, pres, pre_recv).wait()

    @pl.when(lat == 0)
    def _():
        pres[0] = jnp.zeros((16, 128), BF16)

    @pl.when(lat == LATS - 1)
    def _():
        pres[ZY + 1] = jnp.zeros((16, 128), BF16)

    around = jnp.concatenate(
        [pres[2 - a : 2 - a + ZY].reshape(256, 128) for a in range(3)], axis=1
    )

    flat[0:288, :] = pres[...].reshape(288, 128).astype(F32)
    for side, b, at in ((0, 0, 0), (1, 2, 15)):
        edge_of = [flat[pl.ds(16 * (2 - a) + at, 16, stride=16), :] for a in range(3)]
        rim = dot(jnp.concatenate(edge_of, axis=1).astype(BF16), w_turned[b])
        for q in range(4):
            rims[side, q // 2, q % 2] = rim[:, 128 * q : 128 * (q + 1)].astype(BF16)
    rim_west = remote(
        rims.at[0], rims_in.at[x], rim_send.at[0], rim_recv.at[x],
        (zy + ZY - 1) % ZY, X - 1, lat,
    )
    rim_east = remote(
        rims.at[1], rims_in.at[x], rim_send.at[1], rim_recv.at[x], (zy + 1) % ZY, 0, lat
    )
    rim_west.start()
    rim_east.start()

    column = lax.broadcasted_iota(jnp.int32, (256, 256), 0) % 16
    sum_x = []
    for h in range(2):
        at = slice(256 * h, 256 * (h + 1))
        result = jnp.zeros((256, 256), F32)
        for b in range(3):
            acc = dot(around, w_turned[b, :, at])
            if b == 0:
                acc = jnp.where(column == 15, 0.0, pltpu.roll(acc, 255, 0))
            if b == 2:
                acc = jnp.where(column == 0, 0.0, pltpu.roll(acc, 1, 0))
            result = result + acc
        for q in range(2):
            base = 512 * h + 256 * q
            flat[base : base + 256, :] = result[:, 128 * q : 128 * (q + 1)]
            for to in range(X):
                for j in range(4):
                    piece = flat[pl.ds(base + 4 * to + j, 16, stride=16), :]
                    mine[to, h, q, j] = piece.astype(BF16)
        for dx in (2, 1, 3):
            to = (x + dx) % X
            sum_x.append(push_to(mine.at[to, h], sums_in.at[3 * h + dx - 1], zy, to, lat))

    all_pres(0, False)
    all_pres(8, False)

    for h in range(2):
        total = mine[x, h].astype(F32)
        for copy in sum_x[3 * h : 3 * h + 3]:
            copy.wait_recv()
        for i in range(X - 1):
            total = total + sums_in[3 * h + i].astype(F32)
        flat[128 * h : 128 * (h + 1), :] = total.reshape(128, 128)

    def add_rims(j):
        for i in range(X):
            pltpu.make_async_copy(rims_in.at[i], rims_in.at[i], rim_recv.at[i]).wait()
        for q in range(4):
            at = slice(64 * q + 16 * j, 64 * q + 16 * (j + 1))
            total = flat[at]
            for i in range(X):
                total = total + rims_in[i, q // 2, q % 2].astype(F32)
            flat[at] = total

    @pl.when(x == 0)
    def _():
        add_rims(0)

    @pl.when(x == X - 1)
    def _():
        add_rims(3)

    for t in range(ZY):
        out[t] = flat[pl.ds(t, 16, stride=16), :].astype(BF16)

    rim_west.wait_send()
    rim_east.wait_send()
    drain()


PUSHES = 80


def body(state, conv_weight, conv_bias, w_qkv, w_out, cotangent):
    vmem = pl.BlockSpec(memory_space=pltpu.VMEM)
    anywhere = pl.BlockSpec(memory_space=pl.ANY)
    dma = pltpu.SemaphoreType.DMA
    out = pl.pallas_call(
        kernel,
        out_shape=jax.ShapeDtypeStruct((ZY, 16, 128), BF16),
        in_specs=[anywhere] * 6,
        out_specs=vmem,
        scratch_shapes=[
            pltpu.VMEM((2, 16, 4, 512), BF16),
            pltpu.VMEM((72, 512), BF16),
            pltpu.VMEM((ZY, 16, 128), BF16),
            pltpu.VMEM((ZY, 16, 128), BF16),
            pltpu.VMEM((X, 80, 128), BF16),
            pltpu.VMEM((X, 128), F32),
            pltpu.VMEM((3, ZY, X, 16, 128), BF16),
            pltpu.VMEM((ZY, X, 16, 128), BF16),
            pltpu.VMEM((1024, 128), F32),
            pltpu.VMEM((3, 256, 512), BF16),
            pltpu.VMEM((256, 512), BF16),
            pltpu.VMEM((4, 256, 128), BF16),
            pltpu.VMEM((4, 80, 128), BF16),
            pltpu.VMEM((2, 2304, 128), BF16),
            pltpu.VMEM((512, 384), BF16),
            pltpu.VMEM((128, 512), BF16),
            pltpu.VMEM((256, 128), F32),
            pltpu.VMEM((X, 256, 128), BF16),
            pltpu.VMEM((X, 256, 128), F32),
            pltpu.VMEM((6, 128, 128), BF16),
            pltpu.VMEM((6, 128, 128), BF16),
            pltpu.VMEM((ZY, 16, 128), BF16),
            pltpu.VMEM((ZY + 2, 16, 128), BF16),
            pltpu.VMEM((X, 2, 2, 4, ZY, 128), BF16),
            pltpu.VMEM((6, 2, 4, ZY, 128), BF16),
            pltpu.VMEM((2, 2, 2, ZY, 128), BF16),
            pltpu.VMEM((X, 2, 2, ZY, 128), BF16),
            pltpu.VMEM((3, 384, 512), BF16),
            pltpu.VMEM((384, 512), BF16),
            dma((8,)),
            dma((3 * X,)),
            dma((4,)),
            dma((ZY,)),
            dma,
            dma((ZY,)),
            dma,
            dma((ZY,)),
            dma,
            dma((ZY,)),
            dma((2,)),
            dma((X,)),
            dma((2,)),
            dma((2,)),
            dma((2,)),
            dma((PUSHES,)),
            dma((PUSHES,)),
        ],
        compiler_params=pltpu.CompilerParams(
            collective_id=0, has_side_effects=True, vmem_limit_bytes=VMEM_LIMIT
        ),
    )(state, cotangent, conv_weight, conv_bias.reshape(X, 128), w_qkv, w_out)
    return out.reshape(16, 4, 4, 128).transpose(0, 2, 1, 3).reshape(16, 4, 512)


def solution(mesh):
    return jax.shard_map(
        body,
        mesh=mesh,
        in_specs=(P("lat", "lon", None), P("lon", None), P(), P(), P(), P("lat", "lon", None)),
        out_specs=P("lat", "lon", None),
        check_vma=False,
    )
```

```python
import functools
import math

import jax
import jax.numpy as jnp
from jax import lax
from jax.experimental import pallas as pl
from jax.experimental.pallas import tpu as pltpu
from jax.sharding import PartitionSpec as P

X = 4
Y = 8
ZY = 16
LATS = 8
ROWS = ZY * LATS
CAP = 20.0
INV_ROOT = 1.0 / math.sqrt(128.0)
F32 = jnp.float32
BF16 = jnp.bfloat16
VMEM_LIMIT = 60 * 1024 * 1024

NN = (((1,), (0,)), ((), ()))
NT = (((1,), (1,)), ((), ()))
TN = (((0,), (0,)), ((), ()))


def dot(a, b, dims=NN):
    return lax.dot_general(a, b, dims, preferred_element_type=F32)


def kernel(
    st_hbm, ct_hbm, cw_hbm, bias_hbm, wqkv, wout, out,
    raw, raw_w, st, ct, wp, bias,
    rows, cots, flat, grid, cot_grid, cot_blocks, w_one, w_all, wq, wo,
    pre, acts, blocks, parts, parts_in, own_pre, pres, mine, sums_in, rims, rims_in,
    w_turned, wq_turned,
    load_sem, w_send, w_recv, row_send, row_recv, cot_send, cot_recv, pre_send, pre_recv,
    end_send, rim_send, rim_recv, middle_send, side_send, side_recv,
    send, recv,
):
    lon = lax.axis_index("lon")
    lat = lax.axis_index("lat")
    zy, x = lon // X, lon % X
    z, y = zy // Y, zy % Y
    core = lat % 2
    sib = lat + 1 - 2 * core
    mine_of = jnp.where(z == core, y, ZY - 1 - y)
    row = lat * ZY + mine_of
    up, down = (lat + 1) % LATS, (lat + LATS - 1) % LATS

    def owner(t):
        return jnp.where(t < Y, core * Y + t, (1 - core) * Y + ZY - 1 - t)

    east, west = (x + 1) % X, (x + X - 1) % X

    def remote(src, dst, send_sem, recv_sem, to_zy, to_x, to_lat):
        return pltpu.make_async_remote_copy(
            src_ref=src,
            dst_ref=dst,
            send_sem=send_sem,
            recv_sem=recv_sem,
            device_id={"lon": to_zy * X + to_x, "lat": to_lat},
            device_id_type=pl.DeviceIdType.MESH,
        )

    started = []

    def push_to(src, dst, to_zy, to_x, to_lat):
        i = len(started)
        copy = remote(src, dst, send.at[i], recv.at[i], to_zy, to_x, to_lat)
        copy.start()
        started.append(copy)
        return copy

    drained = [0]

    def drain():
        for copy in started[drained[0] :]:
            copy.wait_send()
        drained[0] = len(started)

    def push(ref, to_zy, to_x, to_lat):
        return push_to(ref, ref, to_zy, to_x, to_lat)

    def load(i, src, dst):
        copy = pltpu.make_async_copy(src, dst, load_sem.at[i])
        copy.start()
        return copy

    weight_load = load(0, cw_hbm, raw_w)
    state_load = load(1, st_hbm, raw.at[0])
    cot_load = load(2, ct_hbm, raw.at[1])
    barrier = pltpu.get_barrier_semaphore()

    def hello(to_zy, to_x, to_lat):
        pl.semaphore_signal(
            barrier,
            inc=1,
            device_id={"lon": to_zy * X + to_x, "lat": to_lat},
            device_id_type=pl.DeviceIdType.MESH,
        )

    other_zy = (1 - z) * Y + y
    for dx in range(1, X):
        hello(zy, (x + dx) % X, lat)
    hello(zy, x, sib)

    @pl.loop(1, ZY)
    def _(d):
        hello((zy + d) % ZY, x, lat)

    hello(core * Y, x, down)
    hello((1 - core) * Y, x, up)

    plane = lat // 2
    near = jnp.where(plane < 2, 3, 0) * 2 + core
    for i in range(2):
        hello(other_zy, 2 * core + i, near)

    @pl.when(x == 0)
    def _():
        for i in range(X):
            hello((zy + ZY - 1) % ZY, i, lat)

    @pl.when(x == X - 1)
    def _():
        for i in range(X):
            hello((zy + 1) % ZY, i, lat)

    loads = [load(3, bias_hbm, bias)]
    for t in range(3):
        source = wqkv.at[:, pl.ds(pl.multiple_of(t * 512 + x * 128, 128), 128)]
        loads.append(load(4 + t, source, wq.at[:, 128 * t : 128 * (t + 1)]))
    loads.append(load(7, wout.at[pl.ds(pl.multiple_of(x * 128, 128), 128)], wo))

    weight_load.wait()
    for q in range(X):
        piece = raw_w[:, 128 * q : 128 * (q + 1)].astype(F32)
        wp[q] = jnp.concatenate([piece, jnp.zeros((8, 128), F32)], axis=0).astype(BF16)

    edge = (mine_of == 0) | (mine_of == ZY - 1)
    sends_weight = x // 2 == core
    crosses = sends_weight & ((plane == 0) | (plane == 3))
    pl.semaphore_wait(
        barrier,
        (X - 1) + (ZY - 1) + 1 + 2 + jnp.where(edge, ZY, 0) + jnp.where(crosses, 2 * X, 0),
    )

    slot = z * 2 + x % 2

    def all_weights(start):
        def across(copy):
            if start:
                copy.start()
            else:
                copy.wait_send()

        @pl.when(crosses)
        def _():
            for k in range(2):
                to_lat = jnp.where(plane == 3, k, 2 + k) * 2 + core
                for t in range(X):
                    across(
                        remote(
                            wp.at[t], w_one.at[slot], w_send.at[X + X * k + t],
                            w_recv.at[slot], other_zy, t, to_lat,
                        )
                    )

        @pl.when(sends_weight)
        def _():
            for t in range(X):
                if start:
                    @pl.when(t == x)
                    def _():
                        pltpu.make_async_copy(
                            wp.at[t], w_one.at[slot], w_recv.at[slot]
                        ).start()

                @pl.when(t != x)
                def _():
                    across(
                        remote(
                            wp.at[t], w_one.at[slot], w_send.at[t], w_recv.at[slot],
                            zy, t, lat,
                        )
                    )

    all_weights(True)

    def relayout(which, dst):
        for r in range(16):
            for q in range(4):
                piece = raw[which, r, :, 128 * q : 128 * (q + 1)].astype(F32)
                flat[pl.ds(16 * r + q, 4, stride=4), :] = piece
        dst[...] = flat[0:256, :].astype(BF16).reshape(16, 16, 128)

    state_load.wait()
    relayout(0, st)

    across_z = [(1 - z) * Y + (y + k) % Y for k in range(Y)]
    along_y = [z * Y + (y + k) % Y for k in range(1, Y)]

    def row_of(place):
        return jnp.where(place // Y == core, place % Y, ZY - 1 - place % Y)

    def all_rows(src, dst, send_sem, recv_sem, start):
        for k, place in enumerate(across_z + along_y):
            copy = remote(
                src.at[row_of(place)], dst, send_sem.at[k], recv_sem, place, x, lat
            )
            if start:
                copy.start()
            else:
                copy.wait_send()
        if start:
            pltpu.make_async_copy(src.at[mine_of], dst, recv_sem).start()

    def middle_rows(start):
        for i, t, to in ((0, Y - 1, Y), (1, Y, Y - 1)):
            dst = rows.at[2 * i, zy, x]
            if start:
                @pl.when(to == mine_of)
                def _():
                    pltpu.make_async_copy(st.at[t], dst, side_recv.at[i]).start()

            @pl.when(to != mine_of)
            def _():
                copy = remote(
                    st.at[t], dst, middle_send.at[i], side_recv.at[i], owner(to), x, lat
                )
                if start:
                    copy.start()
                else:
                    copy.wait_send()

    def side_rows(start):
        for i, last, middle, to_lat, step in (
            (0, ZY - 1, Y - 1, up, 1),
            (1, 0, Y, down, -1),
        ):
            @pl.when(mine_of != middle)
            def _():
                to_zy = jnp.where(mine_of == last, zy, owner(mine_of + step))
                copy = remote(
                    rows.at[1, :, x], rows.at[2 * i, :, x], side_send.at[i], side_recv.at[i],
                    to_zy, x, jnp.where(mine_of == last, to_lat, lat),
                )
                if start:
                    copy.start()
                else:
                    copy.wait_send()

    all_rows(st, rows.at[1, zy, x], row_send, row_recv, True)
    middle_rows(True)

    def half(place, which):
        return pl.ds(pl.multiple_of((place * 2 + which) * 144, 16), 144)

    def take_weight(part):
        both = []
        for i in range(2):
            at = w_one.at[2 * part + i]
            pltpu.make_async_copy(at, at, w_recv.at[2 * part + i]).wait()
            both.append(w_one[2 * part + i].astype(F32)[:72])
        w_all[part, half(y, core), :] = jnp.concatenate(both, axis=0).astype(BF16)

    def along(turn, place, step):
        to = z * Y + (y + Y + step) % Y
        return push(w_all.at[(z, 1 - z)[turn], half(place, core)], to, x, lat)

    pair = []

    def to_pair(turn, place):
        pair.append(push(w_all.at[(z, 1 - z)[turn], half(place, core)], zy, x, sib))

    take_weight(z)
    rights, lefts = [along(0, y, 1)], [along(0, y, -1)]
    to_pair(0, y)
    take_weight(1 - z)
    nearest = [along(1, y, step) for step in (1, -1, 2, -2)]
    to_pair(1, y)

    def forward(step):
        for copies, way, steps in ((rights, 1, 4), (lefts, -1, 3)):
            if step < steps:
                copies[step].wait_recv()
                place = (y + Y - way * (step + 1)) % Y
                if step + 1 < steps:
                    copies.append(along(0, place, way))
                to_pair(0, place)

    handed = []

    def hand_on(which, on):
        step = (1, -1, 2, -2)[which]
        nearest[which].wait_recv()
        place = (y + Y - step) % Y
        if on:
            by = 2 if step > 0 else -2
            handed.append((along(1, place, by), (y + Y - step - by) % Y))
        to_pair(1, place)

    def round_x(whole, west_half, east_half):
        return (
            push(whole, zy, east, lat),
            push(whole, zy, west, lat),
            west_half,
            east_half,
        )

    def round_x_on(to_east, to_west, west_half, east_half):
        to_east.wait_recv()
        on_east = push(west_half, zy, east, lat)
        to_west.wait_recv()
        return on_east, push(east_half, zy, west, lat)

    cot_load.wait()
    relayout(1, ct)
    all_rows(ct, cots.at[zy, x], cot_send, cot_recv, True)

    forward(0)
    pltpu.make_async_copy(rows.at[1, :, x], rows.at[1, :, x], row_recv).wait()
    side_rows(True)
    row_x = round_x(rows.at[1, :, x], rows.at[1, 0:8, west], rows.at[1, 8:16, east])
    hand_on(0, True)
    hand_on(1, True)
    forward(1)
    hand_on(2, False)
    hand_on(3, True)
    row_on = round_x_on(*row_x)
    for i in range(2):
        at = rows.at[2 * i, :, x]
        pltpu.make_async_copy(at, at, side_recv.at[i]).wait()
    side_x = [
        [push(rows.at[2 * i, :, x], zy, (x + dx) % X, lat) for i in range(2)]
        for dx in (2, 1, 3)
    ]
    forward(2)
    for copy, place in handed:
        copy.wait_recv()
        to_pair(1, place)

    def whole_row(a):
        flat[...] = rows[a].reshape(1024, 128).astype(F32)
        for q in range(4):
            part = flat[pl.ds(q, 256, stride=4), :]
            if a == 0:
                part = jnp.where(row == 0, 0.0, part)
            if a == 2:
                part = jnp.where(row == ROWS - 1, 0.0, part)
            grid[a, :, 128 * q : 128 * (q + 1)] = part.astype(BF16)

    for copy in row_on:
        copy.wait_recv()
    whole_row(1)

    pltpu.make_async_copy(cots.at[:, x], cots.at[:, x], cot_recv).wait()
    cot_x = [push(cots.at[:, x], zy, (x + dx) % X, lat) for dx in range(1, X)]

    forward(3)

    for copy in loads:
        copy.wait()
    for copy in pair:
        copy.wait_recv()

    def tap(i):
        if i < 4:
            return w_all[0, 512 * i : 512 * (i + 1), :]
        if i > 4:
            return w_all[1, 512 * i - 2304 : 512 * (i + 1) - 2304, :]
        return jnp.concatenate([w_all[0, 2048:2304, :], w_all[1, 0:256, :]], axis=0)

    two = jnp.zeros((256, 256), F32)
    third = jnp.zeros((256, 128), F32)
    for a in (1, 0, 2):
        if a != 1:
            for copies in side_x:
                copies[a // 2].wait_recv()
            whole_row(a)
        two = two + dot(grid[a], jnp.concatenate([tap(3 * a), tap(3 * a + 1)], axis=1))
        third = third + dot(grid[a], tap(3 * a + 2))
    preact = (
        bias[pl.ds(x, 1), :]
        + pltpu.roll(two[:, 0:128], 1, 0)
        + two[:, 128:256]
        + pltpu.roll(third, 255, 0)
    )
    pre[...] = preact
    acts[x] = (preact * jax.nn.sigmoid(preact)).astype(BF16)
    act_x = [push(acts.at[x], zy, (x + dx) % X, lat) for dx in (2, 1, 3)]

    for a in range(3):
        for b in range(3):
            w_turned[b, 128 * a : 128 * (a + 1), :] = tap(3 * a + b).T
    for t in range(3):
        wq_turned[128 * t : 128 * (t + 1), :] = wq[:, 128 * t : 128 * (t + 1)].T

    for copy in cot_x:
        copy.wait_recv()
    flat[...] = cots[...].reshape(1024, 128).astype(F32)
    for q in range(4):
        part = flat[pl.ds(q, 256, stride=4), :].astype(BF16)
        cot_grid[:, 128 * q : 128 * (q + 1)] = part
        cot_blocks[q] = part

    out_grad = dot(cot_grid[...], wo[...], NT).astype(BF16)
    for copy in act_x:
        copy.wait_recv()
    activated = jnp.concatenate([acts[s] for s in range(X)], axis=1)
    projected = dot(activated, wq[...]).astype(BF16)
    queries, keys, values = (projected[:, 128 * t : 128 * (t + 1)] for t in range(3))
    capped = jnp.tanh(dot(queries, keys, NT) * (INV_ROOT / CAP))
    expo = jnp.exp(CAP * capped)
    probs = expo * (1.0 / jnp.sum(expo, axis=-1, keepdims=True))
    probs_b = probs.astype(BF16)
    attended = dot(probs_b, values).astype(BF16)
    centre = jnp.sum(out_grad.astype(F32) * attended.astype(F32), axis=-1, keepdims=True)
    score_grad = (
        probs * (dot(out_grad, values, NT) - centre) * (1.0 - capped * capped) * INV_ROOT
    ).astype(BF16)
    grads = jnp.concatenate(
        [
            dot(score_grad, keys).astype(BF16),
            dot(score_grad, queries, TN).astype(BF16),
            dot(probs_b, out_grad, TN).astype(BF16),
        ],
        axis=1,
    )
    head_part = dot(grads, wq_turned[...])
    for q in range(X):
        blocks[q] = head_part[:, 128 * q : 128 * (q + 1)]

    early = len(started)
    part_x = []
    sides = (1 - z, z)
    halves = [pl.ds(pl.multiple_of(side * 128, 128), 128) for side in sides]
    for half_of in range(2):
        at = halves[half_of]
        for dx in (2, 1, 3):
            i = 3 * half_of + dx - 1
            to = (x + dx) % X
            parts[i] = blocks[to, at].astype(BF16)
            part_x.append(push_to(parts.at[i], parts_in.at[i], zy, to, lat))
    preact = pre[...]
    s = jax.nn.sigmoid(preact)
    pre[...] = s * (1.0 + preact * (1.0 - s))
    for copy in started[:early]:
        copy.wait_send()
    drained[0] = early
    all_weights(False)
    all_rows(st, rows.at[1, zy, x], row_send, row_recv, False)
    all_rows(ct, cots.at[zy, x], cot_send, cot_recv, False)
    middle_rows(False)
    side_rows(False)

    def all_pres(half_of, start):
        def send_all(places, slot, sems, base, to_lat):
            for k, place in enumerate(places):
                copy = remote(
                    own_pre.at[place], pres.at[slot], sems.at[base + k], pre_recv,
                    place, x, to_lat,
                )
                if start:
                    copy.start()
                else:
                    copy.wait_send()

        def ends(slot, to_lat):
            places = along_y + [zy] if half_of else across_z
            send_all(places, slot, end_send, Y * half_of, to_lat)

        send_all((across_z, along_y)[half_of], 1 + mine_of, pre_send, Y * half_of, lat)
        if start and half_of:
            pltpu.make_async_copy(own_pre.at[zy], pres.at[1 + mine_of], pre_recv).start()

        @pl.when(mine_of == ZY - 1)
        def _():
            ends(0, up)

        @pl.when(mine_of == 0)
        def _():
            ends(ZY + 1, down)

    for half_of in range(2):
        at = halves[half_of]
        first = 8 * sides[half_of]
        grad_act = blocks[x, at] + cot_blocks[x, at].astype(F32)
        for i in range(3 * half_of, 3 * half_of + 3):
            part_x[i].wait_recv()
        for i in range(3 * half_of, 3 * half_of + 3):
            grad_act = grad_act + parts_in[i].astype(F32)
        own_pre[pl.ds(first, 8)] = (
            (grad_act * pre[at]).astype(BF16).reshape(8, 16, 128)
        )
        all_pres(half_of, True)

    drain()
    pltpu.make_async_copy(pres, pres, pre_recv).wait()

    @pl.when(lat == 0)
    def _():
        pres[0] = jnp.zeros((16, 128), BF16)

    @pl.when(lat == LATS - 1)
    def _():
        pres[ZY + 1] = jnp.zeros((16, 128), BF16)

    around = jnp.concatenate(
        [pres[2 - a : 2 - a + ZY].reshape(256, 128) for a in range(3)], axis=1
    )

    flat[0:288, :] = pres[...].reshape(288, 128).astype(F32)
    for side, b, at in ((0, 0, 0), (1, 2, 15)):
        edge_of = [flat[pl.ds(16 * (2 - a) + at, 16, stride=16), :] for a in range(3)]
        rim = dot(jnp.concatenate(edge_of, axis=1).astype(BF16), w_turned[b])
        for q in range(4):
            rims[side, q // 2, q % 2] = rim[:, 128 * q : 128 * (q + 1)].astype(BF16)
    rim_west = remote(
        rims.at[0], rims_in.at[x], rim_send.at[0], rim_recv.at[x],
        (zy + ZY - 1) % ZY, X - 1, lat,
    )
    rim_east = remote(
        rims.at[1], rims_in.at[x], rim_send.at[1], rim_recv.at[x], (zy + 1) % ZY, 0, lat
    )
    rim_west.start()
    rim_east.start()

    column = lax.broadcasted_iota(jnp.int32, (256, 256), 0) % 16
    sum_x = []
    for h in range(2):
        at = slice(256 * h, 256 * (h + 1))
        result = jnp.zeros((256, 256), F32)
        for b in range(3):
            acc = dot(around, w_turned[b, :, at])
            if b == 0:
                acc = jnp.where(column == 15, 0.0, pltpu.roll(acc, 255, 0))
            if b == 2:
                acc = jnp.where(column == 0, 0.0, pltpu.roll(acc, 1, 0))
            result = result + acc
        for q in range(2):
            base = 512 * h + 256 * q
            flat[base : base + 256, :] = result[:, 128 * q : 128 * (q + 1)]
            for to in range(X):
                for j in range(4):
                    piece = flat[pl.ds(base + 4 * to + j, 16, stride=16), :]
                    mine[to, h, q, j] = piece.astype(BF16)
        for dx in (2, 1, 3):
            to = (x + dx) % X
            sum_x.append(push_to(mine.at[to, h], sums_in.at[3 * h + dx - 1], zy, to, lat))

    all_pres(0, False)
    all_pres(1, False)

    for h in range(2):
        total = mine[x, h].astype(F32)
        for copy in sum_x[3 * h : 3 * h + 3]:
            copy.wait_recv()
        for i in range(X - 1):
            total = total + sums_in[3 * h + i].astype(F32)
        flat[128 * h : 128 * (h + 1), :] = total.reshape(128, 128)

    def add_rims(j):
        for i in range(X):
            pltpu.make_async_copy(rims_in.at[i], rims_in.at[i], rim_recv.at[i]).wait()
        for q in range(4):
            at = slice(64 * q + 16 * j, 64 * q + 16 * (j + 1))
            total = flat[at]
            for i in range(X):
                total = total + rims_in[i, q // 2, q % 2].astype(F32)
            flat[at] = total

    @pl.when(x == 0)
    def _():
        add_rims(0)

    @pl.when(x == X - 1)
    def _():
        add_rims(3)

    for t in range(ZY):
        out[t] = flat[pl.ds(t, 16, stride=16), :].astype(BF16)

    rim_west.wait_send()
    rim_east.wait_send()
    drain()


PUSHES = 80


def body(state, conv_weight, conv_bias, w_qkv, w_out, cotangent):
    vmem = pl.BlockSpec(memory_space=pltpu.VMEM)
    anywhere = pl.BlockSpec(memory_space=pl.ANY)
    dma = pltpu.SemaphoreType.DMA
    out = pl.pallas_call(
        kernel,
        out_shape=jax.ShapeDtypeStruct((ZY, 16, 128), BF16),
        in_specs=[anywhere] * 6,
        out_specs=vmem,
        scratch_shapes=[
            pltpu.VMEM((2, 16, 4, 512), BF16),
            pltpu.VMEM((72, 512), BF16),
            pltpu.VMEM((ZY, 16, 128), BF16),
            pltpu.VMEM((ZY, 16, 128), BF16),
            pltpu.VMEM((X, 80, 128), BF16),
            pltpu.VMEM((X, 128), F32),
            pltpu.VMEM((3, ZY, X, 16, 128), BF16),
            pltpu.VMEM((ZY, X, 16, 128), BF16),
            pltpu.VMEM((1024, 128), F32),
            pltpu.VMEM((3, 256, 512), BF16),
            pltpu.VMEM((256, 512), BF16),
            pltpu.VMEM((4, 256, 128), BF16),
            pltpu.VMEM((4, 80, 128), BF16),
            pltpu.VMEM((2, 2304, 128), BF16),
            pltpu.VMEM((512, 384), BF16),
            pltpu.VMEM((128, 512), BF16),
            pltpu.VMEM((256, 128), F32),
            pltpu.VMEM((X, 256, 128), BF16),
            pltpu.VMEM((X, 256, 128), F32),
            pltpu.VMEM((6, 128, 128), BF16),
            pltpu.VMEM((6, 128, 128), BF16),
            pltpu.VMEM((ZY, 16, 128), BF16),
            pltpu.VMEM((ZY + 2, 16, 128), BF16),
            pltpu.VMEM((X, 2, 2, 4, ZY, 128), BF16),
            pltpu.VMEM((6, 2, 4, ZY, 128), BF16),
            pltpu.VMEM((2, 2, 2, ZY, 128), BF16),
            pltpu.VMEM((X, 2, 2, ZY, 128), BF16),
            pltpu.VMEM((3, 384, 512), BF16),
            pltpu.VMEM((384, 512), BF16),
            dma((8,)),
            dma((3 * X,)),
            dma((4,)),
            dma((ZY,)),
            dma,
            dma((ZY,)),
            dma,
            dma((ZY,)),
            dma,
            dma((ZY,)),
            dma((2,)),
            dma((X,)),
            dma((2,)),
            dma((2,)),
            dma((2,)),
            dma((PUSHES,)),
            dma((PUSHES,)),
        ],
        compiler_params=pltpu.CompilerParams(
            collective_id=0, has_side_effects=True, vmem_limit_bytes=VMEM_LIMIT
        ),
    )(state, cotangent, conv_weight, conv_bias.reshape(X, 128), w_qkv, w_out)
    return out.reshape(16, 4, 4, 128).transpose(0, 2, 1, 3).reshape(16, 4, 512)


def solution(mesh):
    return jax.shard_map(
        body,
        mesh=mesh,
        in_specs=(P("lat", "lon", None), P("lon", None), P(), P(), P(), P("lat", "lon", None)),
        out_specs=P("lat", "lon", None),
        check_vma=False,
    )
```

```python
import functools
import math

import jax
import jax.numpy as jnp
from jax import lax
from jax.experimental import pallas as pl
from jax.experimental.pallas import tpu as pltpu
from jax.sharding import PartitionSpec as P

X = 4
Y = 8
ZY = 16
LATS = 8
ROWS = ZY * LATS
CAP = 20.0
INV_ROOT = 1.0 / math.sqrt(128.0)
F32 = jnp.float32
BF16 = jnp.bfloat16
VMEM_LIMIT = 60 * 1024 * 1024

NN = (((1,), (0,)), ((), ()))
NT = (((1,), (1,)), ((), ()))
TN = (((0,), (0,)), ((), ()))


def dot(a, b, dims=NN):
    return lax.dot_general(a, b, dims, preferred_element_type=F32)


def kernel(
    st_hbm, ct_hbm, cw_hbm, bias_hbm, wqkv, wout, out,
    raw, raw_w, st, ct, wp, bias,
    rows, cots, flat, grid, cot_grid, cot_blocks, w_one, w_all, wq, wo,
    pre, acts, blocks, parts, parts_in, own_pre, pres, mine, sums_in, rims, rims_in,
    w_turned, wq_turned,
    load_sem, w_send, w_recv, row_send, row_recv, cot_send, cot_recv, pre_send, pre_recv,
    end_send, rim_send, rim_recv, middle_send, side_send, side_recv,
    send, recv,
):
    lon = lax.axis_index("lon")
    lat = lax.axis_index("lat")
    zy, x = lon // X, lon % X
    z, y = zy // Y, zy % Y
    core = lat % 2
    sib = lat + 1 - 2 * core
    mine_of = jnp.where(z == core, y, ZY - 1 - y)
    row = lat * ZY + mine_of
    up, down = (lat + 1) % LATS, (lat + LATS - 1) % LATS

    def owner(t):
        return jnp.where(t < Y, core * Y + t, (1 - core) * Y + ZY - 1 - t)

    east, west = (x + 1) % X, (x + X - 1) % X

    def remote(src, dst, send_sem, recv_sem, to_zy, to_x, to_lat):
        return pltpu.make_async_remote_copy(
            src_ref=src,
            dst_ref=dst,
            send_sem=send_sem,
            recv_sem=recv_sem,
            device_id={"lon": to_zy * X + to_x, "lat": to_lat},
            device_id_type=pl.DeviceIdType.MESH,
        )

    started = []

    def push_to(src, dst, to_zy, to_x, to_lat):
        i = len(started)
        copy = remote(src, dst, send.at[i], recv.at[i], to_zy, to_x, to_lat)
        copy.start()
        started.append(copy)
        return copy

    drained = [0]

    def drain():
        for copy in started[drained[0] :]:
            copy.wait_send()
        drained[0] = len(started)

    def push(ref, to_zy, to_x, to_lat):
        return push_to(ref, ref, to_zy, to_x, to_lat)

    def load(i, src, dst):
        copy = pltpu.make_async_copy(src, dst, load_sem.at[i])
        copy.start()
        return copy

    weight_load = load(0, cw_hbm, raw_w)
    state_load = load(1, st_hbm, raw.at[0])
    cot_load = load(2, ct_hbm, raw.at[1])
    barrier = pltpu.get_barrier_semaphore()

    def hello(to_zy, to_x, to_lat):
        pl.semaphore_signal(
            barrier,
            inc=1,
            device_id={"lon": to_zy * X + to_x, "lat": to_lat},
            device_id_type=pl.DeviceIdType.MESH,
        )

    other_zy = (1 - z) * Y + y
    for dx in range(1, X):
        hello(zy, (x + dx) % X, lat)
    hello(zy, x, sib)

    @pl.loop(1, ZY)
    def _(d):
        hello((zy + d) % ZY, x, lat)

    hello(core * Y, x, down)
    hello((1 - core) * Y, x, up)

    plane = lat // 2
    near = jnp.where(plane < 2, 3, 0) * 2 + core
    for i in range(2):
        hello(other_zy, 2 * core + i, near)

    @pl.when(x == 0)
    def _():
        for i in range(X):
            hello((zy + ZY - 1) % ZY, i, lat)

    @pl.when(x == X - 1)
    def _():
        for i in range(X):
            hello((zy + 1) % ZY, i, lat)

    loads = [load(3, bias_hbm, bias)]
    for t in range(3):
        source = wqkv.at[:, pl.ds(pl.multiple_of(t * 512 + x * 128, 128), 128)]
        loads.append(load(4 + t, source, wq.at[:, 128 * t : 128 * (t + 1)]))
    loads.append(load(7, wout.at[pl.ds(pl.multiple_of(x * 128, 128), 128)], wo))

    weight_load.wait()
    for q in range(X):
        piece = raw_w[:, 128 * q : 128 * (q + 1)].astype(F32)
        wp[q] = jnp.concatenate([piece, jnp.zeros((8, 128), F32)], axis=0).astype(BF16)

    edge = (mine_of == 0) | (mine_of == ZY - 1)
    sends_weight = x // 2 == core
    crosses = sends_weight & ((plane == 0) | (plane == 3))
    pl.semaphore_wait(
        barrier,
        (X - 1) + (ZY - 1) + 1 + 2 + jnp.where(edge, ZY, 0) + jnp.where(crosses, 2 * X, 0),
    )

    slot = z * 2 + x % 2

    def all_weights(start):
        def across(copy):
            if start:
                copy.start()
            else:
                copy.wait_send()

        @pl.when(crosses)
        def _():
            for k in range(2):
                to_lat = jnp.where(plane == 3, k, 2 + k) * 2 + core
                for t in range(X):
                    across(
                        remote(
                            wp.at[t], w_one.at[slot], w_send.at[X + X * k + t],
                            w_recv.at[slot], other_zy, t, to_lat,
                        )
                    )

        @pl.when(sends_weight)
        def _():
            for t in range(X):
                if start:
                    @pl.when(t == x)
                    def _():
                        pltpu.make_async_copy(
                            wp.at[t], w_one.at[slot], w_recv.at[slot]
                        ).start()

                @pl.when(t != x)
                def _():
                    across(
                        remote(
                            wp.at[t], w_one.at[slot], w_send.at[t], w_recv.at[slot],
                            zy, t, lat,
                        )
                    )

    all_weights(True)

    def relayout(which, dst):
        for r in range(16):
            for q in range(4):
                piece = raw[which, r, :, 128 * q : 128 * (q + 1)].astype(F32)
                flat[pl.ds(16 * r + q, 4, stride=4), :] = piece
        dst[...] = flat[0:256, :].astype(BF16).reshape(16, 16, 128)

    state_load.wait()
    relayout(0, st)

    lead = jnp.where(z == core, Y, 0)

    def all_rows(src, dst, send_sem, recv_sem, start):
        @pl.loop(0, ZY)
        def _(i):
            t = (i + lead) % ZY

            if start:
                @pl.when(t == mine_of)
                def _():
                    pltpu.make_async_copy(src.at[t], dst, recv_sem).start()

            @pl.when(t != mine_of)
            def _():
                copy = remote(
                    src.at[t], dst, send_sem.at[t], recv_sem, owner(t), x, lat
                )
                if start:
                    copy.start()
                else:
                    copy.wait_send()

    def middle_rows(start):
        for i, t, to in ((0, Y - 1, Y), (1, Y, Y - 1)):
            dst = rows.at[2 * i, zy, x]
            if start:
                @pl.when(to == mine_of)
                def _():
                    pltpu.make_async_copy(st.at[t], dst, side_recv.at[i]).start()

            @pl.when(to != mine_of)
            def _():
                copy = remote(
                    st.at[t], dst, middle_send.at[i], side_recv.at[i], owner(to), x, lat
                )
                if start:
                    copy.start()
                else:
                    copy.wait_send()

    def side_rows(start):
        for i, last, middle, to_lat, step in (
            (0, ZY - 1, Y - 1, up, 1),
            (1, 0, Y, down, -1),
        ):
            @pl.when(mine_of != middle)
            def _():
                to_zy = jnp.where(mine_of == last, zy, owner(mine_of + step))
                copy = remote(
                    rows.at[1, :, x], rows.at[2 * i, :, x], side_send.at[i], side_recv.at[i],
                    to_zy, x, jnp.where(mine_of == last, to_lat, lat),
                )
                if start:
                    copy.start()
                else:
                    copy.wait_send()

    all_rows(st, rows.at[1, zy, x], row_send, row_recv, True)
    middle_rows(True)

    def half(place, which):
        return pl.ds(pl.multiple_of((place * 2 + which) * 144, 16), 144)

    def take_weight(part):
        both = []
        for i in range(2):
            at = w_one.at[2 * part + i]
            pltpu.make_async_copy(at, at, w_recv.at[2 * part + i]).wait()
            both.append(w_one[2 * part + i].astype(F32)[:72])
        w_all[part, half(y, core), :] = jnp.concatenate(both, axis=0).astype(BF16)

    def along(turn, place, step):
        to = z * Y + (y + Y + step) % Y
        return push(w_all.at[(z, 1 - z)[turn], half(place, core)], to, x, lat)

    pair = []

    def to_pair(turn, place):
        pair.append(push(w_all.at[(z, 1 - z)[turn], half(place, core)], zy, x, sib))

    take_weight(z)
    rights, lefts = [along(0, y, 1)], [along(0, y, -1)]
    to_pair(0, y)
    take_weight(1 - z)
    nearest = [along(1, y, step) for step in (1, -1, 2, -2)]
    to_pair(1, y)

    def forward(step):
        for copies, way, steps in ((rights, 1, 4), (lefts, -1, 3)):
            if step < steps:
                copies[step].wait_recv()
                place = (y + Y - way * (step + 1)) % Y
                if step + 1 < steps:
                    copies.append(along(0, place, way))
                to_pair(0, place)

    handed = []

    def hand_on(which, on):
        step = (1, -1, 2, -2)[which]
        nearest[which].wait_recv()
        place = (y + Y - step) % Y
        if on:
            by = 2 if step > 0 else -2
            handed.append((along(1, place, by), (y + Y - step - by) % Y))
        to_pair(1, place)

    def round_x(whole, west_half, east_half):
        return (
            push(whole, zy, east, lat),
            push(whole, zy, west, lat),
            west_half,
            east_half,
        )

    def round_x_on(to_east, to_west, west_half, east_half):
        to_east.wait_recv()
        on_east = push(west_half, zy, east, lat)
        to_west.wait_recv()
        return on_east, push(east_half, zy, west, lat)

    cot_load.wait()
    relayout(1, ct)
    all_rows(ct, cots.at[zy, x], cot_send, cot_recv, True)

    forward(0)
    pltpu.make_async_copy(rows.at[1, :, x], rows.at[1, :, x], row_recv).wait()
    side_rows(True)
    row_x = round_x(rows.at[1, :, x], rows.at[1, 0:8, west], rows.at[1, 8:16, east])
    hand_on(0, True)
    hand_on(1, True)
    forward(1)
    hand_on(2, False)
    hand_on(3, True)
    row_on = round_x_on(*row_x)
    for i in range(2):
        at = rows.at[2 * i, :, x]
        pltpu.make_async_copy(at, at, side_recv.at[i]).wait()
    side_x = [
        [push(rows.at[2 * i, :, x], zy, (x + dx) % X, lat) for i in range(2)]
        for dx in (2, 1, 3)
    ]
    forward(2)
    pltpu.make_async_copy(cots.at[:, x], cots.at[:, x], cot_recv).wait()
    cot_x = [push(cots.at[:, x], zy, (x + dx) % X, lat) for dx in range(1, X)]
    for copy, place in handed:
        copy.wait_recv()
        to_pair(1, place)

    def whole_row(a):
        flat[...] = rows[a].reshape(1024, 128).astype(F32)
        for q in range(4):
            part = flat[pl.ds(q, 256, stride=4), :]
            if a == 0:
                part = jnp.where(row == 0, 0.0, part)
            if a == 2:
                part = jnp.where(row == ROWS - 1, 0.0, part)
            grid[a, :, 128 * q : 128 * (q + 1)] = part.astype(BF16)

    for copy in row_on:
        copy.wait_recv()
    whole_row(1)

    forward(3)

    for copy in loads:
        copy.wait()
    for copy in pair:
        copy.wait_recv()

    def tap(i):
        if i < 4:
            return w_all[0, 512 * i : 512 * (i + 1), :]
        if i > 4:
            return w_all[1, 512 * i - 2304 : 512 * (i + 1) - 2304, :]
        return jnp.concatenate([w_all[0, 2048:2304, :], w_all[1, 0:256, :]], axis=0)

    two = jnp.zeros((256, 256), F32)
    third = jnp.zeros((256, 128), F32)
    for a in (1, 0, 2):
        if a != 1:
            for copies in side_x:
                copies[a // 2].wait_recv()
            whole_row(a)
        two = two + dot(grid[a], jnp.concatenate([tap(3 * a), tap(3 * a + 1)], axis=1))
        third = third + dot(grid[a], tap(3 * a + 2))
    preact = (
        bias[pl.ds(x, 1), :]
        + pltpu.roll(two[:, 0:128], 1, 0)
        + two[:, 128:256]
        + pltpu.roll(third, 255, 0)
    )
    pre[...] = preact
    acts[x] = (preact * jax.nn.sigmoid(preact)).astype(BF16)
    act_x = [push(acts.at[x], zy, (x + dx) % X, lat) for dx in (2, 1, 3)]

    for a in range(3):
        for b in range(3):
            w_turned[b, 128 * a : 128 * (a + 1), :] = tap(3 * a + b).T
    for t in range(3):
        wq_turned[128 * t : 128 * (t + 1), :] = wq[:, 128 * t : 128 * (t + 1)].T

    for copy in cot_x:
        copy.wait_recv()
    flat[...] = cots[...].reshape(1024, 128).astype(F32)
    for q in range(4):
        part = flat[pl.ds(q, 256, stride=4), :].astype(BF16)
        cot_grid[:, 128 * q : 128 * (q + 1)] = part
        cot_blocks[q] = part

    out_grad = dot(cot_grid[...], wo[...], NT).astype(BF16)
    for copy in act_x:
        copy.wait_recv()
    activated = jnp.concatenate([acts[s] for s in range(X)], axis=1)
    projected = dot(activated, wq[...]).astype(BF16)
    queries, keys, values = (projected[:, 128 * t : 128 * (t + 1)] for t in range(3))
    capped = jnp.tanh(dot(queries, keys, NT) * (INV_ROOT / CAP))
    expo = jnp.exp(CAP * capped)
    probs = expo * (1.0 / jnp.sum(expo, axis=-1, keepdims=True))
    probs_b = probs.astype(BF16)
    attended = dot(probs_b, values).astype(BF16)
    centre = jnp.sum(out_grad.astype(F32) * attended.astype(F32), axis=-1, keepdims=True)
    score_grad = (
        probs * (dot(out_grad, values, NT) - centre) * (1.0 - capped * capped) * INV_ROOT
    ).astype(BF16)
    grads = jnp.concatenate(
        [
            dot(score_grad, keys).astype(BF16),
            dot(score_grad, queries, TN).astype(BF16),
            dot(probs_b, out_grad, TN).astype(BF16),
        ],
        axis=1,
    )
    head_part = dot(grads, wq_turned[...])
    for q in range(X):
        blocks[q] = head_part[:, 128 * q : 128 * (q + 1)]

    early = len(started)
    part_x = []
    sides = (1 - z, z)
    halves = [pl.ds(pl.multiple_of(side * 128, 128), 128) for side in sides]
    for half_of in range(2):
        at = halves[half_of]
        for dx in (2, 1, 3):
            i = 3 * half_of + dx - 1
            to = (x + dx) % X
            parts[i] = blocks[to, at].astype(BF16)
            part_x.append(push_to(parts.at[i], parts_in.at[i], zy, to, lat))
    preact = pre[...]
    s = jax.nn.sigmoid(preact)
    pre[...] = s * (1.0 + preact * (1.0 - s))
    for copy in started[:early]:
        copy.wait_send()
    drained[0] = early
    all_weights(False)
    all_rows(st, rows.at[1, zy, x], row_send, row_recv, False)
    all_rows(ct, cots.at[zy, x], cot_send, cot_recv, False)
    middle_rows(False)
    side_rows(False)

    def all_pres(first, start):
        @pl.loop(first, first + 8)
        def _(t):
            dst = pres.at[1 + mine_of]
            if start:
                @pl.when(t == zy)
                def _():
                    pltpu.make_async_copy(own_pre.at[t], dst, pre_recv).start()

            @pl.when(t != zy)
            def _():
                copy = remote(own_pre.at[t], dst, pre_send.at[t], pre_recv, t, x, lat)
                if start:
                    copy.start()
                else:
                    copy.wait_send()

        def ends(slot, to_lat):
            @pl.loop(first, first + 8)
            def _(t):
                copy = remote(
                    own_pre.at[t], pres.at[slot], end_send.at[t], pre_recv, t, x, to_lat
                )
                if start:
                    copy.start()
                else:
                    copy.wait_send()

        @pl.when(mine_of == ZY - 1)
        def _():
            ends(0, up)

        @pl.when(mine_of == 0)
        def _():
            ends(ZY + 1, down)

    for half_of in range(2):
        at = halves[half_of]
        first = 8 * sides[half_of]
        grad_act = blocks[x, at] + cot_blocks[x, at].astype(F32)
        for i in range(3 * half_of, 3 * half_of + 3):
            part_x[i].wait_recv()
        for i in range(3 * half_of, 3 * half_of + 3):
            grad_act = grad_act + parts_in[i].astype(F32)
        own_pre[pl.ds(first, 8)] = (
            (grad_act * pre[at]).astype(BF16).reshape(8, 16, 128)
        )
        all_pres(first, True)

    drain()
    pltpu.make_async_copy(pres, pres, pre_recv).wait()

    @pl.when(lat == 0)
    def _():
        pres[0] = jnp.zeros((16, 128), BF16)

    @pl.when(lat == LATS - 1)
    def _():
        pres[ZY + 1] = jnp.zeros((16, 128), BF16)

    around = jnp.concatenate(
        [pres[2 - a : 2 - a + ZY].reshape(256, 128) for a in range(3)], axis=1
    )

    flat[0:288, :] = pres[...].reshape(288, 128).astype(F32)
    for side, b, at in ((0, 0, 0), (1, 2, 15)):
        edge_of = [flat[pl.ds(16 * (2 - a) + at, 16, stride=16), :] for a in range(3)]
        rim = dot(jnp.concatenate(edge_of, axis=1).astype(BF16), w_turned[b])
        for q in range(4):
            rims[side, q // 2, q % 2] = rim[:, 128 * q : 128 * (q + 1)].astype(BF16)
    rim_west = remote(
        rims.at[0], rims_in.at[x], rim_send.at[0], rim_recv.at[x],
        (zy + ZY - 1) % ZY, X - 1, lat,
    )
    rim_east = remote(
        rims.at[1], rims_in.at[x], rim_send.at[1], rim_recv.at[x], (zy + 1) % ZY, 0, lat
    )
    rim_west.start()
    rim_east.start()

    column = lax.broadcasted_iota(jnp.int32, (256, 256), 0) % 16
    sum_x = []
    for h in range(2):
        at = slice(256 * h, 256 * (h + 1))
        result = jnp.zeros((256, 256), F32)
        for b in range(3):
            acc = dot(around, w_turned[b, :, at])
            if b == 0:
                acc = jnp.where(column == 15, 0.0, pltpu.roll(acc, 255, 0))
            if b == 2:
                acc = jnp.where(column == 0, 0.0, pltpu.roll(acc, 1, 0))
            result = result + acc
        for q in range(2):
            base = 512 * h + 256 * q
            flat[base : base + 256, :] = result[:, 128 * q : 128 * (q + 1)]
            for to in range(X):
                for j in range(4):
                    piece = flat[pl.ds(base + 4 * to + j, 16, stride=16), :]
                    mine[to, h, q, j] = piece.astype(BF16)
        for dx in (2, 1, 3):
            to = (x + dx) % X
            sum_x.append(push_to(mine.at[to, h], sums_in.at[3 * h + dx - 1], zy, to, lat))

    all_pres(0, False)
    all_pres(8, False)

    for h in range(2):
        total = mine[x, h].astype(F32)
        for copy in sum_x[3 * h : 3 * h + 3]:
            copy.wait_recv()
        for i in range(X - 1):
            total = total + sums_in[3 * h + i].astype(F32)
        flat[128 * h : 128 * (h + 1), :] = total.reshape(128, 128)

    def add_rims(j):
        for i in range(X):
            pltpu.make_async_copy(rims_in.at[i], rims_in.at[i], rim_recv.at[i]).wait()
        for q in range(4):
            at = slice(64 * q + 16 * j, 64 * q + 16 * (j + 1))
            total = flat[at]
            for i in range(X):
                total = total + rims_in[i, q // 2, q % 2].astype(F32)
            flat[at] = total

    @pl.when(x == 0)
    def _():
        add_rims(0)

    @pl.when(x == X - 1)
    def _():
        add_rims(3)

    for t in range(ZY):
        out[t] = flat[pl.ds(t, 16, stride=16), :].astype(BF16)

    rim_west.wait_send()
    rim_east.wait_send()
    drain()


PUSHES = 80


def body(state, conv_weight, conv_bias, w_qkv, w_out, cotangent):
    vmem = pl.BlockSpec(memory_space=pltpu.VMEM)
    anywhere = pl.BlockSpec(memory_space=pl.ANY)
    dma = pltpu.SemaphoreType.DMA
    out = pl.pallas_call(
        kernel,
        out_shape=jax.ShapeDtypeStruct((ZY, 16, 128), BF16),
        in_specs=[anywhere] * 6,
        out_specs=vmem,
        scratch_shapes=[
            pltpu.VMEM((2, 16, 4, 512), BF16),
            pltpu.VMEM((72, 512), BF16),
            pltpu.VMEM((ZY, 16, 128), BF16),
            pltpu.VMEM((ZY, 16, 128), BF16),
            pltpu.VMEM((X, 80, 128), BF16),
            pltpu.VMEM((X, 128), F32),
            pltpu.VMEM((3, ZY, X, 16, 128), BF16),
            pltpu.VMEM((ZY, X, 16, 128), BF16),
            pltpu.VMEM((1024, 128), F32),
            pltpu.VMEM((3, 256, 512), BF16),
            pltpu.VMEM((256, 512), BF16),
            pltpu.VMEM((4, 256, 128), BF16),
            pltpu.VMEM((4, 80, 128), BF16),
            pltpu.VMEM((2, 2304, 128), BF16),
            pltpu.VMEM((512, 384), BF16),
            pltpu.VMEM((128, 512), BF16),
            pltpu.VMEM((256, 128), F32),
            pltpu.VMEM((X, 256, 128), BF16),
            pltpu.VMEM((X, 256, 128), F32),
            pltpu.VMEM((6, 128, 128), BF16),
            pltpu.VMEM((6, 128, 128), BF16),
            pltpu.VMEM((ZY, 16, 128), BF16),
            pltpu.VMEM((ZY + 2, 16, 128), BF16),
            pltpu.VMEM((X, 2, 2, 4, ZY, 128), BF16),
            pltpu.VMEM((6, 2, 4, ZY, 128), BF16),
            pltpu.VMEM((2, 2, 2, ZY, 128), BF16),
            pltpu.VMEM((X, 2, 2, ZY, 128), BF16),
            pltpu.VMEM((3, 384, 512), BF16),
            pltpu.VMEM((384, 512), BF16),
            dma((8,)),
            dma((3 * X,)),
            dma((4,)),
            dma((ZY,)),
            dma,
            dma((ZY,)),
            dma,
            dma((ZY,)),
            dma,
            dma((ZY,)),
            dma((2,)),
            dma((X,)),
            dma((2,)),
            dma((2,)),
            dma((2,)),
            dma((PUSHES,)),
            dma((PUSHES,)),
        ],
        compiler_params=pltpu.CompilerParams(
            collective_id=0, has_side_effects=True, vmem_limit_bytes=VMEM_LIMIT
        ),
    )(state, cotangent, conv_weight, conv_bias.reshape(X, 128), w_qkv, w_out)
    return out.reshape(16, 4, 4, 128).transpose(0, 2, 1, 3).reshape(16, 4, 512)


def solution(mesh):
    return jax.shard_map(
        body,
        mesh=mesh,
        in_specs=(P("lat", "lon", None), P("lon", None), P(), P(), P(), P("lat", "lon", None)),
        out_specs=P("lat", "lon", None),
        check_vma=False,
    )
```
